32 devices in a mesh: dp: 2 (over x), expert: 16 (over z, y, core).
Axes of the slice: x: 2, y: 2, z: 4, core: 2. Of those that a mesh axis runs over, the one named last changes fastest.
Arguments:
- tokens: bfloat16 [2048, 2048], P(('dp', 'expert')), may hold values from -6 to 6
- out_grad: bfloat16 [2048, 2048], P(('dp', 'expert')), may hold values from -1.1953125 to 1.1953125
- expert_ids: int32 [2048, 6], P(('dp', 'expert')), may hold values from 0 to 15, all different within a row; in each aligned block of 64 rows (0 to 63, 64 to 127, ...) at most 28 rows name the same one
- gates: bfloat16 [2048, 6], P(('dp', 'expert')), may hold values from 0.049804688 to 0.5
- w_gate: bfloat16 [16, 2048, 704], P('expert'), may hold values from -0.125 to 0.125
- w_up: bfloat16 [16, 2048, 704], P('expert'), may hold values from -0.125 to 0.125
- w_down: bfloat16 [16, 704, 2048], P('expert'), may hold values from -0.21875 to 0.21875
Outputs:
- token_grad: bfloat16 [2048, 2048], P(('dp', 'expert'))
- gate_grad: bfloat16 [2048, 6], P(('dp', 'expert'))
- grad_gate: bfloat16 [16, 2048, 704], P('expert', 'dp')
- grad_up: bfloat16 [16, 2048, 704], P('expert', 'dp')
- grad_down: bfloat16 [16, 704, 2048], P('expert', None, 'dp')
The draws below stay inside these ranges and needn't reach their ends.
Inputs may be any that keep to these rules, and one draw needn't show every extreme that they name: `expert_ids`: each row names 6 different experts. Among the 64 rows of one device no expert is named by more than 28 rows, and in some device some expert is named by exactly 28 rows.
All inputs are finite; a program needn't handle non-finite values.
Results may differ from the reference program's by a relative error of at most 0.0067.
Values may be sent and summed in bfloat16 or wider, within the bound.
No kernel may reach another device: no remote copies, remote signals or barrier semaphores. Data moves between devices by JAX's collectives and lax.ppermute only.
A program may use at most 128 MiB of HBM per device.

```python
import math
import jax
import jax.numpy as jnp
import numpy as np
from jax import lax

D = 2048
FFW = 704
TOPK = 6
TOK_DEV = 64
EXPERTS = 16
CAP = 28
TOKENS = 2048
N_DP = 2


def block_levels(rng, dims, split, least, largest):
    gain, own = 1.0, jax.random.fold_in(rng, 6)
    for dim, parts in split:
        draws = jnp.exp(jax.random.uniform(jax.random.fold_in(own, dim), (parts,), jnp.float32, least / len(split), largest / len(split)))
        gain = gain * jnp.repeat(draws, dims[dim] // parts).reshape([-1 if axis == dim else 1 for axis in range(len(dims))])
    return gain


def assign_block(stream_key, own, number, rows, number_of, top, limit, slope):
    ranking = jax.random.permutation(stream_key, number_of)
    heavy_load, usual = portions_of(number_of, rows * top, limit, slope, True), portions_of(number_of, rows * top, limit, slope, False)
    places = jnp.arange(number_of)

    def named(sizes, offset_by):
        used = int((sizes > 0).sum())
        fixed = max(1, used // 4)
        moved = fixed + (places - fixed + offset_by * (used - fixed)) % max(1, number_of - fixed)
        return jnp.zeros((number_of,), jnp.int32).at[ranking[jnp.where(places < fixed, places, moved)]].set(jnp.asarray(sizes, jnp.int32))

    sizes = jnp.where(number % 4 == 0, named(heavy_load, number // 4), named(usual, number - number // 4 - 1))
    mixed = jax.random.permutation(jax.random.fold_in(own, 3), number_of)
    donor, receiver = mixed[0:number_of // 2 * 2:2], mixed[1:number_of // 2 * 2:2]
    slack = jnp.minimum(sizes[donor] - 1, limit - sizes[receiver]) // 2
    slack = jnp.where((donor == ranking[0]) | (receiver == ranking[0]) | (sizes[receiver] == 0), 0, jnp.maximum(slack, 0))
    moved = jax.random.randint(jax.random.fold_in(own, 4), (number_of // 2,), 0, 1 << 20) % (slack + 1)
    sizes = sizes.at[donor].add(-moved).at[receiver].add(moved)
    items = jnp.searchsorted(jnp.cumsum(sizes), jnp.arange(rows * top), side="right").astype(jnp.int32)
    listing = items.reshape(top, rows).T
    listing = listing[jax.random.permutation(jax.random.fold_in(own, 1), rows)]
    offset_by = jax.random.randint(jax.random.fold_in(own, 2), (rows, 1), 0, top)
    return jnp.take_along_axis(listing, (jnp.arange(top)[None, :] + offset_by) % top, axis=1)


def portions_of(number_of, total, limit, skew, full):
    portions = [(1 << 20) // math.isqrt(rank ** skew) + 1 for rank in range(1, number_of + 1)]
    largest = limit if full else min(limit, max(-(-total // number_of), total * portions[0] // sum(portions)))
    least = 1 if total - largest >= number_of - 1 else 0
    holding, rest = [largest] + [least] * (number_of - 1), total - largest - least * (number_of - 1)
    while rest > 0:
        candidates = [i for i in range(1, number_of) if holding[i] < largest] or [i for i in range(1, number_of) if holding[i] < limit]
        pool, remaining = sum([portions[i] for i in candidates]), rest
        for i in candidates:
            extra = min(limit - holding[i], max(1, remaining * portions[i] // pool), rest)
            holding[i] = holding[i] + extra
            rest = rest - extra
    return np.array(holding)


def scatter_about(stream_key, shape, deviation, bound, pieces=(), kind=jnp.bfloat16):
    loudness = block_levels(stream_key, shape, pieces, -0.22, 0.18) if pieces else 1.0
    array = jax.random.normal(stream_key, shape, jnp.float32) * deviation * loudness
    return jnp.minimum(jnp.maximum(array, -bound), bound).astype(kind)


def setup_inputs(seed: int = 0) -> dict:
    streams_of = jax.random.split(jax.random.key(seed), 8)
    tokens = scatter_about(streams_of[0], (TOKENS, D), 1.0, 6.0, ((0, 32),))
    out_grad = scatter_about(streams_of[1], (TOKENS, D), 0.2, 1.1953125, ((0, 32),))
    expert_ids_keys = jax.random.split(jax.random.fold_in(streams_of[2], 1), TOKENS // TOK_DEV)
    expert_ids_turns = jax.random.permutation(jax.random.fold_in(streams_of[2], 3), TOKENS // TOK_DEV)
    expert_ids = jax.vmap(lambda own, number: assign_block(jax.random.fold_in(streams_of[2], 2), own, number, TOK_DEV, EXPERTS, TOPK, CAP, 2))(expert_ids_keys, expert_ids_turns).reshape((TOKENS, TOPK))
    gates = jnp.clip(jnp.exp(math.log(0.5) - 2.306499 * jax.random.uniform(streams_of[3], (TOKENS, TOPK), jnp.float32) ** block_levels(streams_of[3], (TOKENS, TOPK), ((0, 32),), -0.2, 0.2)), 0.049804688, 0.5).astype(jnp.bfloat16)
    w_gate = scatter_about(streams_of[4], (EXPERTS, D, FFW), D ** -0.5, 0.125, ((0, 16),))
    w_up = scatter_about(streams_of[5], (EXPERTS, D, FFW), D ** -0.5, 0.125, ((0, 16),))
    w_down = scatter_about(streams_of[6], (EXPERTS, FFW, D), FFW ** -0.5, 0.21875, ((0, 16),))
    return dict(tokens=tokens, out_grad=out_grad, expert_ids=expert_ids, gates=gates, w_gate=w_gate, w_up=w_up, w_down=w_down)


def slot_places(expert_ids, experts, capacity):
    flat_ids = expert_ids.reshape(-1).astype(jnp.int32)
    labels = jnp.arange(experts, dtype=jnp.int32)
    onehot = (flat_ids[:, None] == labels[None, :]).astype(jnp.int32)
    earlier = jnp.cumsum(onehot, axis=0) - onehot
    slot_index = jnp.sum(earlier * onehot, axis=1).astype(jnp.int32)
    return (flat_ids * capacity + slot_index).astype(jnp.int32)


def slot_sources(places, slot_total):
    route_total = places.shape[0]
    filler = jnp.zeros((slot_total,), jnp.int32).at[places].set(jnp.arange(route_total, dtype=jnp.int32) + 1)
    return jnp.maximum(filler - 1, 0).astype(jnp.int32), filler > 0


def fill_slots(values, source, filled):
    taken = values[source]
    keep_mask = filled.reshape(filled.shape + (1,) * (taken.ndim - 1))
    return jnp.where(keep_mask, taken, jnp.zeros_like(taken))


def expert_pass(x_rows, dy_rows, g_rows, gate_w, up_w, down_w):
    pre_gate = jnp.dot(x_rows, gate_w, preferred_element_type=jnp.float32)
    pre_up = jnp.dot(x_rows, up_w, preferred_element_type=jnp.float32)
    sigmoid_gate = jax.nn.sigmoid(pre_gate)
    activated = pre_gate * sigmoid_gate
    hidden = (activated * pre_up).astype(jnp.bfloat16)
    expert_out = jnp.dot(hidden, down_w, preferred_element_type=jnp.float32)
    gate_grad = jnp.sum(dy_rows.astype(jnp.float32) * expert_out, axis=-1).astype(jnp.bfloat16)
    scaled = (g_rows.astype(jnp.float32)[:, None] * dy_rows.astype(jnp.float32)).astype(jnp.bfloat16)
    hidden_grad = lax.dot_general(scaled, down_w, (((1,), (1,)), ((), ())), preferred_element_type=jnp.float32)
    pre_gate_grad = (hidden_grad * pre_up * sigmoid_gate * (1.0 + pre_gate * (1.0 - sigmoid_gate))).astype(jnp.bfloat16)
    pre_up_grad = (hidden_grad * activated).astype(jnp.bfloat16)
    route_grad = lax.dot_general(pre_gate_grad, gate_w, (((1,), (1,)), ((), ())), preferred_element_type=jnp.float32)
    route_grad = route_grad + lax.dot_general(pre_up_grad, up_w, (((1,), (1,)), ((), ())), preferred_element_type=jnp.float32)
    return route_grad.astype(jnp.bfloat16), gate_grad, pre_gate_grad, pre_up_grad, hidden, scaled


def reference(tokens, out_grad, expert_ids, gates, w_gate, w_up, w_down):
    members = EXPERTS
    slot_total = EXPERTS * CAP

    def block_fill(x_block, dy_block, id_block, gate_block):
        places = slot_places(id_block, EXPERTS, CAP)
        source, filled = slot_sources(places, slot_total)
        token_source = (source // TOPK).astype(jnp.int32)
        return (places, fill_slots(x_block, token_source, filled), fill_slots(dy_block, token_source, filled),
                fill_slots(gate_block.reshape(-1), source, filled))

    def to_experts(buffer):
        tail = buffer.shape[2:]
        shaped = buffer.reshape((members, EXPERTS, CAP) + tail)
        shaped = jnp.moveaxis(shaped, 1, 0)
        return shaped.reshape((EXPERTS, members * CAP) + tail)

    def from_experts(buffer):
        tail = buffer.shape[2:]
        shaped = buffer.reshape((EXPERTS, members, CAP) + tail)
        shaped = jnp.moveaxis(shaped, 1, 0)
        return shaped.reshape((members, slot_total) + tail)

    def one_expert(expert_items):
        x_expert, dy_expert, g_expert, gate_w, up_w, down_w = expert_items
        route_grad, gate_grad, pre_gate_grad, pre_up_grad, hidden, scaled = expert_pass(
            x_expert, dy_expert, g_expert, gate_w, up_w, down_w)
        contract = (((0,), (0,)), ((), ()))
        part_gate = lax.dot_general(x_expert, pre_gate_grad, contract, preferred_element_type=jnp.float32)
        part_up = lax.dot_general(x_expert, pre_up_grad, contract, preferred_element_type=jnp.float32)
        part_down = lax.dot_general(hidden, scaled, contract, preferred_element_type=jnp.float32)
        return (route_grad, gate_grad, part_gate.astype(jnp.bfloat16), part_up.astype(jnp.bfloat16),
                part_down.astype(jnp.bfloat16))

    def group_step(totals, inputs):
        x_group, dy_group, id_group, g_group = inputs
        places, x_buf, dy_buf, g_buf = jax.vmap(block_fill)(x_group, dy_group, id_group, g_group)
        route_grad, gate_grad, part_gate, part_up, part_down = lax.map(
            one_expert, (to_experts(x_buf), to_experts(dy_buf), to_experts(g_buf), w_gate, w_up, w_down))
        totals = (totals[0] + lax.optimization_barrier(part_gate).astype(jnp.float32),
                  totals[1] + lax.optimization_barrier(part_up).astype(jnp.float32),
                  totals[2] + lax.optimization_barrier(part_down).astype(jnp.float32))
        back_dx = from_experts(route_grad)
        back_dg = from_experts(gate_grad)
        routed = jax.vmap(lambda table, where: table[where])(back_dx, places)
        token_grad = jnp.sum(routed.reshape(members, TOK_DEV, TOPK, D).astype(jnp.float32), axis=2).astype(jnp.bfloat16)
        routed_gate = jax.vmap(lambda table, where: table[where])(back_dg, places)
        return totals, (token_grad, routed_gate.reshape(members, TOK_DEV, TOPK))

    inputs = (tokens.reshape(N_DP, members, TOK_DEV, D), out_grad.reshape(N_DP, members, TOK_DEV, D),
              expert_ids.reshape(N_DP, members, TOK_DEV, TOPK), gates.reshape(N_DP, members, TOK_DEV, TOPK))
    start_sums = (jnp.zeros((EXPERTS, D, FFW), jnp.float32), jnp.zeros((EXPERTS, D, FFW), jnp.float32),
                  jnp.zeros((EXPERTS, FFW, D), jnp.float32))
    totals, (token_grad, gate_grad) = lax.scan(group_step, start_sums, inputs)
    return (token_grad.reshape(TOKENS, D), gate_grad.reshape(TOKENS, TOPK), totals[0].astype(jnp.bfloat16),
            totals[1].astype(jnp.bfloat16), totals[2].astype(jnp.bfloat16))
```

```python
import jax
import jax.numpy as jnp
from jax import lax
from jax.sharding import PartitionSpec as P


def slot_places(expert_ids, experts, capacity):
    flat_ids = expert_ids.reshape(-1)
    labels = jnp.arange(experts, dtype=jnp.int32)
    onehot = (flat_ids[:, None] == labels[None, :]).astype(jnp.int32)
    earlier = jnp.cumsum(onehot, axis=0) - onehot
    slot_index = jnp.sum(earlier * onehot, axis=1)
    return flat_ids * capacity + slot_index


def slot_sources(places, slot_total):
    route_total = places.shape[0]
    filler = (
        jnp.zeros((slot_total,), jnp.int32)
        .at[places]
        .set(jnp.arange(route_total, dtype=jnp.int32) + 1)
    )
    return (jnp.maximum(filler - 1, 0), filler > 0)


def fill_slots(values, source, filled):
    taken = values[source]
    keep_mask = filled.reshape(filled.shape + (1,) * (taken.ndim - 1))
    return jnp.where(keep_mask, taken, jnp.zeros_like(taken))


def expert_pass(x_rows, dy_rows, g_rows, gate_w, up_w, down_w):
    pre_gate = jnp.dot(x_rows, gate_w, preferred_element_type=jnp.float32)
    pre_up = jnp.dot(x_rows, up_w, preferred_element_type=jnp.float32)
    sigmoid_gate = jax.nn.sigmoid(pre_gate)
    activated = pre_gate * sigmoid_gate
    hidden = (activated * pre_up).astype(jnp.bfloat16)
    expert_out = jnp.dot(hidden, down_w, preferred_element_type=jnp.float32)
    gate_grad = jnp.sum(dy_rows.astype(jnp.float32) * expert_out, axis=-1).astype(jnp.bfloat16)
    scaled = (g_rows.astype(jnp.float32)[:, None] * dy_rows.astype(jnp.float32)).astype(
        jnp.bfloat16
    )
    hidden_grad = lax.dot_general(
        scaled, down_w, (((1,), (1,)), ((), ())), preferred_element_type=jnp.float32
    )
    pre_gate_grad = (
        hidden_grad * pre_up * sigmoid_gate * (1.0 + pre_gate * (1.0 - sigmoid_gate))
    ).astype(jnp.bfloat16)
    pre_up_grad = (hidden_grad * activated).astype(jnp.bfloat16)
    route_grad = lax.dot_general(
        pre_gate_grad, gate_w, (((1,), (1,)), ((), ())), preferred_element_type=jnp.float32
    )
    route_grad = route_grad + lax.dot_general(
        pre_up_grad, up_w, (((1,), (1,)), ((), ())), preferred_element_type=jnp.float32
    )
    return (route_grad.astype(jnp.bfloat16), gate_grad, pre_gate_grad, pre_up_grad, hidden, scaled)


def on_device(tokens, out_grad, expert_ids, gates, w_gate, w_up, w_down):
    tok_rows, model_width = tokens.shape
    top_count = expert_ids.shape[1]
    peer_count = lax.axis_size("expert")
    capacity = min(tok_rows, tok_rows * top_count * 6 // (5 * peer_count))
    slot_total = peer_count * capacity
    places = slot_places(expert_ids, peer_count, capacity)
    source, filled = slot_sources(places, slot_total)
    token_source = source // top_count
    x_buf = fill_slots(tokens, token_source, filled).reshape(peer_count, capacity, model_width)
    dy_buf = fill_slots(out_grad, token_source, filled).reshape(peer_count, capacity, model_width)
    g_buf = fill_slots(gates.reshape(-1), source, filled).reshape(peer_count, capacity)
    gate_w = w_gate[0]
    up_w = w_up[0]
    down_w = w_down[0]
    hidden_width = gate_w.shape[1]
    x_in, dy_in, g_in = (
        lax.all_to_all(x_buf, "expert", split_axis=0, concat_axis=0, tiled=True),
        lax.all_to_all(dy_buf, "expert", split_axis=0, concat_axis=0, tiled=True),
        lax.all_to_all(g_buf, "expert", split_axis=0, concat_axis=0, tiled=True),
    )
    lead_dim = x_in.shape[0]
    item_total = x_in.shape[1]
    results = expert_pass(
        x_in.reshape(lead_dim * item_total, model_width),
        dy_in.reshape(lead_dim * item_total, model_width),
        g_in.reshape(lead_dim * item_total),
        gate_w,
        up_w,
        down_w,
    )
    route_grad, gate_grad, pre_gate_grad, pre_up_grad, hidden, scaled = tuple(
        (piece.reshape((lead_dim, item_total) + piece.shape[1:]) for piece in results)
    )
    back_dx, back_dg = (
        lax.all_to_all(route_grad, "expert", split_axis=0, concat_axis=0, tiled=True),
        lax.all_to_all(gate_grad, "expert", split_axis=0, concat_axis=0, tiled=True),
    )
    routed = back_dx.reshape(slot_total, model_width)[places]
    token_grad = jnp.sum(
        routed.reshape(tok_rows, top_count, model_width).astype(jnp.float32), axis=1
    ).astype(jnp.bfloat16)
    gate_grad_out = back_dg.reshape(slot_total)[places].reshape(tok_rows, top_count)
    x_rows = x_in.reshape(slot_total, model_width)
    scaled_rows = scaled.reshape(slot_total, model_width)
    gate_rows = pre_gate_grad.reshape(slot_total, hidden_width)
    up_rows = pre_up_grad.reshape(slot_total, hidden_width)
    hidden_rows = hidden.reshape(slot_total, hidden_width)
    contract = (((0,), (0,)), ((), ()))
    part_gate = lax.dot_general(x_rows, gate_rows, contract, preferred_element_type=jnp.float32)
    part_up = lax.dot_general(x_rows, up_rows, contract, preferred_element_type=jnp.float32)
    part_down = lax.dot_general(
        hidden_rows, scaled_rows, contract, preferred_element_type=jnp.float32
    )
    sum_gate, sum_up, sum_down = (
        lax.psum_scatter(
            part_gate.astype(jnp.bfloat16), "dp", scatter_dimension=0, tiled=True
        ).astype(jnp.float32),
        lax.psum_scatter(
            part_up.astype(jnp.bfloat16), "dp", scatter_dimension=0, tiled=True
        ).astype(jnp.float32),
        lax.psum_scatter(
            part_down.astype(jnp.bfloat16), "dp", scatter_dimension=1, tiled=True
        ).astype(jnp.float32),
    )
    return (
        token_grad,
        gate_grad_out,
        sum_gate.astype(jnp.bfloat16)[None],
        sum_up.astype(jnp.bfloat16)[None],
        sum_down.astype(jnp.bfloat16)[None],
    )


def chip_ring(expert_count):
    lines = 4
    chips = expert_count // 2
    depth = chips // 2
    order = [z * 2 for z in range(depth)] + [z * 2 + 1 for z in reversed(range(depth))]
    assert chips == 2 * depth and depth == lines
    return order


def ring_shift(expert_count, by):
    order = chip_ring(expert_count)
    n = len(order)
    pairs = []
    for place, chip in enumerate(order):
        for core in range(2):
            pairs.append((chip * 2 + core, order[(place + by) % n] * 2 + core))
    return sorted(pairs)


def on_ring(tokens, out_grad, expert_ids, gates, w_gate, w_up, w_down):
    rows, width = tokens.shape
    top_count = expert_ids.shape[1]
    experts = lax.axis_size("expert")
    forth, back = ring_shift(experts, 1), ring_shift(experts, -1)
    swap_core = [(i, i ^ 1) for i in range(experts)]
    me = lax.axis_index("expert")
    group = lax.axis_index("dp")
    f32, bf16 = jnp.float32, jnp.bfloat16
    gate_w, up_w, down_w = w_gate[0], w_up[0], w_down[0]
    half = width // lax.axis_size("dp")

    def go(value, pairs):
        return lax.ppermute(value, "expert", pairs)

    def sibling(value):
        return lax.ppermute(value, "expert", swap_core)

    def across(value):
        return lax.ppermute(value, "dp", [(0, 1), (1, 0)])

    meta = jnp.concatenate(
        [expert_ids.astype(bf16), gates, jnp.zeros((rows, 128 - 2 * top_count), bf16)], axis=1
    )
    own = jnp.concatenate([tokens, out_grad, meta], axis=1)

    ahead, behind = [own], [own]
    for _ in range(3):
        ahead.append(go(ahead[-1], forth))
        behind.append(go(behind[-1], back))
    far_x = go(ahead[3][:, :width], forth)
    far_rest = go(behind[3][:, width:], back)
    far = jnp.concatenate([far_x, far_rest], axis=1)
    near_parts = [[own], [ahead[1], behind[1]], [ahead[2], behind[2]], [ahead[3], behind[3]], [far]]
    other_parts = [[across(part) for part in parts] for parts in near_parts]

    def expert_rows(parts):
        chunk = jnp.concatenate(parts + [sibling(part) for part in parts], axis=0)
        x, dy = chunk[:, :width], chunk[:, width : 2 * width]
        chosen = chunk[:, 2 * width : 2 * width + top_count] == me.astype(bf16)
        row_gates = chunk[:, 2 * width + top_count : 2 * width + 2 * top_count]
        gate = jnp.sum(jnp.where(chosen, row_gates, 0).astype(f32), axis=1, keepdims=True)
        pre_gate = jnp.dot(x, gate_w, preferred_element_type=f32)
        pre_up = jnp.dot(x, up_w, preferred_element_type=f32)
        down_grad = lax.dot_general(dy, down_w, (((1,), (1,)), ((), ())), preferred_element_type=f32)
        sigmoid_gate = jax.nn.sigmoid(pre_gate)
        activated = pre_gate * sigmoid_gate
        hidden = activated * pre_up
        hidden_grad = gate * down_grad
        gate_grad = jnp.where(
            jnp.any(chosen, axis=1, keepdims=True),
            jnp.sum(hidden * down_grad, axis=1, keepdims=True),
            0.0,
        )
        pre_gate_grad = (
            hidden_grad * pre_up * sigmoid_gate * (1.0 + pre_gate * (1.0 - sigmoid_gate))
        ).astype(bf16)
        pre_up_grad = (hidden_grad * activated).astype(bf16)
        scaled_hidden = (gate * hidden).astype(bf16)
        return x, dy, gate_grad, pre_gate_grad, pre_up_grad, scaled_hidden

    def input_grad(gate_grad, pre_gate_grad, pre_up_grad):
        contract = (((1,), (1,)), ((), ()))
        route = lax.dot_general(pre_gate_grad, gate_w, contract, preferred_element_type=f32)
        route = route + lax.dot_general(pre_up_grad, up_w, contract, preferred_element_type=f32)
        lanes = jnp.where(jnp.arange(128) == me, gate_grad, 0.0)
        return jnp.concatenate([route.astype(bf16), lanes.astype(bf16)], axis=1)

    near = [expert_rows(parts) for parts in near_parts]
    sums = []
    for parts, items in zip(near_parts, near):
        grads = input_grad(*items[2:5])
        mine = rows * len(parts)
        sums.append(grads[:mine].astype(f32) + sibling(grads[mine:]).astype(f32))

    cut = width // 2
    forth_sum = go(sums[4][:, :cut].astype(bf16), forth).astype(f32)
    back_sum = go(sums[4][:, cut:].astype(bf16), back).astype(f32)
    forth_sum = jnp.pad(forth_sum, ((0, 0), (0, width + 128 - cut)))
    back_sum = jnp.pad(back_sum, ((0, 0), (cut, 0)))
    for step in (3, 2, 1):
        forth_sum = go((sums[step][rows:] + forth_sum).astype(bf16), forth).astype(f32)
        back_sum = go((sums[step][:rows] + back_sum).astype(bf16), back).astype(f32)
    total = sums[0] + forth_sum + back_sum
    token_grad = total[:, :width].astype(bf16)
    gate_table = total[:, width : width + experts]
    picked = expert_ids[:, :, None] == jnp.arange(experts, dtype=jnp.int32)
    gate_grad_out = jnp.sum(jnp.where(picked, gate_table[:, None, :], 0.0), axis=2).astype(bf16)

    others = [expert_rows(parts) for parts in other_parts]
    contract = (((0,), (0,)), ((), ()))

    def weight_grads(items):
        x = jnp.concatenate([lax.dynamic_slice_in_dim(i[0], group * half, half, 1) for i in items], axis=0)
        dy = jnp.concatenate([lax.dynamic_slice_in_dim(i[1], group * half, half, 1) for i in items], axis=0)
        gate_rows, up_rows, hidden_rows = (
            jnp.concatenate([i[place] for i in items], axis=0) for place in (3, 4, 5)
        )
        return (
            lax.dot_general(x, gate_rows, contract, preferred_element_type=f32),
            lax.dot_general(x, up_rows, contract, preferred_element_type=f32),
            lax.dot_general(hidden_rows, dy, contract, preferred_element_type=f32),
        )

    grads = [
        (first + second).astype(bf16)[None]
        for first, second in zip(weight_grads(near), weight_grads(others))
    ]
    return (token_grad, gate_grad_out, *grads)


def solution(mesh):
    in_specs = (
        P(("dp", "expert"), None),
        P(("dp", "expert"), None),
        P(("dp", "expert"), None),
        P(("dp", "expert"), None),
        P("expert", None, None),
        P("expert", None, None),
        P("expert", None, None),
    )
    out_specs = (
        P(("dp", "expert"), None),
        P(("dp", "expert"), None),
        P("expert", "dp", None),
        P("expert", "dp", None),
        P("expert", None, "dp"),
    )
    on_slice = on_ring if (mesh.shape["dp"], mesh.shape["expert"]) == (2, 16) else on_device
    return jax.shard_map(
        on_slice, mesh=mesh, in_specs=in_specs, out_specs=out_specs, check_vma=False
    )
```

```python
import functools

import jax
import jax.numpy as jnp
from jax import lax
from jax.experimental import pallas as pl
from jax.experimental.pallas import tpu as pltpu
from jax.sharding import PartitionSpec as P


def slot_places(expert_ids, experts, capacity):
    flat_ids = expert_ids.reshape(-1)
    labels = jnp.arange(experts, dtype=jnp.int32)
    onehot = (flat_ids[:, None] == labels[None, :]).astype(jnp.int32)
    earlier = jnp.cumsum(onehot, axis=0) - onehot
    slot_index = jnp.sum(earlier * onehot, axis=1)
    return flat_ids * capacity + slot_index


def slot_sources(places, slot_total):
    route_total = places.shape[0]
    filler = (
        jnp.zeros((slot_total,), jnp.int32)
        .at[places]
        .set(jnp.arange(route_total, dtype=jnp.int32) + 1)
    )
    return (jnp.maximum(filler - 1, 0), filler > 0)


def fill_slots(values, source, filled):
    taken = values[source]
    keep_mask = filled.reshape(filled.shape + (1,) * (taken.ndim - 1))
    return jnp.where(keep_mask, taken, jnp.zeros_like(taken))


def expert_pass(x_rows, dy_rows, g_rows, gate_w, up_w, down_w):
    pre_gate = jnp.dot(x_rows, gate_w, preferred_element_type=jnp.float32)
    pre_up = jnp.dot(x_rows, up_w, preferred_element_type=jnp.float32)
    sigmoid_gate = jax.nn.sigmoid(pre_gate)
    activated = pre_gate * sigmoid_gate
    hidden = (activated * pre_up).astype(jnp.bfloat16)
    expert_out = jnp.dot(hidden, down_w, preferred_element_type=jnp.float32)
    gate_grad = jnp.sum(dy_rows.astype(jnp.float32) * expert_out, axis=-1).astype(jnp.bfloat16)
    scaled = (g_rows.astype(jnp.float32)[:, None] * dy_rows.astype(jnp.float32)).astype(
        jnp.bfloat16
    )
    hidden_grad = lax.dot_general(
        scaled, down_w, (((1,), (1,)), ((), ())), preferred_element_type=jnp.float32
    )
    pre_gate_grad = (
        hidden_grad * pre_up * sigmoid_gate * (1.0 + pre_gate * (1.0 - sigmoid_gate))
    ).astype(jnp.bfloat16)
    pre_up_grad = (hidden_grad * activated).astype(jnp.bfloat16)
    route_grad = lax.dot_general(
        pre_gate_grad, gate_w, (((1,), (1,)), ((), ())), preferred_element_type=jnp.float32
    )
    route_grad = route_grad + lax.dot_general(
        pre_up_grad, up_w, (((1,), (1,)), ((), ())), preferred_element_type=jnp.float32
    )
    return (route_grad.astype(jnp.bfloat16), gate_grad, pre_gate_grad, pre_up_grad, hidden, scaled)


def on_device(tokens, out_grad, expert_ids, gates, w_gate, w_up, w_down):
    tok_rows, model_width = tokens.shape
    top_count = expert_ids.shape[1]
    peer_count = lax.axis_size("expert")
    capacity = min(tok_rows, tok_rows * top_count * 6 // (5 * peer_count))
    slot_total = peer_count * capacity
    places = slot_places(expert_ids, peer_count, capacity)
    source, filled = slot_sources(places, slot_total)
    token_source = source // top_count
    x_buf = fill_slots(tokens, token_source, filled).reshape(peer_count, capacity, model_width)
    dy_buf = fill_slots(out_grad, token_source, filled).reshape(peer_count, capacity, model_width)
    g_buf = fill_slots(gates.reshape(-1), source, filled).reshape(peer_count, capacity)
    gate_w = w_gate[0]
    up_w = w_up[0]
    down_w = w_down[0]
    hidden_width = gate_w.shape[1]
    x_in, dy_in, g_in = (
        lax.all_to_all(x_buf, "expert", split_axis=0, concat_axis=0, tiled=True),
        lax.all_to_all(dy_buf, "expert", split_axis=0, concat_axis=0, tiled=True),
        lax.all_to_all(g_buf, "expert", split_axis=0, concat_axis=0, tiled=True),
    )
    lead_dim = x_in.shape[0]
    item_total = x_in.shape[1]
    results = expert_pass(
        x_in.reshape(lead_dim * item_total, model_width),
        dy_in.reshape(lead_dim * item_total, model_width),
        g_in.reshape(lead_dim * item_total),
        gate_w,
        up_w,
        down_w,
    )
    route_grad, gate_grad, pre_gate_grad, pre_up_grad, hidden, scaled = tuple(
        (piece.reshape((lead_dim, item_total) + piece.shape[1:]) for piece in results)
    )
    back_dx, back_dg = (
        lax.all_to_all(route_grad, "expert", split_axis=0, concat_axis=0, tiled=True),
        lax.all_to_all(gate_grad, "expert", split_axis=0, concat_axis=0, tiled=True),
    )
    routed = back_dx.reshape(slot_total, model_width)[places]
    token_grad = jnp.sum(
        routed.reshape(tok_rows, top_count, model_width).astype(jnp.float32), axis=1
    ).astype(jnp.bfloat16)
    gate_grad_out = back_dg.reshape(slot_total)[places].reshape(tok_rows, top_count)
    x_rows = x_in.reshape(slot_total, model_width)
    scaled_rows = scaled.reshape(slot_total, model_width)
    gate_rows = pre_gate_grad.reshape(slot_total, hidden_width)
    up_rows = pre_up_grad.reshape(slot_total, hidden_width)
    hidden_rows = hidden.reshape(slot_total, hidden_width)
    contract = (((0,), (0,)), ((), ()))
    part_gate = lax.dot_general(x_rows, gate_rows, contract, preferred_element_type=jnp.float32)
    part_up = lax.dot_general(x_rows, up_rows, contract, preferred_element_type=jnp.float32)
    part_down = lax.dot_general(
        hidden_rows, scaled_rows, contract, preferred_element_type=jnp.float32
    )
    sum_gate, sum_up, sum_down = (
        lax.psum_scatter(
            part_gate.astype(jnp.bfloat16), "dp", scatter_dimension=0, tiled=True
        ).astype(jnp.float32),
        lax.psum_scatter(
            part_up.astype(jnp.bfloat16), "dp", scatter_dimension=0, tiled=True
        ).astype(jnp.float32),
        lax.psum_scatter(
            part_down.astype(jnp.bfloat16), "dp", scatter_dimension=1, tiled=True
        ).astype(jnp.float32),
    )
    return (
        token_grad,
        gate_grad_out,
        sum_gate.astype(jnp.bfloat16)[None],
        sum_up.astype(jnp.bfloat16)[None],
        sum_down.astype(jnp.bfloat16)[None],
    )


F32, BF16 = jnp.float32, jnp.bfloat16
ROWS_BY_ROWS = (((1,), (1,)), ((), ()))
OVER_ROWS = (((0,), (0,)), ((), ()))
LANES = 128
KERNEL_VMEM = 16 * 2**20
IN_VMEM = pl.BlockSpec(memory_space=pltpu.VMEM)
IN_SMEM = pl.BlockSpec(memory_space=pltpu.SMEM)
NO_COST = pl.CostEstimate(flops=0, bytes_accessed=0, transcendentals=0)


def tiles(total, step):
    return [slice(at, min(at + step, total)) for at in range(0, total, step)]


def stacked(refs, columns):
    return jnp.concatenate([ref[:, columns] for ref in refs], axis=0)


def add_products(blocks, earlier, store):
    hidden_width, _ = blocks[0](0, None)
    for which in range(3):
        for cols in tiles(hidden_width, 256):
            total = earlier[which][cols, :] if earlier else 0.0
            for block in blocks:
                left, right = block(which, cols)
                total += lax.dot_general(left, right, OVER_ROWS, preferred_element_type=F32)
            store(which, cols, total)


def dense_block(parts, grads, start, half, width):
    def block(which, cols):
        if cols is None:
            return grads[0].shape[1], None
        columns = pl.ds(start + (width if which == 2 else 0), half)
        return grads[which][:, cols], stacked(parts, columns)

    return block


def slot_block(ref, half, hidden_width):
    def block(which, cols):
        if cols is None:
            return hidden_width, None
        at = 2 * half + which * hidden_width
        first = half if which == 2 else 0
        return ref[:, at + cols.start : at + cols.stop], ref[:, first : first + half]

    return block


def rows_kernel(part_total, slot_total, has_sums, adds, tok_rows, slots, top_count, half, *refs):
    me_ref, group_ref, refs = refs[0], refs[1], list(refs[2:])

    def take(count):
        taken = refs[:count]
        del refs[:count]
        return taken

    parts, (gate_w, up_w, down_w) = take(part_total), take(3)
    came = take(slot_total)
    earlier = take(3) if has_sums else None
    kept_out, given_out, slots_out = take(3)
    sums = take(3) if adds else None
    grads = take(3)
    pre_gate_out, pre_up_out, hidden_out = grads
    hidden_width, width = gate_w.shape
    x = stacked(parts, slice(0, width))
    dy = stacked(parts, slice(width, 2 * width))
    routing = stacked(parts, slice(2 * width, 2 * width + LANES)).astype(F32)
    total_rows = routing.shape[0]
    lane = lax.broadcasted_iota(jnp.int32, routing.shape, 1)
    me = me_ref[0]
    chosen = (routing == me.astype(F32)) & (lane < top_count)
    shifted = pltpu.roll(routing, LANES - top_count, 1)
    gate = jnp.sum(jnp.where(chosen, shifted, 0.0), axis=1, keepdims=True)
    taken = jnp.sum(jnp.where(chosen, 1.0, 0.0), axis=1, keepdims=True)
    gate_grad = jnp.zeros_like(gate)
    for cols in tiles(hidden_width, 256):
        pre_gate = lax.dot_general(x, gate_w[cols, :], ROWS_BY_ROWS, preferred_element_type=F32)
        pre_up = lax.dot_general(x, up_w[cols, :], ROWS_BY_ROWS, preferred_element_type=F32)
        down_grad = lax.dot_general(dy, down_w[cols, :], ROWS_BY_ROWS, preferred_element_type=F32)
        sigmoid_gate = jax.nn.sigmoid(pre_gate)
        activated = pre_gate * sigmoid_gate
        hidden = activated * pre_up
        gate_grad += jnp.sum(hidden * down_grad, axis=1, keepdims=True)
        hidden_grad = gate * down_grad
        slope = sigmoid_gate * (1.0 + pre_gate * (1.0 - sigmoid_gate))
        pre_gate_out[:, cols] = (hidden_grad * pre_up * slope).astype(BF16)
        pre_up_out[:, cols] = (hidden_grad * activated).astype(BF16)
        hidden_out[:, cols] = (gate * hidden).astype(BF16)
    half_rows = total_rows // 2
    table = jnp.where(lane == me, gate_grad * taken, 0.0).astype(BF16)
    kept_out[:, width:] = table[:half_rows]
    given_out[:, width:] = table[half_rows:]
    for cols in tiles(width, 512):
        route = jnp.dot(pre_gate_out[...], gate_w[:, cols], preferred_element_type=F32)
        route += jnp.dot(pre_up_out[...], up_w[:, cols], preferred_element_type=F32)
        route = route.astype(BF16)
        kept_out[:, cols] = route[:half_rows]
        given_out[:, cols] = route[half_rows:]

    row = lax.broadcasted_iota(jnp.int32, (total_rows, total_rows), 0)
    other = lax.broadcasted_iota(jnp.int32, (total_rows, total_rows), 1)
    before = (other < row) & (other >= row - row % tok_rows)
    taken_lanes = jnp.broadcast_to(taken, routing.shape).astype(BF16)
    count = jnp.dot(before.astype(BF16), taken_lanes, preferred_element_type=F32)
    block_of = lax.broadcasted_iota(jnp.int32, routing.shape, 0) // tok_rows
    place = jnp.where(taken > 0.0, count.astype(jnp.int32) + block_of * slots, LANES)
    picks = (place == lane).astype(BF16)
    slot_rows = slots_out.shape[0]

    def filled(values):
        rows = lax.dot_general(picks, values, OVER_ROWS, preferred_element_type=F32)
        return rows[:slot_rows].astype(BF16)

    away = pl.multiple_of((1 - group_ref[0]) * half, half)
    slots_out[:, :half] = filled(stacked(parts, pl.ds(away, half)))
    slots_out[:, half : 2 * half] = filled(stacked(parts, pl.ds(width + away, half)))
    for which in range(3):
        at = 2 * half + which * hidden_width
        slots_out[:, at : at + hidden_width] = filled(grads[which][...])

    if adds:
        start = pl.multiple_of(group_ref[0] * half, half)
        blocks = [dense_block(parts, grads, start, half, width)]
        blocks += [slot_block(ref, half, hidden_width) for ref in came]

        def store(which, cols, total):
            sums[which][cols, :] = total

        add_products(blocks, earlier, store)


def expert_rows(parts, weights, place, sizes, sums=None, came=(), adds=True):
    me, group = place
    tok_rows, slots, top_count, half = sizes
    total = sum(part.shape[0] for part in parts)
    hidden_width, width = weights[0].shape
    slot_rows = -(-(total // tok_rows * slots) // 16) * 16
    operands = [*parts, *weights, *came, *(sums or ())]
    wide = jax.ShapeDtypeStruct((total // 2, width + LANES), BF16)
    packed = jax.ShapeDtypeStruct((slot_rows, 2 * half + 3 * hidden_width), BF16)
    grad = jax.ShapeDtypeStruct((total, hidden_width), BF16)
    added = jax.ShapeDtypeStruct((hidden_width, half), F32)
    results = [wide, wide, packed] + ([added] * 3 if adds else [grad] * 3)
    first_sum = 2 + len(operands) - 3
    results = pl.pallas_call(
        functools.partial(
            rows_kernel, len(parts), len(came), sums is not None, adds, tok_rows, slots, top_count, half
        ),
        out_shape=results,
        in_specs=[IN_SMEM] * 2 + [IN_VMEM] * len(operands),
        out_specs=[IN_VMEM] * len(results),
        input_output_aliases={first_sum + i: 3 + i for i in range(3)} if sums else {},
        scratch_shapes=[pltpu.VMEM(grad.shape, BF16)] * (3 * adds),
        compiler_params=pltpu.CompilerParams(vmem_limit_bytes=KERNEL_VMEM),
        cost_estimate=NO_COST,
    )(me, group, *operands)
    return list(results[:2]), results[2], list(results[3:])


def sums_kernel(part_total, slot_total, has_last, half, width, *refs):
    group_ref, refs = refs[0], list(refs[1:])

    def take(count):
        taken = refs[:count]
        del refs[:count]
        return taken

    parts, grads = take(part_total), take(3 if part_total else 0)
    came, earlier, outs = take(slot_total), take(3), take(3)
    hidden_width = earlier[0].shape[0]
    blocks = [slot_block(ref, half, hidden_width) for ref in came]
    if parts:
        start = pl.multiple_of(group_ref[0] * half, half)
        blocks.append(dense_block(parts, grads, start, half, width))
    if not has_last:

        def store(which, cols, total):
            outs[which][cols, :] = total

        add_products(blocks, earlier, store)
        return
    rounded, sent = refs

    def store(which, cols, total):
        rounded[which, cols, :] = total.astype(BF16)
        pltpu.make_async_copy(
            rounded.at[which, cols, :], outs[which].at[cols, :], sent.at[which]
        ).start()

    add_products(blocks, earlier, store)
    for which in range(3):
        pltpu.make_async_copy(rounded.at[which], outs[which], sent.at[which]).wait()


def add_rows(came, sums, group, width, parts=(), grads=(), last=False):
    hidden_width, half = sums[0].shape
    operands = [*parts, *grads, *came, *sums]
    added = jax.ShapeDtypeStruct((hidden_width, half), BF16 if last else F32)
    scratch = [pltpu.VMEM((3, hidden_width, half), BF16), pltpu.SemaphoreType.DMA((3,))]
    first_sum = 1 + len(operands) - 3
    return list(
        pl.pallas_call(
            functools.partial(sums_kernel, len(parts), len(came), last, half, width),
            out_shape=[added] * 3,
            in_specs=[IN_SMEM] + [IN_VMEM] * len(operands),
            out_specs=[pl.BlockSpec(memory_space=pl.ANY) if last else IN_VMEM] * 3,
            input_output_aliases={} if last else {first_sum + i: i for i in range(3)},
            scratch_shapes=scratch if last else [],
            compiler_params=pltpu.CompilerParams(vmem_limit_bytes=KERNEL_VMEM),
            cost_estimate=NO_COST,
        )(group, *operands)
    )


def chip_ring(expert_count):
    depth = expert_count // 4
    return [2 * z for z in range(depth)] + [2 * z + 1 for z in reversed(range(depth))]


def ring_shift(expert_count, by):
    order = chip_ring(expert_count)
    total = len(order)
    return sorted(
        (2 * chip + core, 2 * order[(place + by) % total] + core)
        for place, chip in enumerate(order)
        for core in range(2)
    )


def on_ring(tokens, out_grad, expert_ids, gates, w_gate, w_up, w_down):
    rows, width = tokens.shape
    top_count = expert_ids.shape[1]
    experts = lax.axis_size("expert")
    half = width // lax.axis_size("dp")
    capacity = min(rows, rows * top_count * 6 // (5 * experts))
    sizes = (rows, capacity, top_count, half)
    forth, back = ring_shift(experts, 1), ring_shift(experts, -1)
    me = lax.axis_index("expert").astype(jnp.int32)[None]
    group = lax.axis_index("dp").astype(jnp.int32)[None]
    weights = (w_gate[0].T, w_up[0].T, w_down[0])
    place = (me, group)
    stage = lax.optimization_barrier

    def go(value, pairs):
        return lax.ppermute(value, "expert", pairs)

    def sibling(value):
        return lax.ppermute(value, "expert", [(i, i ^ 1) for i in range(experts)])

    def across(value):
        return lax.ppermute(value, "dp", [(0, 1), (1, 0)])

    def near_rows(parts, sums, **options):
        parts = parts + [sibling(part) for part in parts]
        return expert_rows(parts, weights, place, sizes, sums, **options)

    def passed_on(item, fore, rear):
        total = item[0].astype(F32) + item[1].astype(F32)
        fore = go((total[rows:] + fore.astype(F32)).astype(BF16), forth)
        rear = go((total[:rows] + rear.astype(F32)).astype(BF16), back)
        return fore, rear

    routing = jnp.concatenate(
        [expert_ids.astype(BF16), gates, jnp.zeros((rows, LANES - 2 * top_count), BF16)], axis=1
    )
    own = jnp.concatenate([tokens, out_grad, routing], axis=1)

    fore, rear = go(own, forth), go(own, back)
    near0, slots0, sums = near_rows([own], None)
    fore, rear, near0, slots0, sums = stage((fore, rear, near0, slots0, sums))

    held = [fore, rear]
    fore, rear, came0 = go(fore, forth), go(rear, back), across(slots0)
    near1, slots1, sums = near_rows(held, sums)
    fore, rear, came0, near1, slots1, sums = stage((fore, rear, came0, near1, slots1, sums))

    held = [fore, rear]
    fore, rear, came1 = go(fore, forth), go(rear, back), across(slots1)
    near2, slots2, sums = near_rows(held, sums, came=[came0])
    fore, rear, near2, slots2, sums = stage((fore, rear, near2, slots2, sums))

    held = [fore, rear]
    far_x, far_rest = go(fore[:, :width], forth), go(rear[:, width:], back)
    near3, slots3, sums = near_rows(held, sums)
    far_x, far_rest, came1, near3, slots3, sums = stage(
        (far_x, far_rest, came1, near3, slots3, sums)
    )

    came2 = across(slots2)
    far = jnp.concatenate([far_x, far_rest], axis=1)
    far_parts = [far, sibling(far)]
    near3[1] = sibling(near3[1])
    near4, slots4, grads4 = expert_rows(far_parts, weights, place, sizes, adds=False)
    near3, near4, slots4, grads4, far_parts = stage((near3, near4, slots4, grads4, far_parts))
    near4[1] = sibling(near4[1])
    sum4 = (near4[0].astype(F32) + near4[1].astype(F32)).astype(BF16)
    cut = width // 2
    fore, rear = go(sum4[:, :cut], forth), go(sum4[:, cut:], back)
    sums = add_rows([came1], sums, group, width, far_parts, grads4)
    fore, rear, came2, sums = stage((fore, rear, came2, sums))
    fore = jnp.pad(fore, ((0, 0), (0, width + LANES - cut)))
    rear = jnp.pad(rear, ((0, 0), (cut, 0)))

    came3 = across(slots3)
    fore, rear = passed_on(near3, fore, rear)
    near2[1] = sibling(near2[1])
    sums = add_rows([came2], sums, group, width)
    fore, rear, near2, sums = stage((fore, rear, near2, sums))

    fore, rear = passed_on(near2, fore, rear)
    near1[1] = sibling(near1[1])
    fore, rear, came3, near1 = stage((fore, rear, came3, near1))

    came4 = across(slots4)
    fore, rear = passed_on(near1, fore, rear)
    near0[1] = sibling(near0[1])
    sums = add_rows([came3], sums, group, width)
    fore, rear, near0, came4, sums = stage((fore, rear, near0, came4, sums))

    total = near0[0].astype(F32) + near0[1].astype(F32) + fore.astype(F32) + rear.astype(F32)
    token_grad = total[:, :width].astype(BF16)
    gate_table = total[:, width : width + experts]
    picked = expert_ids[:, :, None] == jnp.arange(experts, dtype=jnp.int32)
    gate_grad = jnp.sum(jnp.where(picked, gate_table[:, None, :], 0.0), axis=2).astype(BF16)
    sums = add_rows([came4], sums, group, width, last=True)
    return (token_grad, gate_grad, sums[0].T[None], sums[1].T[None], sums[2][None])


def solution(mesh):
    in_specs = (
        P(("dp", "expert"), None),
        P(("dp", "expert"), None),
        P(("dp", "expert"), None),
        P(("dp", "expert"), None),
        P("expert", None, None),
        P("expert", None, None),
        P("expert", None, None),
    )
    out_specs = (
        P(("dp", "expert"), None),
        P(("dp", "expert"), None),
        P("expert", "dp", None),
        P("expert", "dp", None),
        P("expert", None, "dp"),
    )
    on_slice = on_ring if (mesh.shape["dp"], mesh.shape["expert"]) == (2, 16) else on_device
    return jax.shard_map(
        on_slice, mesh=mesh, in_specs=in_specs, out_specs=out_specs, check_vma=False
    )
```

```python
import functools

import jax
import jax.numpy as jnp
from jax import lax
from jax.experimental import pallas as pl
from jax.experimental.pallas import tpu as pltpu
from jax.sharding import PartitionSpec as P


def slot_places(expert_ids, experts, capacity):
    flat_ids = expert_ids.reshape(-1)
    labels = jnp.arange(experts, dtype=jnp.int32)
    onehot = (flat_ids[:, None] == labels[None, :]).astype(jnp.int32)
    earlier = jnp.cumsum(onehot, axis=0) - onehot
    slot_index = jnp.sum(earlier * onehot, axis=1)
    return flat_ids * capacity + slot_index


def slot_sources(places, slot_total):
    route_total = places.shape[0]
    filler = (
        jnp.zeros((slot_total,), jnp.int32)
        .at[places]
        .set(jnp.arange(route_total, dtype=jnp.int32) + 1)
    )
    return (jnp.maximum(filler - 1, 0), filler > 0)


def fill_slots(values, source, filled):
    taken = values[source]
    keep_mask = filled.reshape(filled.shape + (1,) * (taken.ndim - 1))
    return jnp.where(keep_mask, taken, jnp.zeros_like(taken))


def expert_pass(x_rows, dy_rows, g_rows, gate_w, up_w, down_w):
    pre_gate = jnp.dot(x_rows, gate_w, preferred_element_type=jnp.float32)
    pre_up = jnp.dot(x_rows, up_w, preferred_element_type=jnp.float32)
    sigmoid_gate = jax.nn.sigmoid(pre_gate)
    activated = pre_gate * sigmoid_gate
    hidden = (activated * pre_up).astype(jnp.bfloat16)
    expert_out = jnp.dot(hidden, down_w, preferred_element_type=jnp.float32)
    gate_grad = jnp.sum(dy_rows.astype(jnp.float32) * expert_out, axis=-1).astype(jnp.bfloat16)
    scaled = (g_rows.astype(jnp.float32)[:, None] * dy_rows.astype(jnp.float32)).astype(
        jnp.bfloat16
    )
    hidden_grad = lax.dot_general(
        scaled, down_w, (((1,), (1,)), ((), ())), preferred_element_type=jnp.float32
    )
    pre_gate_grad = (
        hidden_grad * pre_up * sigmoid_gate * (1.0 + pre_gate * (1.0 - sigmoid_gate))
    ).astype(jnp.bfloat16)
    pre_up_grad = (hidden_grad * activated).astype(jnp.bfloat16)
    route_grad = lax.dot_general(
        pre_gate_grad, gate_w, (((1,), (1,)), ((), ())), preferred_element_type=jnp.float32
    )
    route_grad = route_grad + lax.dot_general(
        pre_up_grad, up_w, (((1,), (1,)), ((), ())), preferred_element_type=jnp.float32
    )
    return (route_grad.astype(jnp.bfloat16), gate_grad, pre_gate_grad, pre_up_grad, hidden, scaled)


def on_device(tokens, out_grad, expert_ids, gates, w_gate, w_up, w_down):
    tok_rows, model_width = tokens.shape
    top_count = expert_ids.shape[1]
    peer_count = lax.axis_size("expert")
    capacity = min(tok_rows, tok_rows * top_count * 6 // (5 * peer_count))
    slot_total = peer_count * capacity
    places = slot_places(expert_ids, peer_count, capacity)
    source, filled = slot_sources(places, slot_total)
    token_source = source // top_count
    x_buf = fill_slots(tokens, token_source, filled).reshape(peer_count, capacity, model_width)
    dy_buf = fill_slots(out_grad, token_source, filled).reshape(peer_count, capacity, model_width)
    g_buf = fill_slots(gates.reshape(-1), source, filled).reshape(peer_count, capacity)
    gate_w = w_gate[0]
    up_w = w_up[0]
    down_w = w_down[0]
    hidden_width = gate_w.shape[1]
    x_in, dy_in, g_in = (
        lax.all_to_all(x_buf, "expert", split_axis=0, concat_axis=0, tiled=True),
        lax.all_to_all(dy_buf, "expert", split_axis=0, concat_axis=0, tiled=True),
        lax.all_to_all(g_buf, "expert", split_axis=0, concat_axis=0, tiled=True),
    )
    lead_dim = x_in.shape[0]
    item_total = x_in.shape[1]
    results = expert_pass(
        x_in.reshape(lead_dim * item_total, model_width),
        dy_in.reshape(lead_dim * item_total, model_width),
        g_in.reshape(lead_dim * item_total),
        gate_w,
        up_w,
        down_w,
    )
    route_grad, gate_grad, pre_gate_grad, pre_up_grad, hidden, scaled = tuple(
        (piece.reshape((lead_dim, item_total) + piece.shape[1:]) for piece in results)
    )
    back_dx, back_dg = (
        lax.all_to_all(route_grad, "expert", split_axis=0, concat_axis=0, tiled=True),
        lax.all_to_all(gate_grad, "expert", split_axis=0, concat_axis=0, tiled=True),
    )
    routed = back_dx.reshape(slot_total, model_width)[places]
    token_grad = jnp.sum(
        routed.reshape(tok_rows, top_count, model_width).astype(jnp.float32), axis=1
    ).astype(jnp.bfloat16)
    gate_grad_out = back_dg.reshape(slot_total)[places].reshape(tok_rows, top_count)
    x_rows = x_in.reshape(slot_total, model_width)
    scaled_rows = scaled.reshape(slot_total, model_width)
    gate_rows = pre_gate_grad.reshape(slot_total, hidden_width)
    up_rows = pre_up_grad.reshape(slot_total, hidden_width)
    hidden_rows = hidden.reshape(slot_total, hidden_width)
    contract = (((0,), (0,)), ((), ()))
    part_gate = lax.dot_general(x_rows, gate_rows, contract, preferred_element_type=jnp.float32)
    part_up = lax.dot_general(x_rows, up_rows, contract, preferred_element_type=jnp.float32)
    part_down = lax.dot_general(
        hidden_rows, scaled_rows, contract, preferred_element_type=jnp.float32
    )
    sum_gate, sum_up, sum_down = (
        lax.psum_scatter(
            part_gate.astype(jnp.bfloat16), "dp", scatter_dimension=0, tiled=True
        ).astype(jnp.float32),
        lax.psum_scatter(
            part_up.astype(jnp.bfloat16), "dp", scatter_dimension=0, tiled=True
        ).astype(jnp.float32),
        lax.psum_scatter(
            part_down.astype(jnp.bfloat16), "dp", scatter_dimension=1, tiled=True
        ).astype(jnp.float32),
    )
    return (
        token_grad,
        gate_grad_out,
        sum_gate.astype(jnp.bfloat16)[None],
        sum_up.astype(jnp.bfloat16)[None],
        sum_down.astype(jnp.bfloat16)[None],
    )


F32, BF16 = jnp.float32, jnp.bfloat16
ROWS_BY_ROWS = (((1,), (1,)), ((), ()))
OVER_ROWS = (((0,), (0,)), ((), ()))
LANES = 128
KERNEL_VMEM = 16 * 2**20
IN_VMEM = pl.BlockSpec(memory_space=pltpu.VMEM)
NO_COST = pl.CostEstimate(flops=0, bytes_accessed=0, transcendentals=0)


def tiles(total, step):
    return [slice(at, min(at + step, total)) for at in range(0, total, step)]


def take_parts(refs, layout):
    return [tuple(refs.pop(0) for _ in range(count)) for count in layout]


def stacked(parts, width, start, size):
    in_rest, at = start

    def read(part):
        if len(part) == 2:
            return part[in_rest][:, pl.ds(at, size)]
        return part[0][:, pl.ds(at + width if in_rest else at, size)]

    return jnp.concatenate([read(part) for part in parts], axis=0)


def add_products(blocks, earlier, store, hidden_width):
    for which in range(3):
        for cols in tiles(hidden_width, 256):
            total = earlier[which][cols, :] if earlier else 0.0
            for block in blocks:
                left, right = block(which, cols)
                total += lax.dot_general(left, right, OVER_ROWS, preferred_element_type=F32)
            store(which, cols, total)


def dense_block(parts, grads, start, half, width):
    def block(which, cols):
        return grads[which][:, cols], stacked(parts, width, (which == 2, start), half)

    return block


def slot_block(ref, half, hidden_width):
    def block(which, cols):
        at = 2 * half + which * hidden_width
        first = half if which == 2 else 0
        return ref[:, at + cols.start : at + cols.stop], ref[:, first : first + half]

    return block


def rows_kernel(layout, packs, waiting, slot_total, has_sums, adds, routed, sizes, *refs):
    refs = list(refs)
    tok_rows, slots, top_count, half = sizes
    me, group = lax.axis_index("expert"), lax.axis_index("dp")

    def take(count):
        taken = refs[:count]
        del refs[:count]
        return taken

    parts, (gate_w, up_w, down_w) = take_parts(refs, layout), take(3)
    dense = [(take_parts(refs, parts_layout), take(3)) for parts_layout in waiting]
    came = take(slot_total)
    earlier = take(3) if has_sums else None
    kept_out, given_out = take(2) if routed else (None, None)
    slots_outs = take(len(packs))
    sums = take(3) if adds else None
    grads = take(3)
    pre_gate_out, pre_up_out, hidden_out = grads
    hidden_width, width = gate_w.shape
    x = stacked(parts, width, (0, 0), width)
    dy = stacked(parts, width, (1, 0), width)
    routing = stacked(parts, width, (1, width), LANES).astype(F32)
    total_rows = routing.shape[0]
    lane = lax.broadcasted_iota(jnp.int32, routing.shape, 1)
    chosen = (routing == me.astype(F32)) & (lane < top_count)
    shifted = pltpu.roll(routing, LANES - top_count, 1)
    gate = jnp.sum(jnp.where(chosen, shifted, 0.0), axis=1, keepdims=True)
    taken = jnp.sum(jnp.where(chosen, 1.0, 0.0), axis=1, keepdims=True)
    gate_grad = jnp.zeros_like(gate)
    for cols in tiles(hidden_width, 256):
        pre_gate = lax.dot_general(x, gate_w[cols, :], ROWS_BY_ROWS, preferred_element_type=F32)
        pre_up = lax.dot_general(x, up_w[cols, :], ROWS_BY_ROWS, preferred_element_type=F32)
        down_grad = lax.dot_general(dy, down_w[cols, :], ROWS_BY_ROWS, preferred_element_type=F32)
        sigmoid_gate = jax.nn.sigmoid(pre_gate)
        activated = pre_gate * sigmoid_gate
        hidden = activated * pre_up
        gate_grad += jnp.sum(hidden * down_grad, axis=1, keepdims=True)
        hidden_grad = gate * down_grad
        slope = sigmoid_gate * (1.0 + pre_gate * (1.0 - sigmoid_gate))
        pre_gate_out[:, cols] = (hidden_grad * pre_up * slope).astype(BF16)
        pre_up_out[:, cols] = (hidden_grad * activated).astype(BF16)
        hidden_out[:, cols] = (gate * hidden).astype(BF16)
    if routed:
        half_rows = total_rows // 2
        table = jnp.where(lane == me, gate_grad * taken, 0.0).astype(BF16)
        kept_out[:, width:] = table[:half_rows]
        given_out[:, width:] = table[half_rows:]
        for cols in tiles(width, 512):
            route = jnp.dot(pre_gate_out[...], gate_w[:, cols], preferred_element_type=F32)
            route += jnp.dot(pre_up_out[...], up_w[:, cols], preferred_element_type=F32)
            route = route.astype(BF16)
            kept_out[:, cols] = route[:half_rows]
            given_out[:, cols] = route[half_rows:]

    if packs:
        row = lax.broadcasted_iota(jnp.int32, (total_rows, total_rows), 0)
        other = lax.broadcasted_iota(jnp.int32, (total_rows, total_rows), 1)
        before = (other < row) & (other >= row - row % tok_rows)
        taken_lanes = jnp.broadcast_to(taken, routing.shape).astype(BF16)
        count = jnp.dot(before.astype(BF16), taken_lanes, preferred_element_type=F32)
        part_of = lax.broadcasted_iota(jnp.int32, routing.shape, 0) // tok_rows
        first = jnp.full(routing.shape, LANES, jnp.int32)
        for order, part in enumerate(part for pack in packs for part in pack):
            first = jnp.where(part_of == part, order * slots, first)
        place = jnp.where(taken > 0.0, count.astype(jnp.int32) + first, LANES)
        picks = (place == lane).astype(BF16)

    def fill(values, at):
        rows = lax.dot_general(picks, values, OVER_ROWS, preferred_element_type=F32)
        first = 0
        for out in slots_outs:
            count = out.shape[0]
            out[:, at : at + rows.shape[1]] = rows[first : first + count].astype(BF16)
            first += count

    if packs:
        away = pl.multiple_of((1 - group) * half, half)
        fill(stacked(parts, width, (0, away), half), 0)
        fill(stacked(parts, width, (1, away), half), half)
        for which in range(3):
            fill(grads[which][...], 2 * half + which * hidden_width)

    if adds:
        start = pl.multiple_of(group * half, half)
        blocks = [dense_block(*block, start, half, width) for block in [(parts, grads), *dense]]
        blocks += [slot_block(ref, half, hidden_width) for ref in came]

        def store(which, cols, total):
            sums[which][cols, :] = total

        add_products(blocks, earlier, store, hidden_width)


def flat(parts):
    return [array for part in parts for array in part]


def expert_rows(
    parts, weights, sizes, sums=None, packs=(), waiting=(), came=(), adds=True, routed=True
):
    _, slots, _, half = sizes
    total = sum(part[0].shape[0] for part in parts)
    hidden_width, width = weights[0].shape
    operands = [*flat(parts), *weights]
    for block_parts, block_grads in waiting:
        operands += [*flat(block_parts), *block_grads]
    operands += [*came, *(sums or ())]
    wide = jax.ShapeDtypeStruct((total // 2, width + LANES), BF16)
    grad = jax.ShapeDtypeStruct((total, hidden_width), BF16)
    added = jax.ShapeDtypeStruct((hidden_width, half), F32)
    results = [wide] * (2 * routed)
    for pack in packs:
        shape = (slots * len(pack), 2 * half + 3 * hidden_width)
        results.append(jax.ShapeDtypeStruct(shape, BF16))
    first = len(results)
    results += [added] * 3 if adds else [grad] * 3
    first_sum = len(operands) - 3
    results = pl.pallas_call(
        functools.partial(
            rows_kernel,
            [len(part) for part in parts],
            packs,
            [[len(part) for part in block_parts] for block_parts, _ in waiting],
            len(came),
            sums is not None,
            adds,
            routed,
            sizes,
        ),
        out_shape=results,
        in_specs=[IN_VMEM] * len(operands),
        out_specs=[IN_VMEM] * len(results),
        input_output_aliases={first_sum + i: first + i for i in range(3)} if sums else {},
        scratch_shapes=[pltpu.VMEM(grad.shape, BF16)] * (3 * adds),
        compiler_params=pltpu.CompilerParams(vmem_limit_bytes=KERNEL_VMEM),
        cost_estimate=NO_COST,
    )(*operands)
    return list(results[: 2 * routed]), list(results[2 * routed : first]), list(results[first:])


def sums_kernel(waiting, slot_total, has_last, half, width, *refs):
    refs = list(refs)

    def take(count):
        taken = refs[:count]
        del refs[:count]
        return taken

    dense = [(take_parts(refs, layout), take(3)) for layout in waiting]
    came, earlier, outs = take(slot_total), take(3), take(3)
    hidden_width = earlier[0].shape[0]
    start = pl.multiple_of(lax.axis_index("dp") * half, half)
    blocks = [dense_block(*block, start, half, width) for block in dense]
    blocks += [slot_block(ref, half, hidden_width) for ref in came]
    if not has_last:

        def store(which, cols, total):
            outs[which][cols, :] = total

        add_products(blocks, earlier, store, hidden_width)
        return
    rounded, sent = refs

    def store(which, cols, total):
        rounded[which, cols, :] = total.astype(BF16)
        pltpu.make_async_copy(
            rounded.at[which, cols, :], outs[which].at[cols, :], sent.at[which]
        ).start()

    add_products(blocks, earlier, store, hidden_width)
    for which in range(3):
        pltpu.make_async_copy(rounded.at[which], outs[which], sent.at[which]).wait()


def add_rows(came, sums, width, waiting=(), last=False):
    hidden_width, half = sums[0].shape
    operands = []
    for block_parts, block_grads in waiting:
        operands += [*flat(block_parts), *block_grads]
    operands += [*came, *sums]
    added = jax.ShapeDtypeStruct((hidden_width, half), BF16 if last else F32)
    scratch = [pltpu.VMEM((3, hidden_width, half), BF16), pltpu.SemaphoreType.DMA((3,))]
    first_sum = len(operands) - 3
    return list(
        pl.pallas_call(
            functools.partial(
                sums_kernel,
                [[len(part) for part in block_parts] for block_parts, _ in waiting],
                len(came),
                last,
                half,
                width,
            ),
            out_shape=[added] * 3,
            in_specs=[IN_VMEM] * len(operands),
            out_specs=[pl.BlockSpec(memory_space=pl.ANY) if last else IN_VMEM] * 3,
            input_output_aliases={} if last else {first_sum + i: i for i in range(3)},
            scratch_shapes=scratch if last else [],
            compiler_params=pltpu.CompilerParams(vmem_limit_bytes=KERNEL_VMEM),
            cost_estimate=NO_COST,
        )(*operands)
    )


def pack_kernel(tokens, out_grad, ids, gates, out):
    width = tokens.shape[1]
    top_count = ids.shape[0]
    out[:, :width] = tokens[...]
    out[:, width : 2 * width] = out_grad[...]
    row = lax.broadcasted_iota(jnp.int32, (top_count, LANES), 0)
    lane = lax.broadcasted_iota(jnp.int32, (top_count, LANES), 1)
    routing = 0.0
    for values, at in ((ids[...].astype(F32).astype(BF16), 0), (gates[...], top_count)):
        spread = (lane == row + at).astype(BF16)
        routing += lax.dot_general(values, spread, OVER_ROWS, preferred_element_type=F32)
    out[:, 2 * width :] = routing.astype(BF16)


def packed_rows(tokens, out_grad, expert_ids, gates):
    rows, width = tokens.shape
    return pl.pallas_call(
        pack_kernel,
        out_shape=jax.ShapeDtypeStruct((rows, 2 * width + LANES), BF16),
        in_specs=[IN_VMEM] * 4,
        out_specs=IN_VMEM,
        compiler_params=pltpu.CompilerParams(vmem_limit_bytes=KERNEL_VMEM),
        cost_estimate=NO_COST,
    )(tokens, out_grad, expert_ids.T, gates.T)


def finish_kernel(experts, kept, given, fore, rear, ids, token_out, gate_out):
    rows, width = token_out.shape
    total = kept[...].astype(F32) + given[...].astype(F32) + fore[...].astype(F32)
    total += rear[...].astype(F32)
    token_out[...] = total[:, :width].astype(BF16)
    table = jnp.transpose(total[:, width:])
    chosen = ids[...]
    grad = jnp.zeros(chosen.shape, F32)
    for expert in range(experts):
        grad += jnp.where(chosen == expert, table[expert : expert + 1, :rows], 0.0)
    gate_out[...] = grad.astype(BF16)


def finished(experts, kept, given, fore, rear, expert_ids):
    rows, top_count = expert_ids.shape
    width = kept.shape[1] - LANES
    token_grad, gate_grad = pl.pallas_call(
        functools.partial(finish_kernel, experts),
        out_shape=[
            jax.ShapeDtypeStruct((rows, width), BF16),
            jax.ShapeDtypeStruct((top_count, rows), BF16),
        ],
        in_specs=[IN_VMEM] * 5,
        out_specs=[IN_VMEM] * 2,
        compiler_params=pltpu.CompilerParams(vmem_limit_bytes=KERNEL_VMEM),
        cost_estimate=NO_COST,
    )(kept, given, fore, rear, expert_ids.T)
    return token_grad, gate_grad.T


def chip_ring(expert_count):
    depth = expert_count // 4
    return [2 * z for z in range(depth)] + [2 * z + 1 for z in reversed(range(depth))]


def ring_shift(expert_count, by):
    order = chip_ring(expert_count)
    total = len(order)
    return sorted(
        (2 * chip + core, 2 * order[(place + by) % total] + core)
        for place, chip in enumerate(order)
        for core in range(2)
    )


def on_ring(tokens, out_grad, expert_ids, gates, w_gate, w_up, w_down):
    rows, width = tokens.shape
    top_count = expert_ids.shape[1]
    experts = lax.axis_size("expert")
    half = width // lax.axis_size("dp")
    capacity = min(rows, rows * top_count * 6 // (5 * experts))
    sizes = (rows, capacity, top_count, half)
    forth, back = ring_shift(experts, 1), ring_shift(experts, -1)
    weights = (w_gate[0].T, w_up[0].T, w_down[0])
    stage = lax.optimization_barrier

    def go(value, pairs):
        return lax.ppermute(value, "expert", pairs)

    def sibling(value):
        return lax.ppermute(value, "expert", [(i, i ^ 1) for i in range(experts)])

    def across(value):
        return lax.ppermute(value, "dp", [(0, 1), (1, 0)])

    def with_siblings(parts):
        return parts + [tuple(sibling(array) for array in part) for part in parts]

    def expert(parts, sums=None, packs=(), **options):
        return expert_rows(parts, weights, sizes, sums, packs, **options)

    def passed_on(item, fore, rear):
        total = item[0].astype(F32) + item[1].astype(F32)
        fore = go((total[rows:] + fore.astype(F32)).astype(BF16), forth)
        rear = go((total[:rows] + rear.astype(F32)).astype(BF16), back)
        return fore, rear

    own = packed_rows(tokens, out_grad, expert_ids, gates)
    fore, rear, over0 = go(own, forth), go(own, back), across(own)
    parts0 = with_siblings([(own,)])
    near0, _, grads0 = expert(parts0, adds=False)
    fore, rear, over0, near0, block0 = stage((fore, rear, over0, near0, (parts0, grads0)))

    parts = with_siblings([(fore,), (rear,)])
    over1 = across(fore)
    fore, rear = go(fore, forth), go(rear, back)
    near1, slots1, sums = expert(parts, packs=[(1, 3)], waiting=[block0])
    fore, rear, over1, near1, slots1, sums = stage((fore, rear, over1, near1, slots1, sums))

    parts = with_siblings([(fore,), (rear,)])
    fore, rear, came1 = go(fore, forth), go(rear, back), across(slots1[0])
    near2, slots2, sums = expert(parts, sums, [(0, 1, 2, 3)])
    fore, rear, came1, near2, slots2, sums = stage((fore, rear, came1, near2, slots2, sums))

    parts3 = with_siblings([(fore,), (rear,)])
    far_x, far_rest = go(fore[:, :width], forth), go(rear[:, width:], back)
    came2 = across(slots2[0])
    near3, slots3, grads3 = expert(parts3, packs=[(0, 1, 2, 3)], adds=False)
    far_x, far_rest, near3, slots3, block3 = stage((far_x, far_rest, near3, slots3, (parts3, grads3)))

    parts4 = with_siblings([(far_x, far_rest)])
    near3[1], near2[1] = sibling(near3[1]), sibling(near2[1])
    near4, slots4, grads4 = expert(parts4, packs=[(0, 1)], adds=False)
    near2, near3, near4, slots4, block4, came2 = stage(
        (near2, near3, near4, slots4, (parts4, grads4), came2)
    )
    came3 = across(slots3[0])
    near4[1] = sibling(near4[1])
    sum4 = (near4[0].astype(F32) + near4[1].astype(F32)).astype(BF16)
    cut = width // 2
    fore, rear = go(sum4[:, :cut], forth), go(sum4[:, cut:], back)
    sums = add_rows([came1, came2], sums, width, [block3, block4])
    fore, rear, sums = stage((fore, rear, sums))
    fore = jnp.pad(fore, ((0, 0), (0, width + LANES - cut)))
    rear = jnp.pad(rear, ((0, 0), (cut, 0)))

    fore, rear = passed_on(near3, fore, rear)
    over = with_siblings([(over0,), (over1,)])
    fore, rear, over, came3 = stage((fore, rear, over, came3))

    fore, rear = passed_on(near2, fore, rear)
    near1[1], near0[1] = sibling(near1[1]), sibling(near0[1])
    sums = expert(over, sums, came=[came3], routed=False)[2]
    fore, rear, near1, near0, sums = stage((fore, rear, near1, near0, sums))

    came4 = across(slots4[0])
    fore, rear = passed_on(near1, fore, rear)
    fore, rear, came4 = stage((fore, rear, came4))

    token_grad, gate_grad = finished(experts, *near0, fore, rear, expert_ids)
    sums = add_rows([came4], sums, width, last=True)
    return (token_grad, gate_grad, sums[0].T[None], sums[1].T[None], sums[2][None])


def solution(mesh):
    in_specs = (
        P(("dp", "expert"), None),
        P(("dp", "expert"), None),
        P(("dp", "expert"), None),
        P(("dp", "expert"), None),
        P("expert", None, None),
        P("expert", None, None),
        P("expert", None, None),
    )
    out_specs = (
        P(("dp", "expert"), None),
        P(("dp", "expert"), None),
        P("expert", "dp", None),
        P("expert", "dp", None),
        P("expert", None, "dp"),
    )
    on_slice = on_ring if (mesh.shape["dp"], mesh.shape["expert"]) == (2, 16) else on_device
    return jax.shard_map(
        on_slice, mesh=mesh, in_specs=in_specs, out_specs=out_specs, check_vma=False
    )
```

```python
import functools

import jax
import jax.numpy as jnp
from jax import lax
from jax.experimental import pallas as pl
from jax.experimental.pallas import tpu as pltpu
from jax.sharding import PartitionSpec as P


def slot_places(expert_ids, experts, capacity):
    flat_ids = expert_ids.reshape(-1)
    labels = jnp.arange(experts, dtype=jnp.int32)
    onehot = (flat_ids[:, None] == labels[None, :]).astype(jnp.int32)
    earlier = jnp.cumsum(onehot, axis=0) - onehot
    slot_index = jnp.sum(earlier * onehot, axis=1)
    return flat_ids * capacity + slot_index


def slot_sources(places, slot_total):
    route_total = places.shape[0]
    filler = (
        jnp.zeros((slot_total,), jnp.int32)
        .at[places]
        .set(jnp.arange(route_total, dtype=jnp.int32) + 1)
    )
    return (jnp.maximum(filler - 1, 0), filler > 0)


def fill_slots(values, source, filled):
    taken = values[source]
    keep_mask = filled.reshape(filled.shape + (1,) * (taken.ndim - 1))
    return jnp.where(keep_mask, taken, jnp.zeros_like(taken))


def expert_pass(x_rows, dy_rows, g_rows, gate_w, up_w, down_w):
    pre_gate = jnp.dot(x_rows, gate_w, preferred_element_type=jnp.float32)
    pre_up = jnp.dot(x_rows, up_w, preferred_element_type=jnp.float32)
    sigmoid_gate = jax.nn.sigmoid(pre_gate)
    activated = pre_gate * sigmoid_gate
    hidden = (activated * pre_up).astype(jnp.bfloat16)
    expert_out = jnp.dot(hidden, down_w, preferred_element_type=jnp.float32)
    gate_grad = jnp.sum(dy_rows.astype(jnp.float32) * expert_out, axis=-1).astype(jnp.bfloat16)
    scaled = (g_rows.astype(jnp.float32)[:, None] * dy_rows.astype(jnp.float32)).astype(
        jnp.bfloat16
    )
    hidden_grad = lax.dot_general(
        scaled, down_w, (((1,), (1,)), ((), ())), preferred_element_type=jnp.float32
    )
    pre_gate_grad = (
        hidden_grad * pre_up * sigmoid_gate * (1.0 + pre_gate * (1.0 - sigmoid_gate))
    ).astype(jnp.bfloat16)
    pre_up_grad = (hidden_grad * activated).astype(jnp.bfloat16)
    route_grad = lax.dot_general(
        pre_gate_grad, gate_w, (((1,), (1,)), ((), ())), preferred_element_type=jnp.float32
    )
    route_grad = route_grad + lax.dot_general(
        pre_up_grad, up_w, (((1,), (1,)), ((), ())), preferred_element_type=jnp.float32
    )
    return (route_grad.astype(jnp.bfloat16), gate_grad, pre_gate_grad, pre_up_grad, hidden, scaled)


def on_device(tokens, out_grad, expert_ids, gates, w_gate, w_up, w_down):
    tok_rows, model_width = tokens.shape
    top_count = expert_ids.shape[1]
    peer_count = lax.axis_size("expert")
    capacity = min(tok_rows, tok_rows * top_count * 6 // (5 * peer_count))
    slot_total = peer_count * capacity
    places = slot_places(expert_ids, peer_count, capacity)
    source, filled = slot_sources(places, slot_total)
    token_source = source // top_count
    x_buf = fill_slots(tokens, token_source, filled).reshape(peer_count, capacity, model_width)
    dy_buf = fill_slots(out_grad, token_source, filled).reshape(peer_count, capacity, model_width)
    g_buf = fill_slots(gates.reshape(-1), source, filled).reshape(peer_count, capacity)
    gate_w = w_gate[0]
    up_w = w_up[0]
    down_w = w_down[0]
    hidden_width = gate_w.shape[1]
    x_in, dy_in, g_in = (
        lax.all_to_all(x_buf, "expert", split_axis=0, concat_axis=0, tiled=True),
        lax.all_to_all(dy_buf, "expert", split_axis=0, concat_axis=0, tiled=True),
        lax.all_to_all(g_buf, "expert", split_axis=0, concat_axis=0, tiled=True),
    )
    lead_dim = x_in.shape[0]
    item_total = x_in.shape[1]
    results = expert_pass(
        x_in.reshape(lead_dim * item_total, model_width),
        dy_in.reshape(lead_dim * item_total, model_width),
        g_in.reshape(lead_dim * item_total),
        gate_w,
        up_w,
        down_w,
    )
    route_grad, gate_grad, pre_gate_grad, pre_up_grad, hidden, scaled = tuple(
        (piece.reshape((lead_dim, item_total) + piece.shape[1:]) for piece in results)
    )
    back_dx, back_dg = (
        lax.all_to_all(route_grad, "expert", split_axis=0, concat_axis=0, tiled=True),
        lax.all_to_all(gate_grad, "expert", split_axis=0, concat_axis=0, tiled=True),
    )
    routed = back_dx.reshape(slot_total, model_width)[places]
    token_grad = jnp.sum(
        routed.reshape(tok_rows, top_count, model_width).astype(jnp.float32), axis=1
    ).astype(jnp.bfloat16)
    gate_grad_out = back_dg.reshape(slot_total)[places].reshape(tok_rows, top_count)
    x_rows = x_in.reshape(slot_total, model_width)
    scaled_rows = scaled.reshape(slot_total, model_width)
    gate_rows = pre_gate_grad.reshape(slot_total, hidden_width)
    up_rows = pre_up_grad.reshape(slot_total, hidden_width)
    hidden_rows = hidden.reshape(slot_total, hidden_width)
    contract = (((0,), (0,)), ((), ()))
    part_gate = lax.dot_general(x_rows, gate_rows, contract, preferred_element_type=jnp.float32)
    part_up = lax.dot_general(x_rows, up_rows, contract, preferred_element_type=jnp.float32)
    part_down = lax.dot_general(
        hidden_rows, scaled_rows, contract, preferred_element_type=jnp.float32
    )
    sum_gate, sum_up, sum_down = (
        lax.psum_scatter(
            part_gate.astype(jnp.bfloat16), "dp", scatter_dimension=0, tiled=True
        ).astype(jnp.float32),
        lax.psum_scatter(
            part_up.astype(jnp.bfloat16), "dp", scatter_dimension=0, tiled=True
        ).astype(jnp.float32),
        lax.psum_scatter(
            part_down.astype(jnp.bfloat16), "dp", scatter_dimension=1, tiled=True
        ).astype(jnp.float32),
    )
    return (
        token_grad,
        gate_grad_out,
        sum_gate.astype(jnp.bfloat16)[None],
        sum_up.astype(jnp.bfloat16)[None],
        sum_down.astype(jnp.bfloat16)[None],
    )


F32, BF16 = jnp.float32, jnp.bfloat16
ROWS_BY_ROWS = (((1,), (1,)), ((), ()))
OVER_ROWS = (((0,), (0,)), ((), ()))
LANES = 128
KERNEL_VMEM = 16 * 2**20
ALL_VMEM = 60 * 2**20
IN_VMEM = pl.BlockSpec(memory_space=pltpu.VMEM)
WHEREVER = pl.BlockSpec(memory_space=pl.ANY)
NO_COST = pl.CostEstimate(flops=0, bytes_accessed=0, transcendentals=0)


def tiles(total, step):
    return [slice(at, min(at + step, total)) for at in range(0, total, step)]


def used_rows(part):
    return part[0].shape[0] - part[0].shape[0] % 16


def take_parts(refs, layout):
    return [tuple(refs.pop(0) for _ in range(count)) for count in layout]


def stacked(parts, width, start, size):
    in_rest, at = start

    def read(part):
        rows = slice(0, used_rows(part))
        if len(part) == 2:
            return part[in_rest][rows, pl.ds(at, size)]
        return part[0][rows, pl.ds(at + width if in_rest else at, size)]

    return jnp.concatenate([read(part) for part in parts], axis=0)


def add_products(blocks, earlier, store, hidden_width):
    for which in range(3):
        for cols in tiles(hidden_width, 256):
            total = earlier[which][cols, :] if earlier else 0.0
            for block in blocks:
                left, right = block(which, cols)
                total += lax.dot_general(left, right, OVER_ROWS, preferred_element_type=F32)
            store(which, cols, total)


def dense_block(parts, grads, start, half, width):
    def block(which, cols):
        return grads[which][:, cols], stacked(parts, width, (which == 2, start), half)

    return block


def slot_block(ref, half, hidden_width):
    def block(which, cols):
        at = 2 * half + which * hidden_width
        first = half if which == 2 else 0
        return ref[:, at + cols.start : at + cols.stop], ref[:, first : first + half]

    return block


def choices(routing, top_count):
    lane = lax.broadcasted_iota(jnp.int32, routing.shape, 1)
    chosen = (routing == lax.axis_index("expert").astype(F32)) & (lane < top_count)
    shifted = pltpu.roll(routing, LANES - top_count, 1)
    gate = jnp.sum(jnp.where(chosen, shifted, 0.0), axis=1, keepdims=True)
    taken = jnp.sum(jnp.where(chosen, 1.0, 0.0), axis=1, keepdims=True)
    return gate, taken


def write_slots(outs, packs, carried, parts, grads, taken, sizes, width):
    tok_rows, slots, _, half = sizes
    total_rows, hidden_width = grads[0].shape
    shape = (total_rows, LANES)
    row = lax.broadcasted_iota(jnp.int32, (total_rows, total_rows), 0)
    other = lax.broadcasted_iota(jnp.int32, (total_rows, total_rows), 1)
    before = (other < row) & (other >= row - row % tok_rows)
    taken_lanes = jnp.broadcast_to(taken, shape).astype(BF16)
    count = jnp.dot(before.astype(BF16), taken_lanes, preferred_element_type=F32)
    part_of = lax.broadcasted_iota(jnp.int32, shape, 0) // tok_rows
    first = jnp.full(shape, LANES, jnp.int32)
    for order, part in enumerate(part for pack in packs for part in pack):
        first = jnp.where(part_of == part, order * slots, first)
    place = jnp.where(taken > 0.0, count.astype(jnp.int32) + first, LANES)
    picks = (place == lax.broadcasted_iota(jnp.int32, shape, 1)).astype(BF16)
    away = pl.multiple_of((1 - lax.axis_index("dp")) * half, half)

    def fill(values, at):
        rows = lax.dot_general(picks, values, OVER_ROWS, preferred_element_type=F32)
        columns = slice(at, at + rows.shape[1])
        first = 0
        for order, (out, pack) in enumerate(zip(outs, packs)):
            count = len(pack) * slots
            block = rows[first : first + count]
            if order == 0 and carried is not None:
                block = jnp.concatenate([carried[:, columns].astype(F32), block], axis=0)
            out[:, columns] = block.astype(BF16)
            first += count

    fill(stacked(parts, width, (0, away), half), 0)
    fill(stacked(parts, width, (1, away), half), half)
    for which in range(3):
        fill(grads[which][...], 2 * half + which * hidden_width)


def slots_kernel(layout, packs, has_carried, sizes, width, *refs):
    refs = list(refs)
    parts = take_parts(refs, layout)
    grads, refs = refs[:3], refs[3:]
    carried = refs.pop(0) if has_carried else None
    routing = stacked(parts, width, (1, width), LANES).astype(F32)
    _, taken = choices(routing, sizes[2])
    write_slots(refs, packs, carried, parts, grads, taken, sizes, width)


def slot_rows(parts, grads, sizes, width, packs, carried=None):
    _, slots, _, half = sizes
    operands = [*flat(parts), *grads] + ([carried] if carried is not None else [])
    shapes = []
    for order, pack in enumerate(packs):
        count = slots * len(pack)
        if order == 0 and carried is not None:
            count += carried.shape[0]
        shapes.append((count, 2 * half + 3 * grads[0].shape[1]))
    return list(
        pl.pallas_call(
            functools.partial(
                slots_kernel,
                [len(part) for part in parts],
                packs,
                carried is not None,
                sizes,
                width,
            ),
            out_shape=[jax.ShapeDtypeStruct(shape, BF16) for shape in shapes],
            in_specs=[IN_VMEM] * len(operands),
            out_specs=[IN_VMEM] * len(shapes),
            compiler_params=pltpu.CompilerParams(vmem_limit_bytes=KERNEL_VMEM),
            cost_estimate=NO_COST,
        )(*operands)
    )


def rows_kernel(layout, packs, waiting, slot_total, after, has_sums, adds, routed, sizes, *refs):
    refs = list(refs)
    _, _, top_count, half = sizes

    def take(count):
        taken = refs[:count]
        del refs[:count]
        return taken

    parts, (gate_w, up_w, down_w) = take_parts(refs, layout), take(3)
    dense = [(take_parts(refs, parts_layout), take(3)) for parts_layout in waiting]
    came = take(slot_total)
    take(after)
    earlier = take(3) if has_sums else None
    kept_out, given_out = take(2) if routed else (None, None)
    slots_outs = take(len(packs))
    sums = take(3) if adds else None
    grads = take(3)
    pre_gate_out, pre_up_out, hidden_out = grads
    hidden_width, width = gate_w.shape
    x = stacked(parts, width, (0, 0), width)
    dy = stacked(parts, width, (1, 0), width)
    routing = stacked(parts, width, (1, width), LANES).astype(F32)
    gate, taken = choices(routing, top_count)
    gate_grad = jnp.zeros_like(gate)
    for cols in tiles(hidden_width, 256):
        pre_gate = lax.dot_general(x, gate_w[cols, :], ROWS_BY_ROWS, preferred_element_type=F32)
        pre_up = lax.dot_general(x, up_w[cols, :], ROWS_BY_ROWS, preferred_element_type=F32)
        down_grad = lax.dot_general(dy, down_w[cols, :], ROWS_BY_ROWS, preferred_element_type=F32)
        sigmoid_gate = jax.nn.sigmoid(pre_gate)
        activated = pre_gate * sigmoid_gate
        hidden = activated * pre_up
        gate_grad += jnp.sum(hidden * down_grad, axis=1, keepdims=True)
        hidden_grad = gate * down_grad
        slope = sigmoid_gate * (1.0 + pre_gate * (1.0 - sigmoid_gate))
        pre_gate_out[:, cols] = (hidden_grad * pre_up * slope).astype(BF16)
        pre_up_out[:, cols] = (hidden_grad * activated).astype(BF16)
        hidden_out[:, cols] = (gate * hidden).astype(BF16)
    if routed:
        half_rows = routing.shape[0] // 2
        lane = lax.broadcasted_iota(jnp.int32, routing.shape, 1)
        table = jnp.where(lane == lax.axis_index("expert"), gate_grad * taken, 0.0).astype(BF16)
        kept_out[:, width:] = table[:half_rows]
        given_out[:, width:] = table[half_rows:]
        for cols in tiles(width, 512):
            route = jnp.dot(pre_gate_out[...], gate_w[:, cols], preferred_element_type=F32)
            route += jnp.dot(pre_up_out[...], up_w[:, cols], preferred_element_type=F32)
            route = route.astype(BF16)
            kept_out[:, cols] = route[:half_rows]
            given_out[:, cols] = route[half_rows:]

    if packs:
        write_slots(slots_outs, packs, None, parts, grads, taken, sizes, width)
    if adds:
        start = pl.multiple_of(lax.axis_index("dp") * half, half)
        blocks = [dense_block(*block, start, half, width) for block in [(parts, grads), *dense]]
        blocks += [slot_block(ref, half, hidden_width) for ref in came]

        def store(which, cols, total):
            sums[which][cols, :] = total

        add_products(blocks, earlier, store, hidden_width)


def flat(parts):
    return [array for part in parts for array in part]


def expert_rows(
    parts, weights, sizes, sums=None, packs=(), waiting=(), came=(), after=(), adds=True, routed=True
):
    _, slots, _, half = sizes
    total = sum(used_rows(part) for part in parts)
    hidden_width, width = weights[0].shape
    operands = [*flat(parts), *weights]
    for block_parts, block_grads in waiting:
        operands += [*flat(block_parts), *block_grads]
    operands += [*came, *after, *(sums or ())]
    wide = jax.ShapeDtypeStruct((total // 2, width + LANES), BF16)
    grad = jax.ShapeDtypeStruct((total, hidden_width), BF16)
    added = jax.ShapeDtypeStruct((hidden_width, half), F32)
    results = [wide] * (2 * routed)
    for pack in packs:
        shape = (slots * len(pack), 2 * half + 3 * hidden_width)
        results.append(jax.ShapeDtypeStruct(shape, BF16))
    first = len(results)
    results += [added] * 3 if adds else [grad] * 3
    first_sum = len(operands) - 3
    results = pl.pallas_call(
        functools.partial(
            rows_kernel,
            [len(part) for part in parts],
            packs,
            [[len(part) for part in block_parts] for block_parts, _ in waiting],
            len(came),
            len(after),
            sums is not None,
            adds,
            routed,
            sizes,
        ),
        out_shape=results,
        in_specs=[WHEREVER if any(o is a for a in after) else IN_VMEM for o in operands],
        out_specs=[IN_VMEM] * len(results),
        input_output_aliases={first_sum + i: first + i for i in range(3)} if sums else {},
        scratch_shapes=[pltpu.VMEM(grad.shape, BF16)] * (3 * adds),
        compiler_params=pltpu.CompilerParams(vmem_limit_bytes=KERNEL_VMEM),
        cost_estimate=NO_COST,
    )(*operands)
    return list(results[: 2 * routed]), list(results[2 * routed : first]), list(results[first:])


def sums_kernel(waiting, slot_total, has_last, half, width, *refs):
    refs = list(refs)

    def take(count):
        taken = refs[:count]
        del refs[:count]
        return taken

    dense = [(take_parts(refs, layout), take(3)) for layout in waiting]
    came, earlier, outs = take(slot_total), take(3), take(3)
    hidden_width = earlier[0].shape[0]
    start = pl.multiple_of(lax.axis_index("dp") * half, half)
    blocks = [dense_block(*block, start, half, width) for block in dense]
    blocks += [slot_block(ref, half, hidden_width) for ref in came]
    if not has_last:

        def store(which, cols, total):
            outs[which][cols, :] = total

        add_products(blocks, earlier, store, hidden_width)
        return
    rounded, sent = refs

    def store(which, cols, total):
        rounded[which, cols, :] = total.astype(BF16)
        pltpu.make_async_copy(
            rounded.at[which, cols, :], outs[which].at[cols, :], sent.at[which]
        ).start()

    add_products(blocks, earlier, store, hidden_width)
    for which in range(3):
        pltpu.make_async_copy(rounded.at[which], outs[which], sent.at[which]).wait()


def add_rows(came, sums, width, waiting=(), last=False):
    hidden_width, half = sums[0].shape
    operands = []
    for block_parts, block_grads in waiting:
        operands += [*flat(block_parts), *block_grads]
    operands += [*came, *sums]
    added = jax.ShapeDtypeStruct((hidden_width, half), BF16 if last else F32)
    scratch = [pltpu.VMEM((3, hidden_width, half), BF16), pltpu.SemaphoreType.DMA((3,))]
    first_sum = len(operands) - 3
    return list(
        pl.pallas_call(
            functools.partial(
                sums_kernel,
                [[len(part) for part in block_parts] for block_parts, _ in waiting],
                len(came),
                last,
                half,
                width,
            ),
            out_shape=[added] * 3,
            in_specs=[IN_VMEM] * len(operands),
            out_specs=[WHEREVER if last else IN_VMEM] * 3,
            input_output_aliases={} if last else {first_sum + i: i for i in range(3)},
            scratch_shapes=scratch if last else [],
            compiler_params=pltpu.CompilerParams(vmem_limit_bytes=KERNEL_VMEM),
            cost_estimate=NO_COST,
        )(*operands)
    )


def pack_kernel(tokens, out_grad, ids, gates, out, ids_held, gates_held, sent):
    width = tokens.shape[1]
    top_count = ids.shape[0]
    copies = [
        pltpu.make_async_copy(ids, ids_held, sent.at[0]),
        pltpu.make_async_copy(gates, gates_held, sent.at[1]),
        pltpu.make_async_copy(tokens, out.at[:, pl.ds(0, width)], sent.at[2]),
        pltpu.make_async_copy(out_grad, out.at[:, pl.ds(width, width)], sent.at[3]),
    ]
    for copy in copies:
        copy.start()
    row = lax.broadcasted_iota(jnp.int32, (top_count, LANES), 0)
    lane = lax.broadcasted_iota(jnp.int32, (top_count, LANES), 1)
    routing = 0.0
    for held, copy, at in ((ids_held, copies[0], 0), (gates_held, copies[1], top_count)):
        copy.wait()
        values = held[...].astype(F32).astype(BF16)
        spread = (lane == row + at).astype(BF16)
        routing += lax.dot_general(values, spread, OVER_ROWS, preferred_element_type=F32)
    out[:, 2 * width :] = routing.astype(BF16)
    copies[2].wait()
    copies[3].wait()


def packed_rows(tokens, out_grad, expert_ids, gates):
    rows, width = tokens.shape
    top_count = expert_ids.shape[1]
    return pl.pallas_call(
        pack_kernel,
        out_shape=jax.ShapeDtypeStruct((rows, 2 * width + LANES), BF16),
        in_specs=[WHEREVER] * 4,
        out_specs=IN_VMEM,
        scratch_shapes=[
            pltpu.VMEM((top_count, rows), jnp.int32),
            pltpu.VMEM((top_count, rows), BF16),
            pltpu.SemaphoreType.DMA((4,)),
        ],
        compiler_params=pltpu.CompilerParams(vmem_limit_bytes=ALL_VMEM),
        cost_estimate=NO_COST,
    )(tokens, out_grad, expert_ids.T, gates.T)


def finish_kernel(experts, kept, given, fore, rear, ids, token_out, gate_out):
    rows, width = token_out.shape
    total = kept[...].astype(F32) + given[...].astype(F32) + fore[...].astype(F32)
    total += rear[...].astype(F32)
    token_out[...] = total[:, :width].astype(BF16)
    table = jnp.transpose(total[:, width:])
    chosen = ids[...]
    grad = jnp.zeros(chosen.shape, F32)
    for expert in range(experts):
        grad += jnp.where(chosen == expert, table[expert : expert + 1, :rows], 0.0)
    gate_out[...] = grad.astype(BF16)


def finished(experts, kept, given, fore, rear, expert_ids):
    rows, top_count = expert_ids.shape
    width = kept.shape[1] - LANES
    token_grad, gate_grad = pl.pallas_call(
        functools.partial(finish_kernel, experts),
        out_shape=[
            jax.ShapeDtypeStruct((rows, width), BF16),
            jax.ShapeDtypeStruct((top_count, rows), BF16),
        ],
        in_specs=[IN_VMEM] * 5,
        out_specs=[IN_VMEM] * 2,
        compiler_params=pltpu.CompilerParams(vmem_limit_bytes=KERNEL_VMEM),
        cost_estimate=NO_COST,
    )(kept, given, fore, rear, expert_ids.T)
    return token_grad, gate_grad.T


def chip_ring(expert_count):
    depth = expert_count // 4
    return [2 * z for z in range(depth)] + [2 * z + 1 for z in reversed(range(depth))]


def ring_shift(expert_count, by):
    order = chip_ring(expert_count)
    total = len(order)
    return sorted(
        (2 * chip + core, 2 * order[(place + by) % total] + core)
        for place, chip in enumerate(order)
        for core in range(2)
    )


def on_ring(tokens, out_grad, expert_ids, gates, w_gate, w_up, w_down):
    rows, width = tokens.shape
    top_count = expert_ids.shape[1]
    experts = lax.axis_size("expert")
    half = width // lax.axis_size("dp")
    capacity = min(rows, rows * top_count * 6 // (5 * experts))
    sizes = (rows, capacity, top_count, half)
    forth, back = ring_shift(experts, 1), ring_shift(experts, -1)
    weights = (w_gate[0].T, w_up[0].T, w_down[0])
    stage = lax.optimization_barrier

    def go(value, pairs):
        return lax.ppermute(value, "expert", pairs)

    def sibling(value):
        return lax.ppermute(value, "expert", [(i, i ^ 1) for i in range(experts)])

    def across(value):
        return lax.ppermute(value, "dp", [(0, 1), (1, 0)])

    def with_siblings(parts):
        return parts + [tuple(sibling(array) for array in part) for part in parts]

    def expert(parts, sums=None, packs=(), **options):
        return expert_rows(parts, weights, sizes, sums, packs, **options)

    def passed_on(item, fore, rear):
        total = item[0].astype(F32) + item[1].astype(F32)
        fore = go((total[rows:] + fore.astype(F32)).astype(BF16), forth)
        rear = go((total[:rows] + rear.astype(F32)).astype(BF16), back)
        return fore, rear

    own = packed_rows(tokens, out_grad, expert_ids, gates)
    fore, rear, over0 = go(own, forth), go(own, back), across(own)
    parts0 = with_siblings([(own,)])
    near0, _, grads0 = expert(parts0, adds=False)
    fore, rear, over0, near0, block0 = stage((fore, rear, over0, near0, (parts0, grads0)))

    parts = with_siblings([(fore,), (rear,)])
    over1 = across(jnp.concatenate([fore, rear], axis=0))
    fore, rear = go(fore, forth), go(rear, back)
    near1, _, sums = expert(parts, waiting=[block0])
    fore, rear, near1, sums = stage((fore, rear, near1, sums))

    parts = with_siblings([(fore,), (rear,)])
    over2 = across(jnp.pad(fore, ((0, 8), (0, 0))))
    fore, rear = go(fore, forth), go(rear, back)
    near2, slots2, sums = expert(parts, sums, [(1, 3)])
    fore, rear, over1, near2, slots2, sums = stage((fore, rear, over1, near2, slots2, sums))

    parts3 = with_siblings([(fore,), (rear,)])
    far_x, far_rest = go(fore[:, :width], forth), go(rear[:, width:], back)
    came2 = across(slots2[0])
    near3, _, grads3 = expert(parts3, adds=False)
    far_x, far_rest, over2, near3, block3 = stage(
        (far_x, far_rest, over2, near3, (parts3, grads3))
    )

    parts4 = with_siblings([(far_x, far_rest)])
    near3[1], near2[1] = sibling(near3[1]), sibling(near2[1])
    slots3 = slot_rows(*block3, sizes, width, [(0, 1, 2), (3,)])
    near4, _, grads4 = expert(parts4, after=slots3, adds=False)
    near2, near3, near4, slots3, block4, came2 = stage(
        (near2, near3, near4, slots3, (parts4, grads4), came2)
    )
    came3 = across(slots3[0])
    near4[1] = sibling(near4[1])
    sum4 = (near4[0].astype(F32) + near4[1].astype(F32)).astype(BF16)
    cut = width // 2
    fore, rear = go(sum4[:, :cut], forth), go(sum4[:, cut:], back)
    near1[1] = sibling(near1[1])
    fore, rear, near1 = stage((fore, rear, near1))
    fore = jnp.pad(fore, ((0, 0), (0, width + LANES - cut)))
    rear = jnp.pad(rear, ((0, 0), (cut, 0)))

    fore, rear = passed_on(near3, fore, rear)
    over = with_siblings([(over0,), (over2,)])
    sums = add_rows([came2], sums, width, [block3, block4])
    slots4 = slot_rows(*block4, sizes, width, [(0, 1)], slots3[1])
    fore, rear, over, came3, sums, slots4 = stage((fore, rear, over, came3, sums, slots4))

    came4 = across(slots4[0])
    fore, rear = passed_on(near2, fore, rear)
    near0[1] = sibling(near0[1])
    over1 = with_siblings([(over1,)])
    sums = expert(over, sums, came=[came3], routed=False)[2]
    fore, rear, near0, over1, sums = stage((fore, rear, near0, over1, sums))

    fore, rear = passed_on(near1, fore, rear)
    sums = expert(over1, sums, routed=False)[2]
    fore, rear, came4, sums = stage((fore, rear, came4, sums))

    token_grad, gate_grad = finished(experts, *near0, fore, rear, expert_ids)
    sums = add_rows([came4], sums, width, last=True)
    return (token_grad, gate_grad, sums[0].T[None], sums[1].T[None], sums[2][None])


def solution(mesh):
    in_specs = (
        P(("dp", "expert"), None),
        P(("dp", "expert"), None),
        P(("dp", "expert"), None),
        P(("dp", "expert"), None),
        P("expert", None, None),
        P("expert", None, None),
        P("expert", None, None),
    )
    out_specs = (
        P(("dp", "expert"), None),
        P(("dp", "expert"), None),
        P("expert", "dp", None),
        P("expert", "dp", None),
        P("expert", None, "dp"),
    )
    on_slice = on_ring if (mesh.shape["dp"], mesh.shape["expert"]) == (2, 16) else on_device
    return jax.shard_map(
        on_slice, mesh=mesh, in_specs=in_specs, out_specs=out_specs, check_vma=False
    )
```

```python
import functools

import jax
import jax.numpy as jnp
from jax import lax
from jax.experimental import pallas as pl
from jax.experimental.pallas import tpu as pltpu
from jax.sharding import PartitionSpec as P


def slot_places(expert_ids, experts, capacity):
    flat_ids = expert_ids.reshape(-1)
    labels = jnp.arange(experts, dtype=jnp.int32)
    onehot = (flat_ids[:, None] == labels[None, :]).astype(jnp.int32)
    earlier = jnp.cumsum(onehot, axis=0) - onehot
    slot_index = jnp.sum(earlier * onehot, axis=1)
    return flat_ids * capacity + slot_index


def slot_sources(places, slot_total):
    route_total = places.shape[0]
    filler = (
        jnp.zeros((slot_total,), jnp.int32)
        .at[places]
        .set(jnp.arange(route_total, dtype=jnp.int32) + 1)
    )
    return (jnp.maximum(filler - 1, 0), filler > 0)


def fill_slots(values, source, filled):
    taken = values[source]
    keep_mask = filled.reshape(filled.shape + (1,) * (taken.ndim - 1))
    return jnp.where(keep_mask, taken, jnp.zeros_like(taken))


def expert_pass(x_rows, dy_rows, g_rows, gate_w, up_w, down_w):
    pre_gate = jnp.dot(x_rows, gate_w, preferred_element_type=jnp.float32)
    pre_up = jnp.dot(x_rows, up_w, preferred_element_type=jnp.float32)
    sigmoid_gate = jax.nn.sigmoid(pre_gate)
    activated = pre_gate * sigmoid_gate
    hidden = (activated * pre_up).astype(jnp.bfloat16)
    expert_out = jnp.dot(hidden, down_w, preferred_element_type=jnp.float32)
    gate_grad = jnp.sum(dy_rows.astype(jnp.float32) * expert_out, axis=-1).astype(jnp.bfloat16)
    scaled = (g_rows.astype(jnp.float32)[:, None] * dy_rows.astype(jnp.float32)).astype(
        jnp.bfloat16
    )
    hidden_grad = lax.dot_general(
        scaled, down_w, (((1,), (1,)), ((), ())), preferred_element_type=jnp.float32
    )
    pre_gate_grad = (
        hidden_grad * pre_up * sigmoid_gate * (1.0 + pre_gate * (1.0 - sigmoid_gate))
    ).astype(jnp.bfloat16)
    pre_up_grad = (hidden_grad * activated).astype(jnp.bfloat16)
    route_grad = lax.dot_general(
        pre_gate_grad, gate_w, (((1,), (1,)), ((), ())), preferred_element_type=jnp.float32
    )
    route_grad = route_grad + lax.dot_general(
        pre_up_grad, up_w, (((1,), (1,)), ((), ())), preferred_element_type=jnp.float32
    )
    return (route_grad.astype(jnp.bfloat16), gate_grad, pre_gate_grad, pre_up_grad, hidden, scaled)


def on_device(tokens, out_grad, expert_ids, gates, w_gate, w_up, w_down):
    tok_rows, model_width = tokens.shape
    top_count = expert_ids.shape[1]
    peer_count = lax.axis_size("expert")
    capacity = min(tok_rows, tok_rows * top_count * 6 // (5 * peer_count))
    slot_total = peer_count * capacity
    places = slot_places(expert_ids, peer_count, capacity)
    source, filled = slot_sources(places, slot_total)
    token_source = source // top_count
    x_buf = fill_slots(tokens, token_source, filled).reshape(peer_count, capacity, model_width)
    dy_buf = fill_slots(out_grad, token_source, filled).reshape(peer_count, capacity, model_width)
    g_buf = fill_slots(gates.reshape(-1), source, filled).reshape(peer_count, capacity)
    gate_w = w_gate[0]
    up_w = w_up[0]
    down_w = w_down[0]
    hidden_width = gate_w.shape[1]
    x_in, dy_in, g_in = (
        lax.all_to_all(x_buf, "expert", split_axis=0, concat_axis=0, tiled=True),
        lax.all_to_all(dy_buf, "expert", split_axis=0, concat_axis=0, tiled=True),
        lax.all_to_all(g_buf, "expert", split_axis=0, concat_axis=0, tiled=True),
    )
    lead_dim = x_in.shape[0]
    item_total = x_in.shape[1]
    results = expert_pass(
        x_in.reshape(lead_dim * item_total, model_width),
        dy_in.reshape(lead_dim * item_total, model_width),
        g_in.reshape(lead_dim * item_total),
        gate_w,
        up_w,
        down_w,
    )
    route_grad, gate_grad, pre_gate_grad, pre_up_grad, hidden, scaled = tuple(
        (piece.reshape((lead_dim, item_total) + piece.shape[1:]) for piece in results)
    )
    back_dx, back_dg = (
        lax.all_to_all(route_grad, "expert", split_axis=0, concat_axis=0, tiled=True),
        lax.all_to_all(gate_grad, "expert", split_axis=0, concat_axis=0, tiled=True),
    )
    routed = back_dx.reshape(slot_total, model_width)[places]
    token_grad = jnp.sum(
        routed.reshape(tok_rows, top_count, model_width).astype(jnp.float32), axis=1
    ).astype(jnp.bfloat16)
    gate_grad_out = back_dg.reshape(slot_total)[places].reshape(tok_rows, top_count)
    x_rows = x_in.reshape(slot_total, model_width)
    scaled_rows = scaled.reshape(slot_total, model_width)
    gate_rows = pre_gate_grad.reshape(slot_total, hidden_width)
    up_rows = pre_up_grad.reshape(slot_total, hidden_width)
    hidden_rows = hidden.reshape(slot_total, hidden_width)
    contract = (((0,), (0,)), ((), ()))
    part_gate = lax.dot_general(x_rows, gate_rows, contract, preferred_element_type=jnp.float32)
    part_up = lax.dot_general(x_rows, up_rows, contract, preferred_element_type=jnp.float32)
    part_down = lax.dot_general(
        hidden_rows, scaled_rows, contract, preferred_element_type=jnp.float32
    )
    sum_gate, sum_up, sum_down = (
        lax.psum_scatter(
            part_gate.astype(jnp.bfloat16), "dp", scatter_dimension=0, tiled=True
        ).astype(jnp.float32),
        lax.psum_scatter(
            part_up.astype(jnp.bfloat16), "dp", scatter_dimension=0, tiled=True
        ).astype(jnp.float32),
        lax.psum_scatter(
            part_down.astype(jnp.bfloat16), "dp", scatter_dimension=1, tiled=True
        ).astype(jnp.float32),
    )
    return (
        token_grad,
        gate_grad_out,
        sum_gate.astype(jnp.bfloat16)[None],
        sum_up.astype(jnp.bfloat16)[None],
        sum_down.astype(jnp.bfloat16)[None],
    )


F32, BF16 = jnp.float32, jnp.bfloat16
ROWS_BY_ROWS = (((1,), (1,)), ((), ()))
OVER_ROWS = (((0,), (0,)), ((), ()))
LANES = 128
KERNEL_VMEM = 16 * 2**20
ALL_VMEM = 60 * 2**20
IN_VMEM = pl.BlockSpec(memory_space=pltpu.VMEM)
WHEREVER = pl.BlockSpec(memory_space=pl.ANY)
NO_COST = pl.CostEstimate(flops=0, bytes_accessed=0, transcendentals=0)


def tiles(total, step):
    return [slice(at, min(at + step, total)) for at in range(0, total, step)]


def used_rows(part):
    return part[0].shape[0] - part[0].shape[0] % 16


def take_parts(refs, layout):
    return [tuple(refs.pop(0) for _ in range(count)) for count in layout]


def stacked(parts, width, start, size):
    in_rest, at = start

    def read(part):
        rows = slice(0, used_rows(part))
        if len(part) == 2:
            return part[in_rest][rows, pl.ds(at, size)]
        return part[0][rows, pl.ds(at + width if in_rest else at, size)]

    return jnp.concatenate([read(part) for part in parts], axis=0)


def add_products(blocks, earlier, store, hidden_width):
    for which in range(3):
        for cols in tiles(hidden_width, 256):
            total = earlier[which][cols, :] if earlier else 0.0
            for block in blocks:
                left, right = block(which, cols)
                total += lax.dot_general(left, right, OVER_ROWS, preferred_element_type=F32)
            store(which, cols, total)


def dense_block(parts, grads, start, half, width):
    def block(which, cols):
        return grads[which][:, cols], stacked(parts, width, (which == 2, start), half)

    return block


def slot_block(ref, half, hidden_width):
    def block(which, cols):
        at = 2 * half + which * hidden_width
        first = half if which == 2 else 0
        return ref[:, at + cols.start : at + cols.stop], ref[:, first : first + half]

    return block


def choices(routing, top_count):
    lane = lax.broadcasted_iota(jnp.int32, routing.shape, 1)
    chosen = (routing == lax.axis_index("expert").astype(F32)) & (lane < top_count)
    shifted = pltpu.roll(routing, LANES - top_count, 1)
    gate = jnp.sum(jnp.where(chosen, shifted, 0.0), axis=1, keepdims=True)
    taken = jnp.sum(jnp.where(chosen, 1.0, 0.0), axis=1, keepdims=True)
    return gate, taken


def write_slots(outs, packs, carried, parts, grads, taken, sizes, width):
    tok_rows, slots, _, half = sizes
    total_rows, hidden_width = grads[0].shape
    shape = (total_rows, LANES)
    row = lax.broadcasted_iota(jnp.int32, (total_rows, total_rows), 0)
    other = lax.broadcasted_iota(jnp.int32, (total_rows, total_rows), 1)
    before = (other < row) & (other >= row - row % tok_rows)
    taken_lanes = jnp.broadcast_to(taken, shape).astype(BF16)
    count = jnp.dot(before.astype(BF16), taken_lanes, preferred_element_type=F32)
    part_of = lax.broadcasted_iota(jnp.int32, shape, 0) // tok_rows
    first = jnp.full(shape, LANES, jnp.int32)
    for order, part in enumerate(part for pack in packs for part in pack):
        first = jnp.where(part_of == part, order * slots, first)
    place = jnp.where(taken > 0.0, count.astype(jnp.int32) + first, LANES)
    picks = (place == lax.broadcasted_iota(jnp.int32, shape, 1)).astype(BF16)
    away = pl.multiple_of((1 - lax.axis_index("dp")) * half, half)

    def fill(values, at):
        rows = lax.dot_general(picks, values, OVER_ROWS, preferred_element_type=F32)
        columns = slice(at, at + rows.shape[1])
        first = 0
        for order, (out, pack) in enumerate(zip(outs, packs)):
            count = len(pack) * slots
            block = rows[first : first + count]
            if order == 0 and carried is not None:
                block = jnp.concatenate([carried[:, columns].astype(F32), block], axis=0)
            out[:, columns] = block.astype(BF16)
            first += count

    fill(stacked(parts, width, (0, away), half), 0)
    fill(stacked(parts, width, (1, away), half), half)
    for which in range(3):
        fill(grads[which][...], 2 * half + which * hidden_width)


def slots_kernel(layout, packs, has_carried, sizes, width, *refs):
    refs = list(refs)
    parts = take_parts(refs, layout)
    grads, refs = refs[:3], refs[3:]
    carried = refs.pop(0) if has_carried else None
    routing = stacked(parts, width, (1, width), LANES).astype(F32)
    _, taken = choices(routing, sizes[2])
    write_slots(refs, packs, carried, parts, grads, taken, sizes, width)


def slot_rows(parts, grads, sizes, width, packs, carried=None):
    _, slots, _, half = sizes
    operands = [*flat(parts), *grads] + ([carried] if carried is not None else [])
    shapes = []
    for order, pack in enumerate(packs):
        count = slots * len(pack)
        if order == 0 and carried is not None:
            count += carried.shape[0]
        shapes.append((count, 2 * half + 3 * grads[0].shape[1]))
    return list(
        pl.pallas_call(
            functools.partial(
                slots_kernel,
                [len(part) for part in parts],
                packs,
                carried is not None,
                sizes,
                width,
            ),
            out_shape=[jax.ShapeDtypeStruct(shape, BF16) for shape in shapes],
            in_specs=[IN_VMEM] * len(operands),
            out_specs=[IN_VMEM] * len(shapes),
            compiler_params=pltpu.CompilerParams(vmem_limit_bytes=KERNEL_VMEM),
            cost_estimate=NO_COST,
        )(*operands)
    )


def rows_kernel(layout, packs, waiting, slot_total, after, has_sums, adds, routed, sizes, *refs):
    refs = list(refs)
    _, _, top_count, half = sizes

    def take(count):
        taken = refs[:count]
        del refs[:count]
        return taken

    parts, (gate_w, up_w, down_w) = take_parts(refs, layout), take(3)
    dense = [(take_parts(refs, parts_layout), take(3)) for parts_layout in waiting]
    came = take(slot_total)
    take(after)
    earlier = take(3) if has_sums else None
    kept_out, given_out = take(2) if routed else (None, None)
    slots_outs = take(len(packs))
    sums = take(3) if adds else None
    grads = take(3)
    pre_gate_out, pre_up_out, hidden_out = grads
    hidden_width, width = gate_w.shape
    x = stacked(parts, width, (0, 0), width)
    dy = stacked(parts, width, (1, 0), width)
    routing = stacked(parts, width, (1, width), LANES).astype(F32)
    gate, taken = choices(routing, top_count)
    gate_grad = jnp.zeros_like(gate)
    for cols in tiles(hidden_width, 256):
        pre_gate = lax.dot_general(x, gate_w[cols, :], ROWS_BY_ROWS, preferred_element_type=F32)
        pre_up = lax.dot_general(x, up_w[cols, :], ROWS_BY_ROWS, preferred_element_type=F32)
        down_grad = lax.dot_general(dy, down_w[cols, :], ROWS_BY_ROWS, preferred_element_type=F32)
        sigmoid_gate = jax.nn.sigmoid(pre_gate)
        activated = pre_gate * sigmoid_gate
        hidden = activated * pre_up
        gate_grad += jnp.sum(hidden * down_grad, axis=1, keepdims=True)
        hidden_grad = gate * down_grad
        slope = sigmoid_gate * (1.0 + pre_gate * (1.0 - sigmoid_gate))
        pre_gate_out[:, cols] = (hidden_grad * pre_up * slope).astype(BF16)
        pre_up_out[:, cols] = (hidden_grad * activated).astype(BF16)
        hidden_out[:, cols] = (gate * hidden).astype(BF16)
    if routed:
        half_rows = routing.shape[0] // 2
        lane = lax.broadcasted_iota(jnp.int32, routing.shape, 1)
        table = jnp.where(lane == lax.axis_index("expert"), gate_grad * taken, 0.0).astype(BF16)
        kept_out[:, width:] = table[:half_rows]
        given_out[:, width:] = table[half_rows:]
        for cols in tiles(width, 512):
            route = jnp.dot(pre_gate_out[...], gate_w[:, cols], preferred_element_type=F32)
            route += jnp.dot(pre_up_out[...], up_w[:, cols], preferred_element_type=F32)
            route = route.astype(BF16)
            kept_out[:, cols] = route[:half_rows]
            given_out[:, cols] = route[half_rows:]

    if packs:
        write_slots(slots_outs, packs, None, parts, grads, taken, sizes, width)
    if adds:
        start = pl.multiple_of(lax.axis_index("dp") * half, half)
        blocks = [dense_block(*block, start, half, width) for block in [(parts, grads), *dense]]
        blocks += [slot_block(ref, half, hidden_width) for ref in came]

        def store(which, cols, total):
            sums[which][cols, :] = total

        add_products(blocks, earlier, store, hidden_width)


def flat(parts):
    return [array for part in parts for array in part]


def expert_rows(
    parts, weights, sizes, sums=None, packs=(), waiting=(), came=(), after=(), adds=True, routed=True
):
    _, slots, _, half = sizes
    total = sum(used_rows(part) for part in parts)
    hidden_width, width = weights[0].shape
    operands = [*flat(parts), *weights]
    for block_parts, block_grads in waiting:
        operands += [*flat(block_parts), *block_grads]
    operands += [*came, *after, *(sums or ())]
    wide = jax.ShapeDtypeStruct((total // 2, width + LANES), BF16)
    grad = jax.ShapeDtypeStruct((total, hidden_width), BF16)
    added = jax.ShapeDtypeStruct((hidden_width, half), F32)
    results = [wide] * (2 * routed)
    for pack in packs:
        shape = (slots * len(pack), 2 * half + 3 * hidden_width)
        results.append(jax.ShapeDtypeStruct(shape, BF16))
    first = len(results)
    results += [added] * 3 if adds else [grad] * 3
    first_sum = len(operands) - 3
    results = pl.pallas_call(
        functools.partial(
            rows_kernel,
            [len(part) for part in parts],
            packs,
            [[len(part) for part in block_parts] for block_parts, _ in waiting],
            len(came),
            len(after),
            sums is not None,
            adds,
            routed,
            sizes,
        ),
        out_shape=results,
        in_specs=[WHEREVER if any(o is a for a in after) else IN_VMEM for o in operands],
        out_specs=[IN_VMEM] * len(results),
        input_output_aliases={first_sum + i: first + i for i in range(3)} if sums else {},
        scratch_shapes=[pltpu.VMEM(grad.shape, BF16)] * (3 * adds),
        compiler_params=pltpu.CompilerParams(vmem_limit_bytes=KERNEL_VMEM),
        cost_estimate=NO_COST,
    )(*operands)
    return list(results[: 2 * routed]), list(results[2 * routed : first]), list(results[first:])


def sums_kernel(waiting, slot_total, half, width, *refs):
    refs = list(refs)

    def take(count):
        taken = refs[:count]
        del refs[:count]
        return taken

    dense = [(take_parts(refs, layout), take(3)) for layout in waiting]
    came, earlier, outs = take(slot_total), take(3), take(3)
    hidden_width = earlier[0].shape[0]
    start = pl.multiple_of(lax.axis_index("dp") * half, half)
    blocks = [dense_block(*block, start, half, width) for block in dense]
    blocks += [slot_block(ref, half, hidden_width) for ref in came]

    def store(which, cols, total):
        outs[which][cols, :] = total

    add_products(blocks, earlier, store, hidden_width)


def add_rows(came, sums, width, waiting=()):
    hidden_width, half = sums[0].shape
    operands = []
    for block_parts, block_grads in waiting:
        operands += [*flat(block_parts), *block_grads]
    operands += [*came, *sums]
    added = jax.ShapeDtypeStruct((hidden_width, half), F32)
    first_sum = len(operands) - 3
    return list(
        pl.pallas_call(
            functools.partial(
                sums_kernel,
                [[len(part) for part in block_parts] for block_parts, _ in waiting],
                len(came),
                half,
                width,
            ),
            out_shape=[added] * 3,
            in_specs=[IN_VMEM] * len(operands),
            out_specs=[IN_VMEM] * 3,
            input_output_aliases={first_sum + i: i for i in range(3)},
            compiler_params=pltpu.CompilerParams(vmem_limit_bytes=KERNEL_VMEM),
            cost_estimate=NO_COST,
        )(*operands)
    )


def pack_kernel(tokens, out_grad, ids, gates, out, ids_held, gates_held, sent):
    width = tokens.shape[1]
    top_count = ids.shape[0]
    copies = [
        pltpu.make_async_copy(ids, ids_held, sent.at[0]),
        pltpu.make_async_copy(gates, gates_held, sent.at[1]),
        pltpu.make_async_copy(tokens, out.at[:, pl.ds(0, width)], sent.at[2]),
        pltpu.make_async_copy(out_grad, out.at[:, pl.ds(width, width)], sent.at[3]),
    ]
    for copy in copies:
        copy.start()
    row = lax.broadcasted_iota(jnp.int32, (top_count, LANES), 0)
    lane = lax.broadcasted_iota(jnp.int32, (top_count, LANES), 1)
    routing = 0.0
    for held, copy, at in ((ids_held, copies[0], 0), (gates_held, copies[1], top_count)):
        copy.wait()
        values = held[...].astype(F32).astype(BF16)
        spread = (lane == row + at).astype(BF16)
        routing += lax.dot_general(values, spread, OVER_ROWS, preferred_element_type=F32)
    out[:, 2 * width :] = routing.astype(BF16)
    copies[2].wait()
    copies[3].wait()


def packed_rows(tokens, out_grad, expert_ids, gates):
    rows, width = tokens.shape
    top_count = expert_ids.shape[1]
    return pl.pallas_call(
        pack_kernel,
        out_shape=jax.ShapeDtypeStruct((rows, 2 * width + LANES), BF16),
        in_specs=[WHEREVER] * 4,
        out_specs=IN_VMEM,
        scratch_shapes=[
            pltpu.VMEM((top_count, rows), jnp.int32),
            pltpu.VMEM((top_count, rows), BF16),
            pltpu.SemaphoreType.DMA((4,)),
        ],
        compiler_params=pltpu.CompilerParams(vmem_limit_bytes=ALL_VMEM),
        cost_estimate=NO_COST,
    )(tokens, out_grad, expert_ids.T, gates.T)


def finish_kernel(experts, *refs):
    kept, given, fore, rear, ids, came, *refs = refs
    earlier, (token_out, gate_out), sums = refs[:3], refs[3:5], refs[5:8]
    rounded, sent = refs[8:]
    hidden_width, half = earlier[0].shape

    def store(which, cols, total):
        rounded[which, cols, :] = total.astype(BF16)
        pltpu.make_async_copy(
            rounded.at[which, cols, :], sums[which].at[cols, :], sent.at[which]
        ).start()

    add_products([slot_block(came, half, hidden_width)], earlier, store, hidden_width)
    rows, width = token_out.shape
    total = kept[...].astype(F32) + given[...].astype(F32) + fore[...].astype(F32)
    total += rear[...].astype(F32)
    token_out[...] = total[:, :width].astype(BF16)
    table = jnp.transpose(total[:, width:])
    chosen = ids[...]
    grad = jnp.zeros(chosen.shape, F32)
    for expert in range(experts):
        grad += jnp.where(chosen == expert, table[expert : expert + 1, :rows], 0.0)
    gate_out[...] = grad.astype(BF16)
    for which in range(3):
        pltpu.make_async_copy(rounded.at[which], sums[which], sent.at[which]).wait()


def finished(experts, kept, given, fore, rear, expert_ids, came, sums):
    rows, top_count = expert_ids.shape
    hidden_width, half = sums[0].shape
    token_grad, gate_grad, *sums = pl.pallas_call(
        functools.partial(finish_kernel, experts),
        out_shape=[
            jax.ShapeDtypeStruct((rows, kept.shape[1] - LANES), BF16),
            jax.ShapeDtypeStruct((top_count, rows), BF16),
        ]
        + [jax.ShapeDtypeStruct((hidden_width, half), BF16)] * 3,
        in_specs=[IN_VMEM] * 9,
        out_specs=[IN_VMEM] * 2 + [WHEREVER] * 3,
        scratch_shapes=[
            pltpu.VMEM((3, hidden_width, half), BF16),
            pltpu.SemaphoreType.DMA((3,)),
        ],
        compiler_params=pltpu.CompilerParams(vmem_limit_bytes=KERNEL_VMEM),
        cost_estimate=NO_COST,
    )(kept, given, fore, rear, expert_ids.T, came, *sums)
    return token_grad, gate_grad.T, sums


def chip_ring(expert_count):
    depth = expert_count // 4
    return [2 * z for z in range(depth)] + [2 * z + 1 for z in reversed(range(depth))]


def ring_shift(expert_count, by):
    order = chip_ring(expert_count)
    total = len(order)
    return sorted(
        (2 * chip + core, 2 * order[(place + by) % total] + core)
        for place, chip in enumerate(order)
        for core in range(2)
    )


def on_ring(tokens, out_grad, expert_ids, gates, w_gate, w_up, w_down):
    rows, width = tokens.shape
    top_count = expert_ids.shape[1]
    experts = lax.axis_size("expert")
    half = width // lax.axis_size("dp")
    capacity = min(rows, rows * top_count * 6 // (5 * experts))
    sizes = (rows, capacity, top_count, half)
    forth, back = ring_shift(experts, 1), ring_shift(experts, -1)
    weights = (w_gate[0].T, w_up[0].T, w_down[0])
    stage = lax.optimization_barrier

    def go(value, pairs):
        return lax.ppermute(value, "expert", pairs)

    def sibling(value):
        return lax.ppermute(value, "expert", [(i, i ^ 1) for i in range(experts)])

    def across(value):
        return lax.ppermute(value, "dp", [(0, 1), (1, 0)])

    def with_siblings(parts):
        return parts + [tuple(sibling(array) for array in part) for part in parts]

    def expert(parts, sums=None, packs=(), **options):
        return expert_rows(parts, weights, sizes, sums, packs, **options)

    def passed_on(item, fore, rear):
        total = item[0].astype(F32) + item[1].astype(F32)
        fore = go((total[rows:] + fore.astype(F32)).astype(BF16), forth)
        rear = go((total[:rows] + rear.astype(F32)).astype(BF16), back)
        return fore, rear

    own = packed_rows(tokens, out_grad, expert_ids, gates)
    fore, rear, over0 = go(own, forth), go(own, back), across(own)
    parts0 = with_siblings([(own,)])
    near0, _, grads0 = expert(parts0, adds=False)
    fore, rear, over0, near0, block0 = stage((fore, rear, over0, near0, (parts0, grads0)))

    parts = with_siblings([(fore,), (rear,)])
    over1 = across(jnp.concatenate([fore, rear], axis=0))
    fore, rear = go(fore, forth), go(rear, back)
    near1, _, sums = expert(parts, waiting=[block0])
    fore, rear, near1, sums = stage((fore, rear, near1, sums))

    parts = with_siblings([(fore,), (rear,)])
    over2 = across(jnp.pad(fore, ((0, 0), (0, LANES))))
    fore, rear = go(fore, forth), go(rear, back)
    near2, slots2, sums = expert(parts, sums, [(1, 3)])
    fore, rear, over1, near2, slots2, sums = stage((fore, rear, over1, near2, slots2, sums))

    parts3 = with_siblings([(fore,), (rear,)])
    far_x, far_rest = go(fore[:, :width], forth), go(rear[:, width:], back)
    came2 = across(slots2[0])
    near3, _, grads3 = expert(parts3, adds=False)
    far_x, far_rest, over2, near3, block3 = stage(
        (far_x, far_rest, over2, near3, (parts3, grads3))
    )

    parts4 = with_siblings([(far_x, far_rest)])
    near3[1], near2[1] = sibling(near3[1]), sibling(near2[1])
    slots3 = slot_rows(*block3, sizes, width, [(0, 1, 2), (3,)])
    near4, _, grads4 = expert(parts4, after=slots3, adds=False)
    near2, near3, near4, slots3, block4, came2 = stage(
        (near2, near3, near4, slots3, (parts4, grads4), came2)
    )
    came3 = across(slots3[0])
    near4[1] = sibling(near4[1])
    sum4 = (near4[0].astype(F32) + near4[1].astype(F32)).astype(BF16)
    cut = width // 2
    fore, rear = go(sum4[:, :cut], forth), go(sum4[:, cut:], back)
    fore, rear, near1, over0, over2 = stage((fore, rear, near1, over0, over2))
    fore = jnp.pad(fore, ((0, 0), (0, width + LANES - cut)))
    rear = jnp.pad(rear, ((0, 0), (cut, 0)))

    fore, rear = passed_on(near3, fore, rear)
    over = with_siblings([(over0,), (over2,)])
    sums = add_rows([came2], sums, width, [block3, block4])
    slots4 = slot_rows(*block4, sizes, width, [(0, 1)], slots3[1])
    fore, rear, near1, over1, over, came3, sums, slots4 = stage(
        (fore, rear, near1, over1, over, came3, sums, slots4)
    )

    came4 = across(slots4[0])
    fore, rear = passed_on(near2, fore, rear)
    near1[1] = sibling(near1[1])
    over1 = with_siblings([(over1,)])
    sums = expert(over, sums, routed=False)[2]
    fore, rear, near0, near1, over1, sums = stage((fore, rear, near0, near1, over1, sums))

    fore, rear = passed_on(near1, fore, rear)
    near0[1] = sibling(near0[1])
    sums = expert(over1, sums, came=[came3], routed=False)[2]
    fore, rear, near0, came4, sums = stage((fore, rear, near0, came4, sums))

    token_grad, gate_grad, sums = finished(experts, *near0, fore, rear, expert_ids, came4, sums)
    return (token_grad, gate_grad, sums[0].T[None], sums[1].T[None], sums[2][None])


def solution(mesh):
    in_specs = (
        P(("dp", "expert"), None),
        P(("dp", "expert"), None),
        P(("dp", "expert"), None),
        P(("dp", "expert"), None),
        P("expert", None, None),
        P("expert", None, None),
        P("expert", None, None),
    )
    out_specs = (
        P(("dp", "expert"), None),
        P(("dp", "expert"), None),
        P("expert", "dp", None),
        P("expert", "dp", None),
        P("expert", None, "dp"),
    )
    on_slice = on_ring if (mesh.shape["dp"], mesh.shape["expert"]) == (2, 16) else on_device
    return jax.shard_map(
        on_slice, mesh=mesh, in_specs=in_specs, out_specs=out_specs, check_vma=False
    )
```

```python
import functools

import jax
import jax.numpy as jnp
from jax import lax
from jax.experimental import pallas as pl
from jax.experimental.pallas import tpu as pltpu
from jax.sharding import PartitionSpec as P


def slot_places(expert_ids, experts, capacity):
    flat_ids = expert_ids.reshape(-1)
    labels = jnp.arange(experts, dtype=jnp.int32)
    onehot = (flat_ids[:, None] == labels[None, :]).astype(jnp.int32)
    earlier = jnp.cumsum(onehot, axis=0) - onehot
    slot_index = jnp.sum(earlier * onehot, axis=1)
    return flat_ids * capacity + slot_index


def slot_sources(places, slot_total):
    route_total = places.shape[0]
    filler = (
        jnp.zeros((slot_total,), jnp.int32)
        .at[places]
        .set(jnp.arange(route_total, dtype=jnp.int32) + 1)
    )
    return (jnp.maximum(filler - 1, 0), filler > 0)


def fill_slots(values, source, filled):
    taken = values[source]
    keep_mask = filled.reshape(filled.shape + (1,) * (taken.ndim - 1))
    return jnp.where(keep_mask, taken, jnp.zeros_like(taken))


def expert_pass(x_rows, dy_rows, g_rows, gate_w, up_w, down_w):
    pre_gate = jnp.dot(x_rows, gate_w, preferred_element_type=jnp.float32)
    pre_up = jnp.dot(x_rows, up_w, preferred_element_type=jnp.float32)
    sigmoid_gate = jax.nn.sigmoid(pre_gate)
    activated = pre_gate * sigmoid_gate
    hidden = (activated * pre_up).astype(jnp.bfloat16)
    expert_out = jnp.dot(hidden, down_w, preferred_element_type=jnp.float32)
    gate_grad = jnp.sum(dy_rows.astype(jnp.float32) * expert_out, axis=-1).astype(jnp.bfloat16)
    scaled = (g_rows.astype(jnp.float32)[:, None] * dy_rows.astype(jnp.float32)).astype(
        jnp.bfloat16
    )
    hidden_grad = lax.dot_general(
        scaled, down_w, (((1,), (1,)), ((), ())), preferred_element_type=jnp.float32
    )
    pre_gate_grad = (
        hidden_grad * pre_up * sigmoid_gate * (1.0 + pre_gate * (1.0 - sigmoid_gate))
    ).astype(jnp.bfloat16)
    pre_up_grad = (hidden_grad * activated).astype(jnp.bfloat16)
    route_grad = lax.dot_general(
        pre_gate_grad, gate_w, (((1,), (1,)), ((), ())), preferred_element_type=jnp.float32
    )
    route_grad = route_grad + lax.dot_general(
        pre_up_grad, up_w, (((1,), (1,)), ((), ())), preferred_element_type=jnp.float32
    )
    return (route_grad.astype(jnp.bfloat16), gate_grad, pre_gate_grad, pre_up_grad, hidden, scaled)


def on_device(tokens, out_grad, expert_ids, gates, w_gate, w_up, w_down):
    tok_rows, model_width = tokens.shape
    top_count = expert_ids.shape[1]
    peer_count = lax.axis_size("expert")
    capacity = min(tok_rows, tok_rows * top_count * 6 // (5 * peer_count))
    slot_total = peer_count * capacity
    places = slot_places(expert_ids, peer_count, capacity)
    source, filled = slot_sources(places, slot_total)
    token_source = source // top_count
    x_buf = fill_slots(tokens, token_source, filled).reshape(peer_count, capacity, model_width)
    dy_buf = fill_slots(out_grad, token_source, filled).reshape(peer_count, capacity, model_width)
    g_buf = fill_slots(gates.reshape(-1), source, filled).reshape(peer_count, capacity)
    gate_w = w_gate[0]
    up_w = w_up[0]
    down_w = w_down[0]
    hidden_width = gate_w.shape[1]
    x_in, dy_in, g_in = (
        lax.all_to_all(x_buf, "expert", split_axis=0, concat_axis=0, tiled=True),
        lax.all_to_all(dy_buf, "expert", split_axis=0, concat_axis=0, tiled=True),
        lax.all_to_all(g_buf, "expert", split_axis=0, concat_axis=0, tiled=True),
    )
    lead_dim = x_in.shape[0]
    item_total = x_in.shape[1]
    results = expert_pass(
        x_in.reshape(lead_dim * item_total, model_width),
        dy_in.reshape(lead_dim * item_total, model_width),
        g_in.reshape(lead_dim * item_total),
        gate_w,
        up_w,
        down_w,
    )
    route_grad, gate_grad, pre_gate_grad, pre_up_grad, hidden, scaled = tuple(
        (piece.reshape((lead_dim, item_total) + piece.shape[1:]) for piece in results)
    )
    back_dx, back_dg = (
        lax.all_to_all(route_grad, "expert", split_axis=0, concat_axis=0, tiled=True),
        lax.all_to_all(gate_grad, "expert", split_axis=0, concat_axis=0, tiled=True),
    )
    routed = back_dx.reshape(slot_total, model_width)[places]
    token_grad = jnp.sum(
        routed.reshape(tok_rows, top_count, model_width).astype(jnp.float32), axis=1
    ).astype(jnp.bfloat16)
    gate_grad_out = back_dg.reshape(slot_total)[places].reshape(tok_rows, top_count)
    x_rows = x_in.reshape(slot_total, model_width)
    scaled_rows = scaled.reshape(slot_total, model_width)
    gate_rows = pre_gate_grad.reshape(slot_total, hidden_width)
    up_rows = pre_up_grad.reshape(slot_total, hidden_width)
    hidden_rows = hidden.reshape(slot_total, hidden_width)
    contract = (((0,), (0,)), ((), ()))
    part_gate = lax.dot_general(x_rows, gate_rows, contract, preferred_element_type=jnp.float32)
    part_up = lax.dot_general(x_rows, up_rows, contract, preferred_element_type=jnp.float32)
    part_down = lax.dot_general(
        hidden_rows, scaled_rows, contract, preferred_element_type=jnp.float32
    )
    sum_gate, sum_up, sum_down = (
        lax.psum_scatter(
            part_gate.astype(jnp.bfloat16), "dp", scatter_dimension=0, tiled=True
        ).astype(jnp.float32),
        lax.psum_scatter(
            part_up.astype(jnp.bfloat16), "dp", scatter_dimension=0, tiled=True
        ).astype(jnp.float32),
        lax.psum_scatter(
            part_down.astype(jnp.bfloat16), "dp", scatter_dimension=1, tiled=True
        ).astype(jnp.float32),
    )
    return (
        token_grad,
        gate_grad_out,
        sum_gate.astype(jnp.bfloat16)[None],
        sum_up.astype(jnp.bfloat16)[None],
        sum_down.astype(jnp.bfloat16)[None],
    )


F32, BF16 = jnp.float32, jnp.bfloat16
ROWS_BY_ROWS = (((1,), (1,)), ((), ()))
OVER_ROWS = (((0,), (0,)), ((), ()))
LANES = 128
KERNEL_VMEM = 16 * 2**20
ALL_VMEM = 60 * 2**20
IN_VMEM = pl.BlockSpec(memory_space=pltpu.VMEM)
WHEREVER = pl.BlockSpec(memory_space=pl.ANY)
NO_COST = pl.CostEstimate(flops=0, bytes_accessed=0, transcendentals=0)


def tiles(total, step):
    return [slice(at, min(at + step, total)) for at in range(0, total, step)]


def used_rows(part):
    return part[0].shape[0] - part[0].shape[0] % 16


def take_parts(refs, layout):
    return [tuple(refs.pop(0) for _ in range(count)) for count in layout]


def stacked(parts, width, start, size):
    in_rest, at = start

    def read(part):
        rows = slice(0, used_rows(part))
        if len(part) == 2:
            return part[in_rest][rows, pl.ds(at, size)]
        return part[0][rows, pl.ds(at + width if in_rest else at, size)]

    return jnp.concatenate([read(part) for part in parts], axis=0)


def add_products(blocks, earlier, store, hidden_width):
    for which in range(3):
        for cols in tiles(hidden_width, 256):
            total = earlier[which][cols, :] if earlier else 0.0
            for block in blocks:
                left, right = block(which, cols)
                total += lax.dot_general(left, right, OVER_ROWS, preferred_element_type=F32)
            store(which, cols, total)


def dense_block(parts, grads, start, half, width):
    def block(which, cols):
        return grads[which][:, cols], stacked(parts, width, (which == 2, start), half)

    return block


def slot_block(ref, half, hidden_width):
    def block(which, cols):
        at = 2 * half + which * hidden_width
        first = half if which == 2 else 0
        return ref[:, at + cols.start : at + cols.stop], ref[:, first : first + half]

    return block


def choices(routing, top_count):
    lane = lax.broadcasted_iota(jnp.int32, routing.shape, 1)
    chosen = (routing == lax.axis_index("expert").astype(F32)) & (lane < top_count)
    shifted = pltpu.roll(routing, LANES - top_count, 1)
    gate = jnp.sum(jnp.where(chosen, shifted, 0.0), axis=1, keepdims=True)
    taken = jnp.sum(jnp.where(chosen, 1.0, 0.0), axis=1, keepdims=True)
    return gate, taken


def write_slots(outs, packs, carried, parts, grads, taken, sizes, width):
    tok_rows, slots, _, half = sizes
    total_rows, hidden_width = grads[0].shape
    shape = (total_rows, LANES)
    row = lax.broadcasted_iota(jnp.int32, (total_rows, total_rows), 0)
    other = lax.broadcasted_iota(jnp.int32, (total_rows, total_rows), 1)
    before = (other < row) & (other >= row - row % tok_rows)
    taken_lanes = jnp.broadcast_to(taken, shape).astype(BF16)
    count = jnp.dot(before.astype(BF16), taken_lanes, preferred_element_type=F32)
    part_of = lax.broadcasted_iota(jnp.int32, shape, 0) // tok_rows
    first = jnp.full(shape, LANES, jnp.int32)
    for order, part in enumerate(part for pack in packs for part in pack):
        first = jnp.where(part_of == part, order * slots, first)
    place = jnp.where(taken > 0.0, count.astype(jnp.int32) + first, LANES)
    picks = (place == lax.broadcasted_iota(jnp.int32, shape, 1)).astype(BF16)
    away = pl.multiple_of((1 - lax.axis_index("dp")) * half, half)

    def fill(values, at):
        rows = lax.dot_general(picks, values, OVER_ROWS, preferred_element_type=F32)
        columns = slice(at, at + rows.shape[1])
        first = 0
        for order, (out, pack) in enumerate(zip(outs, packs)):
            count = len(pack) * slots
            block = rows[first : first + count]
            if order == 0 and carried is not None:
                block = jnp.concatenate([carried[:, columns].astype(F32), block], axis=0)
            out[:, columns] = block.astype(BF16)
            first += count

    fill(stacked(parts, width, (0, away), half), 0)
    fill(stacked(parts, width, (1, away), half), half)
    for which in range(3):
        fill(grads[which][...], 2 * half + which * hidden_width)


def slots_kernel(layout, packs, has_carried, sizes, width, *refs):
    refs = list(refs)
    parts = take_parts(refs, layout)
    grads, refs = refs[:3], refs[3:]
    carried = refs.pop(0) if has_carried else None
    routing = stacked(parts, width, (1, width), LANES).astype(F32)
    _, taken = choices(routing, sizes[2])
    write_slots(refs, packs, carried, parts, grads, taken, sizes, width)


def slot_rows(parts, grads, sizes, width, packs, carried=None):
    _, slots, _, half = sizes
    operands = [*flat(parts), *grads] + ([carried] if carried is not None else [])
    shapes = []
    for order, pack in enumerate(packs):
        count = slots * len(pack)
        if order == 0 and carried is not None:
            count += carried.shape[0]
        shapes.append((count, 2 * half + 3 * grads[0].shape[1]))
    return list(
        pl.pallas_call(
            functools.partial(
                slots_kernel,
                [len(part) for part in parts],
                packs,
                carried is not None,
                sizes,
                width,
            ),
            out_shape=[jax.ShapeDtypeStruct(shape, BF16) for shape in shapes],
            in_specs=[IN_VMEM] * len(operands),
            out_specs=[IN_VMEM] * len(shapes),
            compiler_params=pltpu.CompilerParams(vmem_limit_bytes=KERNEL_VMEM),
            cost_estimate=NO_COST,
        )(*operands)
    )


def rows_kernel(layout, packs, waiting, slot_total, after, has_sums, adds, routed, sizes, *refs):
    refs = list(refs)
    _, _, top_count, half = sizes

    def take(count):
        taken = refs[:count]
        del refs[:count]
        return taken

    parts, (gate_w, up_w, down_w) = take_parts(refs, layout), take(3)
    dense = [(take_parts(refs, parts_layout), take(3)) for parts_layout in waiting]
    came = take(slot_total)
    take(after)
    earlier = take(3) if has_sums else None
    kept_out, given_out = take(2) if routed else (None, None)
    slots_outs = take(len(packs))
    sums = take(3) if adds else None
    grads = take(3)
    pre_gate_out, pre_up_out, hidden_out = grads
    hidden_width, width = gate_w.shape
    x = stacked(parts, width, (0, 0), width)
    dy = stacked(parts, width, (1, 0), width)
    routing = stacked(parts, width, (1, width), LANES).astype(F32)
    gate, taken = choices(routing, top_count)
    gate_grad = jnp.zeros_like(gate)
    for cols in tiles(hidden_width, 256):
        pre_gate = lax.dot_general(x, gate_w[cols, :], ROWS_BY_ROWS, preferred_element_type=F32)
        pre_up = lax.dot_general(x, up_w[cols, :], ROWS_BY_ROWS, preferred_element_type=F32)
        down_grad = lax.dot_general(dy, down_w[cols, :], ROWS_BY_ROWS, preferred_element_type=F32)
        sigmoid_gate = jax.nn.sigmoid(pre_gate)
        activated = pre_gate * sigmoid_gate
        hidden = activated * pre_up
        gate_grad += jnp.sum(hidden * down_grad, axis=1, keepdims=True)
        hidden_grad = gate * down_grad
        slope = sigmoid_gate * (1.0 + pre_gate * (1.0 - sigmoid_gate))
        pre_gate_out[:, cols] = (hidden_grad * pre_up * slope).astype(BF16)
        pre_up_out[:, cols] = (hidden_grad * activated).astype(BF16)
        hidden_out[:, cols] = (gate * hidden).astype(BF16)
    if routed:
        half_rows = routing.shape[0] // 2
        lane = lax.broadcasted_iota(jnp.int32, routing.shape, 1)
        table = jnp.where(lane == lax.axis_index("expert"), gate_grad * taken, 0.0).astype(BF16)
        kept_out[:, width:] = table[:half_rows]
        given_out[:, width:] = table[half_rows:]
        for cols in tiles(width, 512):
            route = jnp.dot(pre_gate_out[...], gate_w[:, cols], preferred_element_type=F32)
            route += jnp.dot(pre_up_out[...], up_w[:, cols], preferred_element_type=F32)
            route = route.astype(BF16)
            kept_out[:, cols] = route[:half_rows]
            given_out[:, cols] = route[half_rows:]

    if packs:
        write_slots(slots_outs, packs, None, parts, grads, taken, sizes, width)
    if adds:
        start = pl.multiple_of(lax.axis_index("dp") * half, half)
        blocks = [dense_block(*block, start, half, width) for block in [(parts, grads), *dense]]
        blocks += [slot_block(ref, half, hidden_width) for ref in came]

        def store(which, cols, total):
            sums[which][cols, :] = total

        add_products(blocks, earlier, store, hidden_width)


def flat(parts):
    return [array for part in parts for array in part]


def expert_rows(
    parts, weights, sizes, sums=None, packs=(), waiting=(), came=(), after=(), adds=True, routed=True
):
    _, slots, _, half = sizes
    total = sum(used_rows(part) for part in parts)
    hidden_width, width = weights[0].shape
    operands = [*flat(parts), *weights]
    for block_parts, block_grads in waiting:
        operands += [*flat(block_parts), *block_grads]
    operands += [*came, *after, *(sums or ())]
    wide = jax.ShapeDtypeStruct((total // 2, width + LANES), BF16)
    grad = jax.ShapeDtypeStruct((total, hidden_width), BF16)
    added = jax.ShapeDtypeStruct((hidden_width, half), F32)
    results = [wide] * (2 * routed)
    for pack in packs:
        shape = (slots * len(pack), 2 * half + 3 * hidden_width)
        results.append(jax.ShapeDtypeStruct(shape, BF16))
    first = len(results)
    results += [added] * 3 if adds else [grad] * 3
    first_sum = len(operands) - 3
    results = pl.pallas_call(
        functools.partial(
            rows_kernel,
            [len(part) for part in parts],
            packs,
            [[len(part) for part in block_parts] for block_parts, _ in waiting],
            len(came),
            len(after),
            sums is not None,
            adds,
            routed,
            sizes,
        ),
        out_shape=results,
        in_specs=[WHEREVER if any(o is a for a in after) else IN_VMEM for o in operands],
        out_specs=[IN_VMEM] * len(results),
        input_output_aliases={first_sum + i: first + i for i in range(3)} if sums else {},
        scratch_shapes=[pltpu.VMEM(grad.shape, BF16)] * (3 * adds),
        compiler_params=pltpu.CompilerParams(vmem_limit_bytes=KERNEL_VMEM),
        cost_estimate=NO_COST,
    )(*operands)
    return list(results[: 2 * routed]), list(results[2 * routed : first]), list(results[first:])


def sums_kernel(waiting, slot_total, half, width, *refs):
    refs = list(refs)

    def take(count):
        taken = refs[:count]
        del refs[:count]
        return taken

    dense = [(take_parts(refs, layout), take(3)) for layout in waiting]
    came, earlier, outs = take(slot_total), take(3), take(3)
    hidden_width = earlier[0].shape[0]
    start = pl.multiple_of(lax.axis_index("dp") * half, half)
    blocks = [dense_block(*block, start, half, width) for block in dense]
    blocks += [slot_block(ref, half, hidden_width) for ref in came]

    def store(which, cols, total):
        outs[which][cols, :] = total

    add_products(blocks, earlier, store, hidden_width)


def add_rows(came, sums, width, waiting=()):
    hidden_width, half = sums[0].shape
    operands = []
    for block_parts, block_grads in waiting:
        operands += [*flat(block_parts), *block_grads]
    operands += [*came, *sums]
    added = jax.ShapeDtypeStruct((hidden_width, half), F32)
    first_sum = len(operands) - 3
    return list(
        pl.pallas_call(
            functools.partial(
                sums_kernel,
                [[len(part) for part in block_parts] for block_parts, _ in waiting],
                len(came),
                half,
                width,
            ),
            out_shape=[added] * 3,
            in_specs=[IN_VMEM] * len(operands),
            out_specs=[IN_VMEM] * 3,
            input_output_aliases={first_sum + i: i for i in range(3)},
            compiler_params=pltpu.CompilerParams(vmem_limit_bytes=KERNEL_VMEM),
            cost_estimate=NO_COST,
        )(*operands)
    )


def pack_kernel(tokens, out_grad, ids, gates, out, ids_held, sent):
    width = tokens.shape[1]
    top_count = ids.shape[0]
    copies = [
        pltpu.make_async_copy(ids, ids_held, sent.at[0]),
        pltpu.make_async_copy(tokens, out.at[:, pl.ds(0, width)], sent.at[1]),
        pltpu.make_async_copy(out_grad, out.at[:, pl.ds(width, width)], sent.at[2]),
    ]
    for copy in copies:
        copy.start()
    row = lax.broadcasted_iota(jnp.int32, (top_count, LANES), 0)
    lane = lax.broadcasted_iota(jnp.int32, (top_count, LANES), 1)
    copies[0].wait()
    routing = 0.0
    for values, at in ((ids_held[...].astype(F32).astype(BF16), 0), (gates[...], top_count)):
        spread = (lane == row + at).astype(BF16)
        routing += lax.dot_general(values, spread, OVER_ROWS, preferred_element_type=F32)
    out[:, 2 * width :] = routing.astype(BF16)
    copies[1].wait()
    copies[2].wait()


def packed_rows(tokens, out_grad, expert_ids, gates):
    rows, width = tokens.shape
    top_count = expert_ids.shape[1]
    return pl.pallas_call(
        pack_kernel,
        out_shape=jax.ShapeDtypeStruct((rows, 2 * width + LANES), BF16),
        in_specs=[WHEREVER] * 3 + [IN_VMEM],
        out_specs=IN_VMEM,
        scratch_shapes=[
            pltpu.VMEM((top_count, rows), jnp.int32),
            pltpu.SemaphoreType.DMA((3,)),
        ],
        compiler_params=pltpu.CompilerParams(vmem_limit_bytes=ALL_VMEM),
        cost_estimate=NO_COST,
    )(tokens, out_grad, expert_ids.T, gates.T)


def finish_kernel(experts, *refs):
    kept, given, fore, rear, ids, came, *refs = refs
    earlier, (token_out, gate_out), sums = refs[:3], refs[3:5], refs[5:8]
    rounded, sent = refs[8:]
    hidden_width, half = earlier[0].shape

    def store(which, cols, total):
        rounded[which, cols, :] = total.astype(BF16)
        pltpu.make_async_copy(
            rounded.at[which, cols, :], sums[which].at[cols, :], sent.at[which]
        ).start()

    add_products([slot_block(came, half, hidden_width)], earlier, store, hidden_width)
    rows, width = token_out.shape
    total = kept[...].astype(F32) + given[...].astype(F32) + fore[...].astype(F32)
    total += rear[...].astype(F32)
    token_out[...] = total[:, :width].astype(BF16)
    table = jnp.transpose(total[:, width:])
    chosen = ids[...]
    grad = jnp.zeros(chosen.shape, F32)
    for expert in range(experts):
        grad += jnp.where(chosen == expert, table[expert : expert + 1, :rows], 0.0)
    gate_out[...] = grad.astype(BF16)
    for which in range(3):
        pltpu.make_async_copy(rounded.at[which], sums[which], sent.at[which]).wait()


def finished(experts, kept, given, fore, rear, expert_ids, came, sums):
    rows, top_count = expert_ids.shape
    hidden_width, half = sums[0].shape
    token_grad, gate_grad, *sums = pl.pallas_call(
        functools.partial(finish_kernel, experts),
        out_shape=[
            jax.ShapeDtypeStruct((rows, kept.shape[1] - LANES), BF16),
            jax.ShapeDtypeStruct((top_count, rows), BF16),
        ]
        + [jax.ShapeDtypeStruct((hidden_width, half), BF16)] * 3,
        in_specs=[IN_VMEM] * 9,
        out_specs=[IN_VMEM] * 2 + [WHEREVER] * 3,
        scratch_shapes=[
            pltpu.VMEM((3, hidden_width, half), BF16),
            pltpu.SemaphoreType.DMA((3,)),
        ],
        compiler_params=pltpu.CompilerParams(vmem_limit_bytes=KERNEL_VMEM),
        cost_estimate=NO_COST,
    )(kept, given, fore, rear, expert_ids.T, came, *sums)
    return token_grad, gate_grad.T, sums


def chip_ring(expert_count):
    depth = expert_count // 4
    return [2 * z for z in range(depth)] + [2 * z + 1 for z in reversed(range(depth))]


def ring_shift(expert_count, by):
    order = chip_ring(expert_count)
    total = len(order)
    return sorted(
        (2 * chip + core, 2 * order[(place + by) % total] + core)
        for place, chip in enumerate(order)
        for core in range(2)
    )


def on_ring(tokens, out_grad, expert_ids, gates, w_gate, w_up, w_down):
    rows, width = tokens.shape
    top_count = expert_ids.shape[1]
    experts = lax.axis_size("expert")
    half = width // lax.axis_size("dp")
    capacity = min(rows, rows * top_count * 6 // (5 * experts))
    sizes = (rows, capacity, top_count, half)
    forth, back = ring_shift(experts, 1), ring_shift(experts, -1)
    weights = (w_gate[0].T, w_up[0].T, w_down[0])
    stage = lax.optimization_barrier

    def go(value, pairs):
        return lax.ppermute(value, "expert", pairs)

    def sibling(value):
        return lax.ppermute(value, "expert", [(i, i ^ 1) for i in range(experts)])

    def across(value):
        return lax.ppermute(value, "dp", [(0, 1), (1, 0)])

    def with_siblings(parts):
        return parts + [tuple(sibling(array) for array in part) for part in parts]

    def expert(parts, sums=None, packs=(), **options):
        return expert_rows(parts, weights, sizes, sums, packs, **options)

    def passed_on(item, fore, rear):
        total = item[0].astype(F32) + item[1].astype(F32)
        fore = go((total[rows:] + fore.astype(F32)).astype(BF16), forth)
        rear = go((total[:rows] + rear.astype(F32)).astype(BF16), back)
        return fore, rear

    own = packed_rows(tokens, out_grad, expert_ids, gates)
    fore, rear, over0 = go(own, forth), go(own, back), across(own)
    parts0 = with_siblings([(own,)])
    near0, _, grads0 = expert(parts0, adds=False)
    fore, rear, over0, near0, block0 = stage((fore, rear, over0, near0, (parts0, grads0)))

    parts = with_siblings([(fore,), (rear,)])
    over1 = across(jnp.concatenate([fore, rear], axis=0))
    fore, rear = go(fore, forth), go(rear, back)
    near1, _, sums = expert(parts, waiting=[block0])
    fore, rear, near1, sums = stage((fore, rear, near1, sums))

    parts = with_siblings([(fore,), (rear,)])
    over2 = across(jnp.pad(fore, ((0, 0), (0, LANES))))
    fore, rear = go(fore, forth), go(rear, back)
    near2, slots2, sums = expert(parts, sums, [(1, 3)])
    fore, rear, over1, near2, slots2, sums = stage((fore, rear, over1, near2, slots2, sums))

    parts3 = with_siblings([(fore,), (rear,)])
    far_x, far_rest = go(fore[:, :width], forth), go(rear[:, width:], back)
    came2 = across(slots2[0])
    near3, _, grads3 = expert(parts3, adds=False)
    far_x, far_rest, over2, near3, block3 = stage(
        (far_x, far_rest, over2, near3, (parts3, grads3))
    )

    parts4 = with_siblings([(far_x, far_rest)])
    near3[1], near2[1] = sibling(near3[1]), sibling(near2[1])
    slots3 = slot_rows(*block3, sizes, width, [(0, 1, 2), (3,)])
    near4, _, grads4 = expert(parts4, after=slots3, adds=False)
    near2, near3, near4, slots3, block4, came2 = stage(
        (near2, near3, near4, slots3, (parts4, grads4), came2)
    )
    came3 = across(slots3[0])
    near4[1] = sibling(near4[1])
    sum4 = (near4[0].astype(F32) + near4[1].astype(F32)).astype(BF16)
    cut = width // 2
    fore, rear = go(sum4[:, :cut], forth), go(sum4[:, cut:], back)
    fore, rear, near1, over0, over2 = stage((fore, rear, near1, over0, over2))
    fore = jnp.pad(fore, ((0, 0), (0, width + LANES - cut)))
    rear = jnp.pad(rear, ((0, 0), (cut, 0)))

    fore, rear = passed_on(near3, fore, rear)
    over = with_siblings([(over0,), (over2,)])
    sums = add_rows([came2], sums, width, [block3, block4])
    slots4 = slot_rows(*block4, sizes, width, [(0, 1)], slots3[1])
    fore, rear, near1, over1, over, came3, sums, slots4 = stage(
        (fore, rear, near1, over1, over, came3, sums, slots4)
    )

    came4 = across(slots4[0])
    fore, rear = passed_on(near2, fore, rear)
    near1[1] = sibling(near1[1])
    over1 = with_siblings([(over1,)])
    sums = expert(over, sums, routed=False)[2]
    fore, rear, near0, near1, over1, sums = stage((fore, rear, near0, near1, over1, sums))

    fore, rear = passed_on(near1, fore, rear)
    near0[1] = sibling(near0[1])
    sums = expert(over1, sums, came=[came3], routed=False)[2]
    fore, rear, near0, came4, sums = stage((fore, rear, near0, came4, sums))

    token_grad, gate_grad, sums = finished(experts, *near0, fore, rear, expert_ids, came4, sums)
    return (token_grad, gate_grad, sums[0].T[None], sums[1].T[None], sums[2][None])


def solution(mesh):
    in_specs = (
        P(("dp", "expert"), None),
        P(("dp", "expert"), None),
        P(("dp", "expert"), None),
        P(("dp", "expert"), None),
        P("expert", None, None),
        P("expert", None, None),
        P("expert", None, None),
    )
    out_specs = (
        P(("dp", "expert"), None),
        P(("dp", "expert"), None),
        P("expert", "dp", None),
        P("expert", "dp", None),
        P("expert", None, "dp"),
    )
    on_slice = on_ring if (mesh.shape["dp"], mesh.shape["expert"]) == (2, 16) else on_device
    return jax.shard_map(
        on_slice, mesh=mesh, in_specs=in_specs, out_specs=out_specs, check_vma=False
    )
```

```python
import functools

import jax
import jax.numpy as jnp
from jax import lax
from jax.experimental import pallas as pl
from jax.experimental.pallas import tpu as pltpu
from jax.sharding import PartitionSpec as P


def slot_places(expert_ids, experts, capacity):
    flat_ids = expert_ids.reshape(-1)
    labels = jnp.arange(experts, dtype=jnp.int32)
    onehot = (flat_ids[:, None] == labels[None, :]).astype(jnp.int32)
    earlier = jnp.cumsum(onehot, axis=0) - onehot
    slot_index = jnp.sum(earlier * onehot, axis=1)
    return flat_ids * capacity + slot_index


def slot_sources(places, slot_total):
    route_total = places.shape[0]
    filler = (
        jnp.zeros((slot_total,), jnp.int32)
        .at[places]
        .set(jnp.arange(route_total, dtype=jnp.int32) + 1)
    )
    return (jnp.maximum(filler - 1, 0), filler > 0)


def fill_slots(values, source, filled):
    taken = values[source]
    keep_mask = filled.reshape(filled.shape + (1,) * (taken.ndim - 1))
    return jnp.where(keep_mask, taken, jnp.zeros_like(taken))


def expert_pass(x_rows, dy_rows, g_rows, gate_w, up_w, down_w):
    pre_gate = jnp.dot(x_rows, gate_w, preferred_element_type=jnp.float32)
    pre_up = jnp.dot(x_rows, up_w, preferred_element_type=jnp.float32)
    sigmoid_gate = jax.nn.sigmoid(pre_gate)
    activated = pre_gate * sigmoid_gate
    hidden = (activated * pre_up).astype(jnp.bfloat16)
    expert_out = jnp.dot(hidden, down_w, preferred_element_type=jnp.float32)
    gate_grad = jnp.sum(dy_rows.astype(jnp.float32) * expert_out, axis=-1).astype(jnp.bfloat16)
    scaled = (g_rows.astype(jnp.float32)[:, None] * dy_rows.astype(jnp.float32)).astype(
        jnp.bfloat16
    )
    hidden_grad = lax.dot_general(
        scaled, down_w, (((1,), (1,)), ((), ())), preferred_element_type=jnp.float32
    )
    pre_gate_grad = (
        hidden_grad * pre_up * sigmoid_gate * (1.0 + pre_gate * (1.0 - sigmoid_gate))
    ).astype(jnp.bfloat16)
    pre_up_grad = (hidden_grad * activated).astype(jnp.bfloat16)
    route_grad = lax.dot_general(
        pre_gate_grad, gate_w, (((1,), (1,)), ((), ())), preferred_element_type=jnp.float32
    )
    route_grad = route_grad + lax.dot_general(
        pre_up_grad, up_w, (((1,), (1,)), ((), ())), preferred_element_type=jnp.float32
    )
    return (route_grad.astype(jnp.bfloat16), gate_grad, pre_gate_grad, pre_up_grad, hidden, scaled)


def on_device(tokens, out_grad, expert_ids, gates, w_gate, w_up, w_down):
    tok_rows, model_width = tokens.shape
    top_count = expert_ids.shape[1]
    peer_count = lax.axis_size("expert")
    capacity = min(tok_rows, tok_rows * top_count * 6 // (5 * peer_count))
    slot_total = peer_count * capacity
    places = slot_places(expert_ids, peer_count, capacity)
    source, filled = slot_sources(places, slot_total)
    token_source = source // top_count
    x_buf = fill_slots(tokens, token_source, filled).reshape(peer_count, capacity, model_width)
    dy_buf = fill_slots(out_grad, token_source, filled).reshape(peer_count, capacity, model_width)
    g_buf = fill_slots(gates.reshape(-1), source, filled).reshape(peer_count, capacity)
    gate_w = w_gate[0]
    up_w = w_up[0]
    down_w = w_down[0]
    hidden_width = gate_w.shape[1]
    x_in, dy_in, g_in = (
        lax.all_to_all(x_buf, "expert", split_axis=0, concat_axis=0, tiled=True),
        lax.all_to_all(dy_buf, "expert", split_axis=0, concat_axis=0, tiled=True),
        lax.all_to_all(g_buf, "expert", split_axis=0, concat_axis=0, tiled=True),
    )
    lead_dim = x_in.shape[0]
    item_total = x_in.shape[1]
    results = expert_pass(
        x_in.reshape(lead_dim * item_total, model_width),
        dy_in.reshape(lead_dim * item_total, model_width),
        g_in.reshape(lead_dim * item_total),
        gate_w,
        up_w,
        down_w,
    )
    route_grad, gate_grad, pre_gate_grad, pre_up_grad, hidden, scaled = tuple(
        (piece.reshape((lead_dim, item_total) + piece.shape[1:]) for piece in results)
    )
    back_dx, back_dg = (
        lax.all_to_all(route_grad, "expert", split_axis=0, concat_axis=0, tiled=True),
        lax.all_to_all(gate_grad, "expert", split_axis=0, concat_axis=0, tiled=True),
    )
    routed = back_dx.reshape(slot_total, model_width)[places]
    token_grad = jnp.sum(
        routed.reshape(tok_rows, top_count, model_width).astype(jnp.float32), axis=1
    ).astype(jnp.bfloat16)
    gate_grad_out = back_dg.reshape(slot_total)[places].reshape(tok_rows, top_count)
    x_rows = x_in.reshape(slot_total, model_width)
    scaled_rows = scaled.reshape(slot_total, model_width)
    gate_rows = pre_gate_grad.reshape(slot_total, hidden_width)
    up_rows = pre_up_grad.reshape(slot_total, hidden_width)
    hidden_rows = hidden.reshape(slot_total, hidden_width)
    contract = (((0,), (0,)), ((), ()))
    part_gate = lax.dot_general(x_rows, gate_rows, contract, preferred_element_type=jnp.float32)
    part_up = lax.dot_general(x_rows, up_rows, contract, preferred_element_type=jnp.float32)
    part_down = lax.dot_general(
        hidden_rows, scaled_rows, contract, preferred_element_type=jnp.float32
    )
    sum_gate, sum_up, sum_down = (
        lax.psum_scatter(
            part_gate.astype(jnp.bfloat16), "dp", scatter_dimension=0, tiled=True
        ).astype(jnp.float32),
        lax.psum_scatter(
            part_up.astype(jnp.bfloat16), "dp", scatter_dimension=0, tiled=True
        ).astype(jnp.float32),
        lax.psum_scatter(
            part_down.astype(jnp.bfloat16), "dp", scatter_dimension=1, tiled=True
        ).astype(jnp.float32),
    )
    return (
        token_grad,
        gate_grad_out,
        sum_gate.astype(jnp.bfloat16)[None],
        sum_up.astype(jnp.bfloat16)[None],
        sum_down.astype(jnp.bfloat16)[None],
    )


F32, BF16 = jnp.float32, jnp.bfloat16
ROWS_BY_ROWS = (((1,), (1,)), ((), ()))
OVER_ROWS = (((0,), (0,)), ((), ()))
LANES = 128
KERNEL_VMEM = 16 * 2**20
ALL_VMEM = 60 * 2**20
IN_VMEM = pl.BlockSpec(memory_space=pltpu.VMEM)
WHEREVER = pl.BlockSpec(memory_space=pl.ANY)
NO_COST = pl.CostEstimate(flops=0, bytes_accessed=0, transcendentals=0)


def tiles(total, step):
    return [slice(at, min(at + step, total)) for at in range(0, total, step)]


def used_rows(part):
    return part[0].shape[0] - part[0].shape[0] % 16


def take_parts(refs, layout):
    return [tuple(refs.pop(0) for _ in range(count)) for count in layout]


def stacked(parts, width, start, size):
    in_rest, at = start

    def read(part):
        rows = slice(0, used_rows(part))
        if len(part) == 2:
            return part[in_rest][rows, pl.ds(at, size)]
        return part[0][rows, pl.ds(at + width if in_rest else at, size)]

    return jnp.concatenate([read(part) for part in parts], axis=0)


def add_products(blocks, earlier, store, hidden_width):
    for which in range(3):
        for cols in tiles(hidden_width, 256):
            total = earlier[which][cols, :] if earlier else 0.0
            for block in blocks:
                left, right = block(which, cols)
                total += lax.dot_general(left, right, OVER_ROWS, preferred_element_type=F32)
            store(which, cols, total)


def dense_block(parts, grads, start, half, width):
    def block(which, cols):
        return grads[which][:, cols], stacked(parts, width, (which == 2, start), half)

    return block


def slot_block(ref, half, hidden_width):
    def block(which, cols):
        at = 2 * half + which * hidden_width
        first = half if which == 2 else 0
        return ref[:, at + cols.start : at + cols.stop], ref[:, first : first + half]

    return block


def choices(routing, top_count, of_sibling=False):
    lane = lax.broadcasted_iota(jnp.int32, routing.shape, 1)
    expert = lax.axis_index("expert")
    expert = expert + 1 - 2 * (expert % 2) if of_sibling else expert
    chosen = (routing == expert.astype(F32)) & (lane < top_count)
    shifted = pltpu.roll(routing, LANES - top_count, 1)
    gate = jnp.sum(jnp.where(chosen, shifted, 0.0), axis=1, keepdims=True)
    taken = jnp.sum(jnp.where(chosen, 1.0, 0.0), axis=1, keepdims=True)
    return gate, taken


def write_slots(outs, packs, carried, parts, grads, taken, sizes, width):
    tok_rows, slots, _, half = sizes
    total_rows, hidden_width = grads[0].shape
    shape = (total_rows, LANES)
    row = lax.broadcasted_iota(jnp.int32, (total_rows, total_rows), 0)
    other = lax.broadcasted_iota(jnp.int32, (total_rows, total_rows), 1)
    before = (other < row) & (other >= row - row % tok_rows)
    taken_lanes = jnp.broadcast_to(taken, shape).astype(BF16)
    count = jnp.dot(before.astype(BF16), taken_lanes, preferred_element_type=F32)
    part_of = lax.broadcasted_iota(jnp.int32, shape, 0) // tok_rows
    first = jnp.full(shape, LANES, jnp.int32)
    for order, part in enumerate(part for pack in packs for part in pack):
        first = jnp.where(part_of == part, order * slots, first)
    place = jnp.where(taken > 0.0, count.astype(jnp.int32) + first, LANES)
    picks = (place == lax.broadcasted_iota(jnp.int32, shape, 1)).astype(BF16)
    away = pl.multiple_of((1 - lax.axis_index("dp")) * half, half)

    def fill(values, at):
        rows = lax.dot_general(picks, values, OVER_ROWS, preferred_element_type=F32)
        columns = slice(at, at + rows.shape[1])
        first = 0
        for order, (out, pack) in enumerate(zip(outs, packs)):
            count = len(pack) * slots
            block = rows[first : first + count]
            if order == 0 and carried is not None:
                block = jnp.concatenate([carried[:, columns].astype(F32), block], axis=0)
            out[:, columns] = block.astype(BF16)
            first += count

    fill(stacked(parts, width, (0, away), half), 0)
    fill(stacked(parts, width, (1, away), half), half)
    for which in range(3):
        fill(grads[which][...], 2 * half + which * hidden_width)


def chosen_kernel(sizes, width, fore, rear, out):
    tok_rows, slots, top_count, _ = sizes
    parts = [(fore,), (rear,)]
    routing = stacked(parts, width, (1, width), LANES).astype(F32)
    shape = routing.shape
    here, beside = choices(routing, top_count)[1], choices(routing, top_count, True)[1]
    taken = jnp.maximum(here, beside)
    row = lax.broadcasted_iota(jnp.int32, (shape[0], shape[0]), 0)
    other = lax.broadcasted_iota(jnp.int32, (shape[0], shape[0]), 1)
    before = (other < row) & (other >= row - row % tok_rows)
    taken_lanes = jnp.broadcast_to(taken, shape).astype(BF16)
    count = jnp.dot(before.astype(BF16), taken_lanes, preferred_element_type=F32)
    first = lax.broadcasted_iota(jnp.int32, shape, 0) // tok_rows * (2 * slots)
    place = jnp.where(taken > 0.0, count.astype(jnp.int32) + first, LANES)
    picks = (place == lax.broadcasted_iota(jnp.int32, shape, 1)).astype(BF16)
    for cols in tiles(out.shape[1], 1024):
        values = jnp.concatenate([fore[:, cols], rear[:, cols]], axis=0)
        rows = lax.dot_general(picks, values, OVER_ROWS, preferred_element_type=F32)
        out[:, cols] = rows[: out.shape[0]].astype(BF16)


def chosen_rows(fore, rear, sizes, width):
    shape = (4 * sizes[1], fore.shape[1])
    return pl.pallas_call(
        functools.partial(chosen_kernel, sizes, width),
        out_shape=jax.ShapeDtypeStruct(shape, BF16),
        in_specs=[IN_VMEM] * 2,
        out_specs=IN_VMEM,
        compiler_params=pltpu.CompilerParams(vmem_limit_bytes=KERNEL_VMEM),
        cost_estimate=NO_COST,
    )(fore, rear)


def slots_kernel(layout, packs, has_carried, sizes, width, *refs):
    refs = list(refs)
    parts = take_parts(refs, layout)
    grads, refs = refs[:3], refs[3:]
    carried = refs.pop(0) if has_carried else None
    routing = stacked(parts, width, (1, width), LANES).astype(F32)
    _, taken = choices(routing, sizes[2])
    write_slots(refs, packs, carried, parts, grads, taken, sizes, width)


def slot_rows(parts, grads, sizes, width, packs, carried=None):
    _, slots, _, half = sizes
    operands = [*flat(parts), *grads] + ([carried] if carried is not None else [])
    shapes = []
    for order, pack in enumerate(packs):
        count = slots * len(pack)
        if order == 0 and carried is not None:
            count += carried.shape[0]
        shapes.append((count, 2 * half + 3 * grads[0].shape[1]))
    return list(
        pl.pallas_call(
            functools.partial(
                slots_kernel,
                [len(part) for part in parts],
                packs,
                carried is not None,
                sizes,
                width,
            ),
            out_shape=[jax.ShapeDtypeStruct(shape, BF16) for shape in shapes],
            in_specs=[IN_VMEM] * len(operands),
            out_specs=[IN_VMEM] * len(shapes),
            compiler_params=pltpu.CompilerParams(vmem_limit_bytes=KERNEL_VMEM),
            cost_estimate=NO_COST,
        )(*operands)
    )


def rows_kernel(layout, packs, waiting, slot_total, after, has_sums, adds, routed, sizes, *refs):
    refs = list(refs)
    _, _, top_count, half = sizes

    def take(count):
        taken = refs[:count]
        del refs[:count]
        return taken

    parts, (gate_w, up_w, down_w) = take_parts(refs, layout), take(3)
    dense = [(take_parts(refs, parts_layout), take(3)) for parts_layout in waiting]
    came = take(slot_total)
    take(after)
    earlier = take(3) if has_sums else None
    kept_out, given_out = take(2) if routed else (None, None)
    slots_outs = take(len(packs))
    sums = take(3) if adds else None
    grads = take(3)
    pre_gate_out, pre_up_out, hidden_out = grads
    hidden_width, width = gate_w.shape
    x = stacked(parts, width, (0, 0), width)
    dy = stacked(parts, width, (1, 0), width)
    routing = stacked(parts, width, (1, width), LANES).astype(F32)
    gate, taken = choices(routing, top_count)
    gate_grad = jnp.zeros_like(gate)
    for cols in tiles(hidden_width, 256):
        pre_gate = lax.dot_general(x, gate_w[cols, :], ROWS_BY_ROWS, preferred_element_type=F32)
        pre_up = lax.dot_general(x, up_w[cols, :], ROWS_BY_ROWS, preferred_element_type=F32)
        down_grad = lax.dot_general(dy, down_w[cols, :], ROWS_BY_ROWS, preferred_element_type=F32)
        sigmoid_gate = jax.nn.sigmoid(pre_gate)
        activated = pre_gate * sigmoid_gate
        hidden = activated * pre_up
        gate_grad += jnp.sum(hidden * down_grad, axis=1, keepdims=True)
        hidden_grad = gate * down_grad
        slope = sigmoid_gate * (1.0 + pre_gate * (1.0 - sigmoid_gate))
        pre_gate_out[:, cols] = (hidden_grad * pre_up * slope).astype(BF16)
        pre_up_out[:, cols] = (hidden_grad * activated).astype(BF16)
        hidden_out[:, cols] = (gate * hidden).astype(BF16)
    if routed:
        half_rows = routing.shape[0] // 2
        lane = lax.broadcasted_iota(jnp.int32, routing.shape, 1)
        table = jnp.where(lane == lax.axis_index("expert"), gate_grad * taken, 0.0).astype(BF16)
        kept_out[:, width:] = table[:half_rows]
        given_out[:, width:] = table[half_rows:]
        for cols in tiles(width, 512):
            route = jnp.dot(pre_gate_out[...], gate_w[:, cols], preferred_element_type=F32)
            route += jnp.dot(pre_up_out[...], up_w[:, cols], preferred_element_type=F32)
            route = route.astype(BF16)
            kept_out[:, cols] = route[:half_rows]
            given_out[:, cols] = route[half_rows:]

    if packs:
        write_slots(slots_outs, packs, None, parts, grads, taken, sizes, width)
    if adds:
        start = pl.multiple_of(lax.axis_index("dp") * half, half)
        blocks = [dense_block(*block, start, half, width) for block in [(parts, grads), *dense]]
        blocks += [slot_block(ref, half, hidden_width) for ref in came]

        def store(which, cols, total):
            sums[which][cols, :] = total

        add_products(blocks, earlier, store, hidden_width)


def flat(parts):
    return [array for part in parts for array in part]


def expert_rows(
    parts, weights, sizes, sums=None, packs=(), waiting=(), came=(), after=(), adds=True, routed=True
):
    _, slots, _, half = sizes
    total = sum(used_rows(part) for part in parts)
    hidden_width, width = weights[0].shape
    operands = [*flat(parts), *weights]
    for block_parts, block_grads in waiting:
        operands += [*flat(block_parts), *block_grads]
    operands += [*came, *after, *(sums or ())]
    wide = jax.ShapeDtypeStruct((total // 2, width + LANES), BF16)
    grad = jax.ShapeDtypeStruct((total, hidden_width), BF16)
    added = jax.ShapeDtypeStruct((hidden_width, half), F32)
    results = [wide] * (2 * routed)
    for pack in packs:
        shape = (slots * len(pack), 2 * half + 3 * hidden_width)
        results.append(jax.ShapeDtypeStruct(shape, BF16))
    first = len(results)
    results += [added] * 3 if adds else [grad] * 3
    first_sum = len(operands) - 3
    results = pl.pallas_call(
        functools.partial(
            rows_kernel,
            [len(part) for part in parts],
            packs,
            [[len(part) for part in block_parts] for block_parts, _ in waiting],
            len(came),
            len(after),
            sums is not None,
            adds,
            routed,
            sizes,
        ),
        out_shape=results,
        in_specs=[WHEREVER if any(o is a for a in after) else IN_VMEM for o in operands],
        out_specs=[IN_VMEM] * len(results),
        input_output_aliases={first_sum + i: first + i for i in range(3)} if sums else {},
        scratch_shapes=[pltpu.VMEM(grad.shape, BF16)] * (3 * adds),
        compiler_params=pltpu.CompilerParams(vmem_limit_bytes=KERNEL_VMEM),
        cost_estimate=NO_COST,
    )(*operands)
    return list(results[: 2 * routed]), list(results[2 * routed : first]), list(results[first:])


def sums_kernel(waiting, slot_total, half, width, *refs):
    refs = list(refs)

    def take(count):
        taken = refs[:count]
        del refs[:count]
        return taken

    dense = [(take_parts(refs, layout), take(3)) for layout in waiting]
    came, earlier, outs = take(slot_total), take(3), take(3)
    hidden_width = earlier[0].shape[0]
    start = pl.multiple_of(lax.axis_index("dp") * half, half)
    blocks = [dense_block(*block, start, half, width) for block in dense]
    blocks += [slot_block(ref, half, hidden_width) for ref in came]

    def store(which, cols, total):
        outs[which][cols, :] = total

    add_products(blocks, earlier, store, hidden_width)


def add_rows(came, sums, width, waiting=()):
    hidden_width, half = sums[0].shape
    operands = []
    for block_parts, block_grads in waiting:
        operands += [*flat(block_parts), *block_grads]
    operands += [*came, *sums]
    added = jax.ShapeDtypeStruct((hidden_width, half), F32)
    first_sum = len(operands) - 3
    return list(
        pl.pallas_call(
            functools.partial(
                sums_kernel,
                [[len(part) for part in block_parts] for block_parts, _ in waiting],
                len(came),
                half,
                width,
            ),
            out_shape=[added] * 3,
            in_specs=[IN_VMEM] * len(operands),
            out_specs=[IN_VMEM] * 3,
            input_output_aliases={first_sum + i: i for i in range(3)},
            compiler_params=pltpu.CompilerParams(vmem_limit_bytes=KERNEL_VMEM),
            cost_estimate=NO_COST,
        )(*operands)
    )


def pack_kernel(tokens, out_grad, ids, gates, out, ids_held, sent):
    width = tokens.shape[1]
    top_count = ids.shape[0]
    copies = [
        pltpu.make_async_copy(ids, ids_held, sent.at[0]),
        pltpu.make_async_copy(tokens, out.at[:, pl.ds(0, width)], sent.at[1]),
        pltpu.make_async_copy(out_grad, out.at[:, pl.ds(width, width)], sent.at[2]),
    ]
    for copy in copies:
        copy.start()
    row = lax.broadcasted_iota(jnp.int32, (top_count, LANES), 0)
    lane = lax.broadcasted_iota(jnp.int32, (top_count, LANES), 1)
    copies[0].wait()
    routing = 0.0
    for values, at in ((ids_held[...].astype(F32).astype(BF16), 0), (gates[...], top_count)):
        spread = (lane == row + at).astype(BF16)
        routing += lax.dot_general(values, spread, OVER_ROWS, preferred_element_type=F32)
    out[:, 2 * width :] = routing.astype(BF16)
    copies[1].wait()
    copies[2].wait()


def packed_rows(tokens, out_grad, expert_ids, gates):
    rows, width = tokens.shape
    top_count = expert_ids.shape[1]
    return pl.pallas_call(
        pack_kernel,
        out_shape=jax.ShapeDtypeStruct((rows, 2 * width + LANES), BF16),
        in_specs=[WHEREVER] * 3 + [IN_VMEM],
        out_specs=IN_VMEM,
        scratch_shapes=[
            pltpu.VMEM((top_count, rows), jnp.int32),
            pltpu.SemaphoreType.DMA((3,)),
        ],
        compiler_params=pltpu.CompilerParams(vmem_limit_bytes=ALL_VMEM),
        cost_estimate=NO_COST,
    )(tokens, out_grad, expert_ids.T, gates.T)


def finish_kernel(experts, *refs):
    kept, given, fore, rear, ids, came, *refs = refs
    earlier, (token_out, gate_out), sums = refs[:3], refs[3:5], refs[5:8]
    rounded, sent = refs[8:]
    hidden_width, half = earlier[0].shape

    def store(which, cols, total):
        rounded[which, cols, :] = total.astype(BF16)
        pltpu.make_async_copy(
            rounded.at[which, cols, :], sums[which].at[cols, :], sent.at[which]
        ).start()

    add_products([slot_block(came, half, hidden_width)], earlier, store, hidden_width)
    rows, width = token_out.shape
    total = kept[...].astype(F32) + given[...].astype(F32) + fore[...].astype(F32)
    total += rear[...].astype(F32)
    token_out[...] = total[:, :width].astype(BF16)
    table = jnp.transpose(total[:, width:])
    chosen = ids[...]
    grad = jnp.zeros(chosen.shape, F32)
    for expert in range(experts):
        grad += jnp.where(chosen == expert, table[expert : expert + 1, :rows], 0.0)
    gate_out[...] = grad.astype(BF16)
    for which in range(3):
        pltpu.make_async_copy(rounded.at[which], sums[which], sent.at[which]).wait()


def finished(experts, kept, given, fore, rear, expert_ids, came, sums):
    rows, top_count = expert_ids.shape
    hidden_width, half = sums[0].shape
    token_grad, gate_grad, *sums = pl.pallas_call(
        functools.partial(finish_kernel, experts),
        out_shape=[
            jax.ShapeDtypeStruct((rows, kept.shape[1] - LANES), BF16),
            jax.ShapeDtypeStruct((top_count, rows), BF16),
        ]
        + [jax.ShapeDtypeStruct((hidden_width, half), BF16)] * 3,
        in_specs=[IN_VMEM] * 9,
        out_specs=[IN_VMEM] * 2 + [WHEREVER] * 3,
        scratch_shapes=[
            pltpu.VMEM((3, hidden_width, half), BF16),
            pltpu.SemaphoreType.DMA((3,)),
        ],
        compiler_params=pltpu.CompilerParams(vmem_limit_bytes=KERNEL_VMEM),
        cost_estimate=NO_COST,
    )(kept, given, fore, rear, expert_ids.T, came, *sums)
    return token_grad, gate_grad.T, sums


def chip_ring(expert_count):
    depth = expert_count // 4
    return [2 * z for z in range(depth)] + [2 * z + 1 for z in reversed(range(depth))]


def ring_shift(expert_count, by):
    order = chip_ring(expert_count)
    total = len(order)
    return sorted(
        (2 * chip + core, 2 * order[(place + by) % total] + core)
        for place, chip in enumerate(order)
        for core in range(2)
    )


def on_ring(tokens, out_grad, expert_ids, gates, w_gate, w_up, w_down):
    rows, width = tokens.shape
    top_count = expert_ids.shape[1]
    experts = lax.axis_size("expert")
    half = width // lax.axis_size("dp")
    capacity = min(rows, rows * top_count * 6 // (5 * experts))
    sizes = (rows, capacity, top_count, half)
    forth, back = ring_shift(experts, 1), ring_shift(experts, -1)
    weights = (w_gate[0].T, w_up[0].T, w_down[0])
    stage = lax.optimization_barrier

    def go(value, pairs):
        return lax.ppermute(value, "expert", pairs)

    def sibling(value):
        return lax.ppermute(value, "expert", [(i, i ^ 1) for i in range(experts)])

    def across(value):
        return lax.ppermute(value, "dp", [(0, 1), (1, 0)])

    def with_siblings(parts):
        return parts + [tuple(sibling(array) for array in part) for part in parts]

    def expert(parts, sums=None, packs=(), **options):
        return expert_rows(parts, weights, sizes, sums, packs, **options)

    def passed_on(item, fore, rear):
        total = item[0].astype(F32) + item[1].astype(F32)
        fore = go((total[rows:] + fore.astype(F32)).astype(BF16), forth)
        rear = go((total[:rows] + rear.astype(F32)).astype(BF16), back)
        return fore, rear

    own = packed_rows(tokens, out_grad, expert_ids, gates)
    fore, rear, over0 = go(own, forth), go(own, back), across(own)
    parts0 = with_siblings([(own,)])
    near0, _, grads0 = expert(parts0, adds=False)
    fore, rear, over0, near0, block0 = stage((fore, rear, over0, near0, (parts0, grads0)))

    parts = with_siblings([(fore,), (rear,)])
    over1 = across(chosen_rows(fore, rear, sizes, width))
    fore, rear = go(fore, forth), go(rear, back)
    near1, _, sums = expert(parts, waiting=[block0])
    fore, rear, near1, sums = stage((fore, rear, near1, sums))

    parts = with_siblings([(fore,), (rear,)])
    over2 = across(jnp.pad(fore, ((0, 0), (0, LANES))))
    fore, rear = go(fore, forth), go(rear, back)
    near2, slots2, sums = expert(parts, sums, [(1, 3)])
    fore, rear, over1, near2, slots2, sums = stage((fore, rear, over1, near2, slots2, sums))

    parts3 = with_siblings([(fore,), (rear,)])
    far_x, far_rest = go(fore[:, :width], forth), go(rear[:, width:], back)
    came2 = across(slots2[0])
    near3, _, grads3 = expert(parts3, adds=False)
    far_x, far_rest, over2, near3, block3 = stage(
        (far_x, far_rest, over2, near3, (parts3, grads3))
    )

    parts4 = with_siblings([(far_x, far_rest)])
    near3[1], near2[1] = sibling(near3[1]), sibling(near2[1])
    slots3 = slot_rows(*block3, sizes, width, [(0, 1, 2), (3,)])
    near4, _, grads4 = expert(parts4, after=slots3, adds=False)
    near2, near3, near4, slots3, block4, came2 = stage(
        (near2, near3, near4, slots3, (parts4, grads4), came2)
    )
    came3 = across(slots3[0])
    near4[1] = sibling(near4[1])
    sum4 = (near4[0].astype(F32) + near4[1].astype(F32)).astype(BF16)
    cut = width // 2
    fore, rear = go(sum4[:, :cut], forth), go(sum4[:, cut:], back)
    fore, rear, near1, over0, over2 = stage((fore, rear, near1, over0, over2))
    fore = jnp.pad(fore, ((0, 0), (0, width + LANES - cut)))
    rear = jnp.pad(rear, ((0, 0), (cut, 0)))

    fore, rear = passed_on(near3, fore, rear)
    over = with_siblings([(over0,), (over2,)])
    sums = add_rows([came2], sums, width, [block3, block4])
    slots4 = slot_rows(*block4, sizes, width, [(0, 1)], slots3[1])
    fore, rear, near1, over1, over, came3, sums, slots4 = stage(
        (fore, rear, near1, over1, over, came3, sums, slots4)
    )

    came4 = across(slots4[0])
    fore, rear = passed_on(near2, fore, rear)
    near1[1] = sibling(near1[1])
    over1 = with_siblings([(over1,)])
    sums = expert(over, sums, routed=False)[2]
    fore, rear, near0, near1, over1, sums = stage((fore, rear, near0, near1, over1, sums))

    fore, rear = passed_on(near1, fore, rear)
    near0[1] = sibling(near0[1])
    sums = expert(over1, sums, came=[came3], routed=False)[2]
    fore, rear, near0, came4, sums = stage((fore, rear, near0, came4, sums))

    token_grad, gate_grad, sums = finished(experts, *near0, fore, rear, expert_ids, came4, sums)
    return (token_grad, gate_grad, sums[0].T[None], sums[1].T[None], sums[2][None])


def solution(mesh):
    in_specs = (
        P(("dp", "expert"), None),
        P(("dp", "expert"), None),
        P(("dp", "expert"), None),
        P(("dp", "expert"), None),
        P("expert", None, None),
        P("expert", None, None),
        P("expert", None, None),
    )
    out_specs = (
        P(("dp", "expert"), None),
        P(("dp", "expert"), None),
        P("expert", "dp", None),
        P("expert", "dp", None),
        P("expert", None, "dp"),
    )
    on_slice = on_ring if (mesh.shape["dp"], mesh.shape["expert"]) == (2, 16) else on_device
    return jax.shard_map(
        on_slice, mesh=mesh, in_specs=in_specs, out_specs=out_specs, check_vma=False
    )
```

```python
import functools

import jax
import jax.numpy as jnp
from jax import lax
from jax.experimental import pallas as pl
from jax.experimental.pallas import tpu as pltpu
from jax.sharding import PartitionSpec as P


def slot_places(expert_ids, experts, capacity):
    flat_ids = expert_ids.reshape(-1)
    labels = jnp.arange(experts, dtype=jnp.int32)
    onehot = (flat_ids[:, None] == labels[None, :]).astype(jnp.int32)
    earlier = jnp.cumsum(onehot, axis=0) - onehot
    slot_index = jnp.sum(earlier * onehot, axis=1)
    return flat_ids * capacity + slot_index


def slot_sources(places, slot_total):
    route_total = places.shape[0]
    filler = (
        jnp.zeros((slot_total,), jnp.int32)
        .at[places]
        .set(jnp.arange(route_total, dtype=jnp.int32) + 1)
    )
    return (jnp.maximum(filler - 1, 0), filler > 0)


def fill_slots(values, source, filled):
    taken = values[source]
    keep_mask = filled.reshape(filled.shape + (1,) * (taken.ndim - 1))
    return jnp.where(keep_mask, taken, jnp.zeros_like(taken))


def expert_pass(x_rows, dy_rows, g_rows, gate_w, up_w, down_w):
    pre_gate = jnp.dot(x_rows, gate_w, preferred_element_type=jnp.float32)
    pre_up = jnp.dot(x_rows, up_w, preferred_element_type=jnp.float32)
    sigmoid_gate = jax.nn.sigmoid(pre_gate)
    activated = pre_gate * sigmoid_gate
    hidden = (activated * pre_up).astype(jnp.bfloat16)
    expert_out = jnp.dot(hidden, down_w, preferred_element_type=jnp.float32)
    gate_grad = jnp.sum(dy_rows.astype(jnp.float32) * expert_out, axis=-1).astype(jnp.bfloat16)
    scaled = (g_rows.astype(jnp.float32)[:, None] * dy_rows.astype(jnp.float32)).astype(
        jnp.bfloat16
    )
    hidden_grad = lax.dot_general(
        scaled, down_w, (((1,), (1,)), ((), ())), preferred_element_type=jnp.float32
    )
    pre_gate_grad = (
        hidden_grad * pre_up * sigmoid_gate * (1.0 + pre_gate * (1.0 - sigmoid_gate))
    ).astype(jnp.bfloat16)
    pre_up_grad = (hidden_grad * activated).astype(jnp.bfloat16)
    route_grad = lax.dot_general(
        pre_gate_grad, gate_w, (((1,), (1,)), ((), ())), preferred_element_type=jnp.float32
    )
    route_grad = route_grad + lax.dot_general(
        pre_up_grad, up_w, (((1,), (1,)), ((), ())), preferred_element_type=jnp.float32
    )
    return (route_grad.astype(jnp.bfloat16), gate_grad, pre_gate_grad, pre_up_grad, hidden, scaled)


def on_device(tokens, out_grad, expert_ids, gates, w_gate, w_up, w_down):
    tok_rows, model_width = tokens.shape
    top_count = expert_ids.shape[1]
    peer_count = lax.axis_size("expert")
    capacity = min(tok_rows, tok_rows * top_count * 6 // (5 * peer_count))
    slot_total = peer_count * capacity
    places = slot_places(expert_ids, peer_count, capacity)
    source, filled = slot_sources(places, slot_total)
    token_source = source // top_count
    x_buf = fill_slots(tokens, token_source, filled).reshape(peer_count, capacity, model_width)
    dy_buf = fill_slots(out_grad, token_source, filled).reshape(peer_count, capacity, model_width)
    g_buf = fill_slots(gates.reshape(-1), source, filled).reshape(peer_count, capacity)
    gate_w = w_gate[0]
    up_w = w_up[0]
    down_w = w_down[0]
    hidden_width = gate_w.shape[1]
    x_in, dy_in, g_in = (
        lax.all_to_all(x_buf, "expert", split_axis=0, concat_axis=0, tiled=True),
        lax.all_to_all(dy_buf, "expert", split_axis=0, concat_axis=0, tiled=True),
        lax.all_to_all(g_buf, "expert", split_axis=0, concat_axis=0, tiled=True),
    )
    lead_dim = x_in.shape[0]
    item_total = x_in.shape[1]
    results = expert_pass(
        x_in.reshape(lead_dim * item_total, model_width),
        dy_in.reshape(lead_dim * item_total, model_width),
        g_in.reshape(lead_dim * item_total),
        gate_w,
        up_w,
        down_w,
    )
    route_grad, gate_grad, pre_gate_grad, pre_up_grad, hidden, scaled = tuple(
        (piece.reshape((lead_dim, item_total) + piece.shape[1:]) for piece in results)
    )
    back_dx, back_dg = (
        lax.all_to_all(route_grad, "expert", split_axis=0, concat_axis=0, tiled=True),
        lax.all_to_all(gate_grad, "expert", split_axis=0, concat_axis=0, tiled=True),
    )
    routed = back_dx.reshape(slot_total, model_width)[places]
    token_grad = jnp.sum(
        routed.reshape(tok_rows, top_count, model_width).astype(jnp.float32), axis=1
    ).astype(jnp.bfloat16)
    gate_grad_out = back_dg.reshape(slot_total)[places].reshape(tok_rows, top_count)
    x_rows = x_in.reshape(slot_total, model_width)
    scaled_rows = scaled.reshape(slot_total, model_width)
    gate_rows = pre_gate_grad.reshape(slot_total, hidden_width)
    up_rows = pre_up_grad.reshape(slot_total, hidden_width)
    hidden_rows = hidden.reshape(slot_total, hidden_width)
    contract = (((0,), (0,)), ((), ()))
    part_gate = lax.dot_general(x_rows, gate_rows, contract, preferred_element_type=jnp.float32)
    part_up = lax.dot_general(x_rows, up_rows, contract, preferred_element_type=jnp.float32)
    part_down = lax.dot_general(
        hidden_rows, scaled_rows, contract, preferred_element_type=jnp.float32
    )
    sum_gate, sum_up, sum_down = (
        lax.psum_scatter(
            part_gate.astype(jnp.bfloat16), "dp", scatter_dimension=0, tiled=True
        ).astype(jnp.float32),
        lax.psum_scatter(
            part_up.astype(jnp.bfloat16), "dp", scatter_dimension=0, tiled=True
        ).astype(jnp.float32),
        lax.psum_scatter(
            part_down.astype(jnp.bfloat16), "dp", scatter_dimension=1, tiled=True
        ).astype(jnp.float32),
    )
    return (
        token_grad,
        gate_grad_out,
        sum_gate.astype(jnp.bfloat16)[None],
        sum_up.astype(jnp.bfloat16)[None],
        sum_down.astype(jnp.bfloat16)[None],
    )


F32, BF16 = jnp.float32, jnp.bfloat16
ROWS_BY_ROWS = (((1,), (1,)), ((), ()))
OVER_ROWS = (((0,), (0,)), ((), ()))
LANES = 128
KERNEL_VMEM = 16 * 2**20
ALL_VMEM = 60 * 2**20
IN_VMEM = pl.BlockSpec(memory_space=pltpu.VMEM)
WHEREVER = pl.BlockSpec(memory_space=pl.ANY)
NO_COST = pl.CostEstimate(flops=0, bytes_accessed=0, transcendentals=0)


def tiles(total, step):
    return [slice(at, min(at + step, total)) for at in range(0, total, step)]


def used_rows(part):
    return part[0].shape[0] - part[0].shape[0] % 16


def take_parts(refs, layout):
    return [tuple(refs.pop(0) for _ in range(count)) for count in layout]


def stacked(parts, width, start, size):
    in_rest, at = start

    def read(part):
        rows = slice(0, used_rows(part))
        if len(part) == 2:
            return part[in_rest][rows, pl.ds(at, size)]
        return part[0][rows, pl.ds(at + width if in_rest else at, size)]

    return jnp.concatenate([read(part) for part in parts], axis=0)


def add_products(blocks, earlier, store, hidden_width):
    for which in range(3):
        for cols in tiles(hidden_width, 256):
            total = earlier[which][cols, :] if earlier else 0.0
            for block in blocks:
                left, right = block(which, cols)
                total += lax.dot_general(left, right, OVER_ROWS, preferred_element_type=F32)
            store(which, cols, total)


def dense_block(parts, grads, start, half, width):
    def block(which, cols):
        return grads[which][:, cols], stacked(parts, width, (which == 2, start), half)

    return block


def slot_block(ref, half, hidden_width):
    def block(which, cols):
        at = 2 * half + which * hidden_width
        first = half if which == 2 else 0
        return ref[:, at + cols.start : at + cols.stop], ref[:, first : first + half]

    return block


def choices(routing, top_count, of_sibling=False):
    lane = lax.broadcasted_iota(jnp.int32, routing.shape, 1)
    expert = lax.axis_index("expert")
    expert = expert + 1 - 2 * (expert % 2) if of_sibling else expert
    chosen = (routing == expert.astype(F32)) & (lane < top_count)
    shifted = pltpu.roll(routing, LANES - top_count, 1)
    gate = jnp.sum(jnp.where(chosen, shifted, 0.0), axis=1, keepdims=True)
    taken = jnp.sum(jnp.where(chosen, 1.0, 0.0), axis=1, keepdims=True)
    return gate, taken


def write_slots(outs, packs, carried, parts, grads, taken, sizes, width):
    tok_rows, slots, _, half = sizes
    total_rows, hidden_width = grads[0].shape
    shape = (total_rows, LANES)
    row = lax.broadcasted_iota(jnp.int32, (total_rows, total_rows), 0)
    other = lax.broadcasted_iota(jnp.int32, (total_rows, total_rows), 1)
    before = (other < row) & (other >= row - row % tok_rows)
    taken_lanes = jnp.broadcast_to(taken, shape).astype(BF16)
    count = jnp.dot(before.astype(BF16), taken_lanes, preferred_element_type=F32)
    part_of = lax.broadcasted_iota(jnp.int32, shape, 0) // tok_rows
    first = jnp.full(shape, LANES, jnp.int32)
    for order, part in enumerate(part for pack in packs for part in pack):
        first = jnp.where(part_of == part, order * slots, first)
    place = jnp.where(taken > 0.0, count.astype(jnp.int32) + first, LANES)
    picks = (place == lax.broadcasted_iota(jnp.int32, shape, 1)).astype(BF16)
    away = pl.multiple_of((1 - lax.axis_index("dp")) * half, half)

    def fill(values, at):
        rows = lax.dot_general(picks, values, OVER_ROWS, preferred_element_type=F32)
        columns = slice(at, at + rows.shape[1])
        first = 0
        for order, (out, pack) in enumerate(zip(outs, packs)):
            count = len(pack) * slots
            block = rows[first : first + count]
            if order == 0 and carried is not None:
                block = jnp.concatenate([carried[:, columns].astype(F32), block], axis=0)
            out[:, columns] = block.astype(BF16)
            first += count

    fill(stacked(parts, width, (0, away), half), 0)
    fill(stacked(parts, width, (1, away), half), half)
    for which in range(3):
        fill(grads[which][...], 2 * half + which * hidden_width)


def chosen_kernel(sizes, width, fore, rear, out):
    tok_rows, slots, top_count, _ = sizes
    parts = [(fore,), (rear,)]
    routing = stacked(parts, width, (1, width), LANES).astype(F32)
    shape = routing.shape
    here, beside = choices(routing, top_count)[1], choices(routing, top_count, True)[1]
    taken = jnp.maximum(here, beside)
    row = lax.broadcasted_iota(jnp.int32, (shape[0], shape[0]), 0)
    other = lax.broadcasted_iota(jnp.int32, (shape[0], shape[0]), 1)
    before = (other < row) & (other >= row - row % tok_rows)
    taken_lanes = jnp.broadcast_to(taken, shape).astype(BF16)
    count = jnp.dot(before.astype(BF16), taken_lanes, preferred_element_type=F32)
    first = lax.broadcasted_iota(jnp.int32, shape, 0) // tok_rows * (2 * slots)
    place = jnp.where(taken > 0.0, count.astype(jnp.int32) + first, LANES)
    picks = (place == lax.broadcasted_iota(jnp.int32, shape, 1)).astype(BF16)
    for cols in tiles(out.shape[1], 1024):
        values = jnp.concatenate([fore[:, cols], rear[:, cols]], axis=0)
        rows = lax.dot_general(picks, values, OVER_ROWS, preferred_element_type=F32)
        out[:, cols] = rows[: out.shape[0]].astype(BF16)


def chosen_rows(fore, rear, sizes, width):
    shape = (4 * sizes[1], fore.shape[1])
    return pl.pallas_call(
        functools.partial(chosen_kernel, sizes, width),
        out_shape=jax.ShapeDtypeStruct(shape, BF16),
        in_specs=[IN_VMEM] * 2,
        out_specs=IN_VMEM,
        compiler_params=pltpu.CompilerParams(vmem_limit_bytes=KERNEL_VMEM),
        cost_estimate=NO_COST,
    )(fore, rear)


def slots_kernel(layout, packs, has_carried, sizes, width, *refs):
    refs = list(refs)
    parts = take_parts(refs, layout)
    grads, refs = refs[:3], refs[3:]
    carried = refs.pop(0) if has_carried else None
    routing = stacked(parts, width, (1, width), LANES).astype(F32)
    _, taken = choices(routing, sizes[2])
    write_slots(refs, packs, carried, parts, grads, taken, sizes, width)


def slot_rows(parts, grads, sizes, width, packs, carried=None):
    _, slots, _, half = sizes
    operands = [*flat(parts), *grads] + ([carried] if carried is not None else [])
    shapes = []
    for order, pack in enumerate(packs):
        count = slots * len(pack)
        if order == 0 and carried is not None:
            count += carried.shape[0]
        shapes.append((count, 2 * half + 3 * grads[0].shape[1]))
    return list(
        pl.pallas_call(
            functools.partial(
                slots_kernel,
                [len(part) for part in parts],
                packs,
                carried is not None,
                sizes,
                width,
            ),
            out_shape=[jax.ShapeDtypeStruct(shape, BF16) for shape in shapes],
            in_specs=[IN_VMEM] * len(operands),
            out_specs=[IN_VMEM] * len(shapes),
            compiler_params=pltpu.CompilerParams(vmem_limit_bytes=KERNEL_VMEM),
            cost_estimate=NO_COST,
        )(*operands)
    )


def rows_kernel(layout, packs, waiting, slot_total, after, has_sums, adds, routed, sizes, *refs):
    refs = list(refs)
    _, _, top_count, half = sizes

    def take(count):
        taken = refs[:count]
        del refs[:count]
        return taken

    parts, (gate_w, up_w, down_w) = take_parts(refs, layout), take(3)
    dense = [(take_parts(refs, parts_layout), take(3)) for parts_layout in waiting]
    came = take(slot_total)
    take(after)
    earlier = take(3) if has_sums else None
    kept_out, given_out = take(2) if routed else (None, None)
    slots_outs = take(len(packs))
    sums = take(3) if adds else None
    grads = take(3)
    pre_gate_out, pre_up_out, hidden_out = grads
    hidden_width, width = gate_w.shape
    x = stacked(parts, width, (0, 0), width)
    dy = stacked(parts, width, (1, 0), width)
    routing = stacked(parts, width, (1, width), LANES).astype(F32)
    gate, taken = choices(routing, top_count)
    gate_grad = jnp.zeros_like(gate)
    for cols in tiles(hidden_width, 256):
        pre_gate = lax.dot_general(x, gate_w[cols, :], ROWS_BY_ROWS, preferred_element_type=F32)
        pre_up = lax.dot_general(x, up_w[cols, :], ROWS_BY_ROWS, preferred_element_type=F32)
        down_grad = lax.dot_general(dy, down_w[cols, :], ROWS_BY_ROWS, preferred_element_type=F32)
        sigmoid_gate = jax.nn.sigmoid(pre_gate)
        activated = pre_gate * sigmoid_gate
        hidden = activated * pre_up
        gate_grad += jnp.sum(hidden * down_grad, axis=1, keepdims=True)
        hidden_grad = gate * down_grad
        slope = sigmoid_gate * (1.0 + pre_gate * (1.0 - sigmoid_gate))
        pre_gate_out[:, cols] = (hidden_grad * pre_up * slope).astype(BF16)
        pre_up_out[:, cols] = (hidden_grad * activated).astype(BF16)
        hidden_out[:, cols] = (gate * hidden).astype(BF16)
    if routed:
        half_rows = routing.shape[0] // 2
        lane = lax.broadcasted_iota(jnp.int32, routing.shape, 1)
        table = jnp.where(lane == lax.axis_index("expert"), gate_grad * taken, 0.0).astype(BF16)
        kept_out[:, width:] = table[:half_rows]
        given_out[:, width:] = table[half_rows:]
        for cols in tiles(width, 1024):
            route = jnp.dot(pre_gate_out[...], gate_w[:, cols], preferred_element_type=F32)
            route += jnp.dot(pre_up_out[...], up_w[:, cols], preferred_element_type=F32)
            route = route.astype(BF16)
            kept_out[:, cols] = route[:half_rows]
            given_out[:, cols] = route[half_rows:]

    if packs:
        write_slots(slots_outs, packs, None, parts, grads, taken, sizes, width)
    if adds:
        start = pl.multiple_of(lax.axis_index("dp") * half, half)
        blocks = [dense_block(*block, start, half, width) for block in [(parts, grads), *dense]]
        blocks += [slot_block(ref, half, hidden_width) for ref in came]

        def store(which, cols, total):
            sums[which][cols, :] = total

        add_products(blocks, earlier, store, hidden_width)


def flat(parts):
    return [array for part in parts for array in part]


def expert_rows(
    parts, weights, sizes, sums=None, packs=(), waiting=(), came=(), after=(), adds=True, routed=True
):
    _, slots, _, half = sizes
    total = sum(used_rows(part) for part in parts)
    hidden_width, width = weights[0].shape
    operands = [*flat(parts), *weights]
    for block_parts, block_grads in waiting:
        operands += [*flat(block_parts), *block_grads]
    operands += [*came, *after, *(sums or ())]
    wide = jax.ShapeDtypeStruct((total // 2, width + LANES), BF16)
    grad = jax.ShapeDtypeStruct((total, hidden_width), BF16)
    added = jax.ShapeDtypeStruct((hidden_width, half), F32)
    results = [wide] * (2 * routed)
    for pack in packs:
        shape = (slots * len(pack), 2 * half + 3 * hidden_width)
        results.append(jax.ShapeDtypeStruct(shape, BF16))
    first = len(results)
    results += [added] * 3 if adds else [grad] * 3
    first_sum = len(operands) - 3
    results = pl.pallas_call(
        functools.partial(
            rows_kernel,
            [len(part) for part in parts],
            packs,
            [[len(part) for part in block_parts] for block_parts, _ in waiting],
            len(came),
            len(after),
            sums is not None,
            adds,
            routed,
            sizes,
        ),
        out_shape=results,
        in_specs=[WHEREVER if any(o is a for a in after) else IN_VMEM for o in operands],
        out_specs=[IN_VMEM] * len(results),
        input_output_aliases={first_sum + i: first + i for i in range(3)} if sums else {},
        scratch_shapes=[pltpu.VMEM(grad.shape, BF16)] * (3 * adds),
        compiler_params=pltpu.CompilerParams(vmem_limit_bytes=KERNEL_VMEM),
        cost_estimate=NO_COST,
    )(*operands)
    return list(results[: 2 * routed]), list(results[2 * routed : first]), list(results[first:])


def sums_kernel(waiting, slot_total, half, width, *refs):
    refs = list(refs)

    def take(count):
        taken = refs[:count]
        del refs[:count]
        return taken

    dense = [(take_parts(refs, layout), take(3)) for layout in waiting]
    came, earlier, outs = take(slot_total), take(3), take(3)
    hidden_width = earlier[0].shape[0]
    start = pl.multiple_of(lax.axis_index("dp") * half, half)
    blocks = [dense_block(*block, start, half, width) for block in dense]
    blocks += [slot_block(ref, half, hidden_width) for ref in came]

    def store(which, cols, total):
        outs[which][cols, :] = total

    add_products(blocks, earlier, store, hidden_width)


def add_rows(came, sums, width, waiting=()):
    hidden_width, half = sums[0].shape
    operands = []
    for block_parts, block_grads in waiting:
        operands += [*flat(block_parts), *block_grads]
    operands += [*came, *sums]
    added = jax.ShapeDtypeStruct((hidden_width, half), F32)
    first_sum = len(operands) - 3
    return list(
        pl.pallas_call(
            functools.partial(
                sums_kernel,
                [[len(part) for part in block_parts] for block_parts, _ in waiting],
                len(came),
                half,
                width,
            ),
            out_shape=[added] * 3,
            in_specs=[IN_VMEM] * len(operands),
            out_specs=[IN_VMEM] * 3,
            input_output_aliases={first_sum + i: i for i in range(3)},
            compiler_params=pltpu.CompilerParams(vmem_limit_bytes=KERNEL_VMEM),
            cost_estimate=NO_COST,
        )(*operands)
    )


def pack_kernel(tokens, out_grad, ids, gates, out, ids_held, sent):
    width = tokens.shape[1]
    top_count = ids.shape[0]
    copies = [
        pltpu.make_async_copy(ids, ids_held, sent.at[0]),
        pltpu.make_async_copy(tokens, out.at[:, pl.ds(0, width)], sent.at[1]),
        pltpu.make_async_copy(out_grad, out.at[:, pl.ds(width, width)], sent.at[2]),
    ]
    for copy in copies:
        copy.start()
    row = lax.broadcasted_iota(jnp.int32, (top_count, LANES), 0)
    lane = lax.broadcasted_iota(jnp.int32, (top_count, LANES), 1)
    copies[0].wait()
    routing = 0.0
    for values, at in ((ids_held[...].astype(F32).astype(BF16), 0), (gates[...], top_count)):
        spread = (lane == row + at).astype(BF16)
        routing += lax.dot_general(values, spread, OVER_ROWS, preferred_element_type=F32)
    out[:, 2 * width :] = routing.astype(BF16)
    copies[1].wait()
    copies[2].wait()


def packed_rows(tokens, out_grad, expert_ids, gates):
    rows, width = tokens.shape
    top_count = expert_ids.shape[1]
    return pl.pallas_call(
        pack_kernel,
        out_shape=jax.ShapeDtypeStruct((rows, 2 * width + LANES), BF16),
        in_specs=[WHEREVER] * 3 + [IN_VMEM],
        out_specs=IN_VMEM,
        scratch_shapes=[
            pltpu.VMEM((top_count, rows), jnp.int32),
            pltpu.SemaphoreType.DMA((3,)),
        ],
        compiler_params=pltpu.CompilerParams(vmem_limit_bytes=ALL_VMEM),
        cost_estimate=NO_COST,
    )(tokens, out_grad, expert_ids.T, gates.T)


def finish_kernel(experts, *refs):
    kept, given, fore, rear, ids, came, *refs = refs
    earlier, (token_out, gate_out), sums = refs[:3], refs[3:5], refs[5:8]
    rounded, sent = refs[8:]
    hidden_width, half = earlier[0].shape

    def store(which, cols, total):
        rounded[which, cols, :] = total.astype(BF16)
        pltpu.make_async_copy(
            rounded.at[which, cols, :], sums[which].at[cols, :], sent.at[which]
        ).start()

    add_products([slot_block(came, half, hidden_width)], earlier, store, hidden_width)
    rows, width = token_out.shape
    total = kept[...].astype(F32) + given[...].astype(F32) + fore[...].astype(F32)
    total += rear[...].astype(F32)
    token_out[...] = total[:, :width].astype(BF16)
    table = jnp.transpose(total[:, width:])
    chosen = ids[...]
    grad = jnp.zeros(chosen.shape, F32)
    for expert in range(experts):
        grad += jnp.where(chosen == expert, table[expert : expert + 1, :rows], 0.0)
    gate_out[...] = grad.astype(BF16)
    for which in range(3):
        pltpu.make_async_copy(rounded.at[which], sums[which], sent.at[which]).wait()


def finished(experts, kept, given, fore, rear, expert_ids, came, sums):
    rows, top_count = expert_ids.shape
    hidden_width, half = sums[0].shape
    token_grad, gate_grad, *sums = pl.pallas_call(
        functools.partial(finish_kernel, experts),
        out_shape=[
            jax.ShapeDtypeStruct((rows, kept.shape[1] - LANES), BF16),
            jax.ShapeDtypeStruct((top_count, rows), BF16),
        ]
        + [jax.ShapeDtypeStruct((hidden_width, half), BF16)] * 3,
        in_specs=[IN_VMEM] * 9,
        out_specs=[IN_VMEM] * 2 + [WHEREVER] * 3,
        scratch_shapes=[
            pltpu.VMEM((3, hidden_width, half), BF16),
            pltpu.SemaphoreType.DMA((3,)),
        ],
        compiler_params=pltpu.CompilerParams(vmem_limit_bytes=KERNEL_VMEM),
        cost_estimate=NO_COST,
    )(kept, given, fore, rear, expert_ids.T, came, *sums)
    return token_grad, gate_grad.T, sums


def chip_ring(expert_count):
    depth = expert_count // 4
    return [2 * z for z in range(depth)] + [2 * z + 1 for z in reversed(range(depth))]


def ring_shift(expert_count, by):
    order = chip_ring(expert_count)
    total = len(order)
    return sorted(
        (2 * chip + core, 2 * order[(place + by) % total] + core)
        for place, chip in enumerate(order)
        for core in range(2)
    )


def on_ring(tokens, out_grad, expert_ids, gates, w_gate, w_up, w_down):
    rows, width = tokens.shape
    top_count = expert_ids.shape[1]
    experts = lax.axis_size("expert")
    half = width // lax.axis_size("dp")
    capacity = min(rows, rows * top_count * 6 // (5 * experts))
    sizes = (rows, capacity, top_count, half)
    forth, back = ring_shift(experts, 1), ring_shift(experts, -1)
    weights = (w_gate[0].T, w_up[0].T, w_down[0])
    stage = lax.optimization_barrier

    def go(value, pairs):
        return lax.ppermute(value, "expert", pairs)

    def sibling(value):
        return lax.ppermute(value, "expert", [(i, i ^ 1) for i in range(experts)])

    def across(value):
        return lax.ppermute(value, "dp", [(0, 1), (1, 0)])

    def with_siblings(parts):
        return parts + [tuple(sibling(array) for array in part) for part in parts]

    def expert(parts, sums=None, packs=(), **options):
        return expert_rows(parts, weights, sizes, sums, packs, **options)

    def passed_on(item, fore, rear):
        total = item[0].astype(F32) + item[1].astype(F32)
        fore = go((total[rows:] + fore.astype(F32)).astype(BF16), forth)
        rear = go((total[:rows] + rear.astype(F32)).astype(BF16), back)
        return fore, rear

    own = packed_rows(tokens, out_grad, expert_ids, gates)
    fore, rear, over0 = go(own, forth), go(own, back), across(own)
    parts0 = with_siblings([(own,)])
    near0, _, grads0 = expert(parts0, adds=False)
    fore, rear, over0, near0, block0 = stage((fore, rear, over0, near0, (parts0, grads0)))

    parts = with_siblings([(fore,), (rear,)])
    over1 = across(chosen_rows(fore, rear, sizes, width))
    fore, rear = go(fore, forth), go(rear, back)
    near1, _, sums = expert(parts, waiting=[block0])
    fore, rear, near1, sums = stage((fore, rear, near1, sums))

    parts = with_siblings([(fore,), (rear,)])
    over2 = across(jnp.pad(fore, ((0, 0), (0, LANES))))
    fore, rear = go(fore, forth), go(rear, back)
    near2, slots2, sums = expert(parts, sums, [(1, 3)])
    fore, rear, over1, near2, slots2, sums = stage((fore, rear, over1, near2, slots2, sums))

    parts3 = with_siblings([(fore,), (rear,)])
    far_x, far_rest = go(fore[:, :width], forth), go(rear[:, width:], back)
    came2 = across(slots2[0])
    near3, _, grads3 = expert(parts3, adds=False)
    far_x, far_rest, over2, near3, block3 = stage(
        (far_x, far_rest, over2, near3, (parts3, grads3))
    )

    parts4 = with_siblings([(far_x, far_rest)])
    near3[1], near2[1] = sibling(near3[1]), sibling(near2[1])
    slots3 = slot_rows(*block3, sizes, width, [(0, 1, 2), (3,)])
    near4, _, grads4 = expert(parts4, after=slots3, adds=False)
    near2, near3, near4, slots3, block4, came2 = stage(
        (near2, near3, near4, slots3, (parts4, grads4), came2)
    )
    came3 = across(slots3[0])
    near4[1] = sibling(near4[1])
    sum4 = (near4[0].astype(F32) + near4[1].astype(F32)).astype(BF16)
    cut = width // 2
    fore, rear = go(sum4[:, :cut], forth), go(sum4[:, cut:], back)
    fore, rear, near1, over0, over2 = stage((fore, rear, near1, over0, over2))
    fore = jnp.pad(fore, ((0, 0), (0, width + LANES - cut)))
    rear = jnp.pad(rear, ((0, 0), (cut, 0)))

    fore, rear = passed_on(near3, fore, rear)
    over = with_siblings([(over0,), (over2,)])
    sums = add_rows([came2], sums, width, [block3, block4])
    slots4 = slot_rows(*block4, sizes, width, [(0, 1)], slots3[1])
    fore, rear, near1, over1, over, came3, sums, slots4 = stage(
        (fore, rear, near1, over1, over, came3, sums, slots4)
    )

    came4 = across(slots4[0])
    fore, rear = passed_on(near2, fore, rear)
    near1[1] = sibling(near1[1])
    over1 = with_siblings([(over1,)])
    sums = expert(over, sums, routed=False)[2]
    fore, rear, near0, near1, over1, sums = stage((fore, rear, near0, near1, over1, sums))

    fore, rear = passed_on(near1, fore, rear)
    near0[1] = sibling(near0[1])
    sums = expert(over1, sums, came=[came3], routed=False)[2]
    fore, rear, near0, came4, sums = stage((fore, rear, near0, came4, sums))

    token_grad, gate_grad, sums = finished(experts, *near0, fore, rear, expert_ids, came4, sums)
    return (token_grad, gate_grad, sums[0].T[None], sums[1].T[None], sums[2][None])


def solution(mesh):
    in_specs = (
        P(("dp", "expert"), None),
        P(("dp", "expert"), None),
        P(("dp", "expert"), None),
        P(("dp", "expert"), None),
        P("expert", None, None),
        P("expert", None, None),
        P("expert", None, None),
    )
    out_specs = (
        P(("dp", "expert"), None),
        P(("dp", "expert"), None),
        P("expert", "dp", None),
        P("expert", "dp", None),
        P("expert", None, "dp"),
    )
    on_slice = on_ring if (mesh.shape["dp"], mesh.shape["expert"]) == (2, 16) else on_device
    return jax.shard_map(
        on_slice, mesh=mesh, in_specs=in_specs, out_specs=out_specs, check_vma=False
    )
```
